32 devices in a mesh: rep: 8 (over y, x, core), tp: 4 (over z).
Axes of the slice: x: 2, y: 2, z: 4, core: 2. Of those that a mesh axis runs over, the one named last changes fastest.
Arguments:
- hidden: bfloat16 [32, 2048], P('rep'), may hold values from -6 to 6
- lengths: int32 [32], P('rep'), may hold values from 1 to 5119, as said below
- page_table: int32 [32, 40], P('rep', 'tp'), may hold values from 0 to 39, as said below
- move_slot: int32 [8], P('rep'), may hold values from 0 to 3
- lat_pool: bfloat16 [1280, 128, 512], P(('rep', 'tp')), may hold values from -6 to 6
- rope_pool: bfloat16 [1280, 64, 128], P(('rep', 'tp')), may hold values from -460 to 460
- norm_attn: float32 [2048], replicated, may hold values from 0.5 to 1.5
- w_query: bfloat16 [2048, 3072], P(None, 'tp'), may hold values from -0.125 to 0.125
- w_latent: bfloat16 [2048, 576], replicated, may hold values from -0.125 to 0.125
- latent_gain: float32 [512], replicated, may hold values from 0.5 to 1.5
- w_key_up: bfloat16 [16, 128, 512], P('tp'), may hold values from -0.5 to 0.5
- w_value_up: bfloat16 [16, 512, 128], P('tp'), may hold values from -0.25 to 0.25
- w_output: bfloat16 [2048, 2048], P('tp'), may hold values from -0.125 to 0.125
- norm_ffn: float32 [2048], replicated, may hold values from 0.5 to 1.5
- w_router: bfloat16 [2048, 64], replicated, may hold values from -0.125 to 0.125
- route_ids: int32 [32, 6], replicated, may hold values from 0 to 63, all different within a row
- expert_gate: bfloat16 [64, 2048, 1408], P('rep', None, 'tp'), may hold values from -0.125 to 0.125
- expert_up: bfloat16 [64, 2048, 1408], P('rep', None, 'tp'), may hold values from -0.125 to 0.125
- expert_down: bfloat16 [64, 1408, 2048], P('rep', 'tp'), may hold values from -0.15625 to 0.15625
- shared_gate: bfloat16 [2048, 2816], P(None, 'tp'), may hold values from -0.125 to 0.125
- shared_up: bfloat16 [2048, 2816], P(None, 'tp'), may hold values from -0.125 to 0.125
- shared_down: bfloat16 [2816, 2048], P('tp'), may hold values from -0.109375 to 0.109375
Outputs:
- mixed: bfloat16 [32, 2048], P('rep')
- lat_cache: bfloat16 [1280, 128, 512], P(('rep', 'tp'))
- rope_cache: bfloat16 [1280, 64, 128], P(('rep', 'tp'))
The draws below stay inside these ranges and needn't reach their ends.
Inputs may be any that keep to these rules, and one draw needn't show every extreme that they name: lengths are heavy-tailed; in every draw some request has exactly 5119 cached tokens. `page_table`: the block of one device (rows of one replica, columns of one index of tp) holds each of its pool's pages exactly once. `route_ids`: the 6 ids of a row differ.
All inputs are finite; a program needn't handle non-finite values.
Results may differ from the reference program's by a relative error of at most 0.013.
Values may be sent and summed in bfloat16 or wider, within the bound.
No kernel may reach another device: no remote copies, remote signals or barrier semaphores. Data moves between devices by JAX's collectives and lax.ppermute only.
A program may use at most 192 MiB of HBM per device.

```python
import jax
import jax.numpy as jnp
from jax import lax

D = 2048
H = 16
NOPE = 128
ROPE = 64
VDIM = 128
LAT = 512
E = 64
FF = 1408
TOPK = 6
SFF = 2816
SINKS = 4
WIN = 4096
PAGE = 128
PAGES = 40
REQ = 4
REQS = 32
PPD = 10
POOL = 40
POOLS = 1280
N_REP = 8
N_TP = 4


def draw_lengths(key, part):
    longest = PAGES * PAGE - 1
    levels = max(1, longest.bit_length())
    first_key, second_key, third_key = jax.random.split(jax.random.fold_in(key, 11), 3)
    exponent = jax.random.randint(first_key, (REQS,), 1, levels + 1)
    spans = jnp.left_shift(jnp.ones((REQS,), jnp.int32), exponent)
    raw_bits = jax.random.randint(second_key, (REQS,), 0, 1 << 20)
    values = jnp.minimum(raw_bits % spans + 1, longest)
    chosen = jax.random.randint(third_key, (), 0, REQS)
    return jnp.where(jnp.arange(REQS, dtype=jnp.int32) == chosen, longest, values).astype(jnp.int32)


def draw_page_table(key, part):
    keys = jax.random.split(jax.random.fold_in(key, 23), N_REP * N_TP)
    orders = jax.vmap(lambda single: jax.random.permutation(single, POOL))(keys)
    blocks = orders.reshape(N_REP, N_TP, REQ, PPD).transpose(0, 2, 1, 3)
    return blocks.reshape(REQS, PAGES).astype(jnp.int32)


def draw_rope_pool(key, part):
    keys = jax.random.split(jax.random.fold_in(key, 37), 1)
    shape = (POOLS, ROPE, PAGE)
    return jnp.clip(jax.random.normal(keys[0], shape, jnp.float32), -6.0, 6.0).astype(jnp.bfloat16)


def with_ends(values, key, low, top_value):
    dims = values.shape
    index_at = [jax.random.randint(jax.random.fold_in(key, axis), (), 0, dims[axis]) for axis in range(len(dims))]
    values = values.at[tuple(index_at)].set(low)
    longest = dims.index(max(dims))
    index_at[longest] = (index_at[longest] + 1) % dims[longest]
    return values.at[tuple(index_at)].set(top_value)


def block_scale(stream_key, shape, cuts, smallest, top_value):
    def one(position, shards_of):
        steps = jax.random.uniform(jax.random.fold_in(jax.random.fold_in(stream_key, 6), position), (shards_of,), jnp.float32, smallest / len(cuts), top_value / len(cuts))
        return jnp.repeat(jnp.exp(steps), shape[position] // shards_of).reshape((-1,) + (1,) * (len(shape) - position - 1))

    loudness = one(*cuts[0])
    for cut in cuts[1:]:
        loudness = loudness * one(*cut)
    return loudness


def choose_distinct(stream_key, rows, number_of, top, lift):
    sequence = jax.random.permutation(jax.random.fold_in(stream_key, 1), number_of)
    pull = sequence
    for power in range(3):
        pull = pull * pull // number_of
    pull = pull * lift // number_of
    chance = jax.random.randint(jax.random.fold_in(stream_key, 2), (rows, number_of), 0, 4096) + pull
    holders = jax.random.permutation(jax.random.fold_in(stream_key, 3), rows)[jnp.arange(number_of) % rows]
    chance = jnp.where(jnp.arange(rows)[:, None] == holders[None, :], 1 << 14, chance)
    merit = chance * number_of + jnp.arange(number_of)
    return lax.top_k(merit.astype(jnp.int32), top)[1].astype(jnp.int32)


def gaussian(own_key, extent, spread, reach, cuts=(), kind=jnp.bfloat16):
    level = block_scale(own_key, extent, cuts, -0.22, 0.18) if cuts else 1.0
    result = jax.random.normal(own_key, extent, jnp.float32) * spread * level
    return jnp.minimum(jnp.maximum(result, -reach), reach).astype(kind)


def setup_inputs(seed: int = 0) -> dict:
    seeds = jax.random.split(jax.random.key(seed), 23)
    return {
        "hidden": gaussian(seeds[0], (REQS, D), 1.0, 6.0, ((0, 8),)),
        "lengths": draw_lengths(jax.random.fold_in(seeds[22], 71), 0),
        "page_table": draw_page_table(jax.random.fold_in(seeds[22], 71), 0),
        "move_slot": with_ends(jax.random.randint(seeds[3], (N_REP,), 0, REQ), jax.random.fold_in(seeds[3], 1), 0, REQ - 1).astype(jnp.int32),
        "lat_pool": gaussian(seeds[4], (POOLS, PAGE, LAT), 1.0, 6.0, ((0, 32),)),
        "rope_pool": draw_rope_pool(jax.random.fold_in(seeds[22], 71), 0),
        "norm_attn": jnp.clip(1.0 + 0.1 * jax.random.normal(seeds[6], (D,), jnp.float32), 0.5, 1.5),
        "w_query": gaussian(seeds[7], (D, H * (NOPE + ROPE)), D ** -0.5, 0.125, ((1, 4),)),
        "w_latent": gaussian(seeds[8], (D, LAT + ROPE), D ** -0.5, 0.125),
        "latent_gain": jnp.clip(1.0 + 0.1 * jax.random.normal(seeds[9], (LAT,), jnp.float32), 0.5, 1.5),
        "w_key_up": gaussian(seeds[10], (H, NOPE, LAT), NOPE ** -0.5, 0.5, ((0, 4),)),
        "w_value_up": gaussian(seeds[11], (H, LAT, VDIM), LAT ** -0.5, 0.25, ((0, 4),)),
        "w_output": gaussian(seeds[12], (H * VDIM, D), (H * VDIM) ** -0.5, 0.125, ((0, 4),)),
        "norm_ffn": jnp.clip(1.0 + 0.1 * jax.random.normal(seeds[13], (D,), jnp.float32), 0.5, 1.5),
        "w_router": gaussian(seeds[14], (D, E), D ** -0.5, 0.125),
        "route_ids": choose_distinct(seeds[15], REQS, E, TOPK, 1536),
        "expert_gate": gaussian(seeds[16], (E, D, FF), D ** -0.5, 0.125, ((0, 8), (2, 4))),
        "expert_up": gaussian(seeds[17], (E, D, FF), D ** -0.5, 0.125, ((0, 8), (2, 4))),
        "expert_down": gaussian(seeds[18], (E, FF, D), FF ** -0.5, 0.15625, ((0, 8), (1, 4))),
        "shared_gate": gaussian(seeds[19], (D, SFF), D ** -0.5, 0.125, ((1, 4),)),
        "shared_up": gaussian(seeds[20], (D, SFF), D ** -0.5, 0.125, ((1, 4),)),
        "shared_down": gaussian(seeds[21], (SFF, D), SFF ** -0.5, 0.109375, ((0, 4),)),
    }


EPS = 1e-06
ROUTE_SCALE = 2.446
NEG = -1e+30

def rms_norm(values, gain):
    values = values.astype(jnp.float32)
    return values * lax.rsqrt(lax.optimization_barrier(jnp.mean(values * values, axis=-1, keepdims=True)) + EPS) * gain

def reference(hidden, lengths, page_table, move_slot, lat_pool, rope_pool, norm_attn, w_query, w_latent, latent_gain, w_key_up, w_value_up, w_output, norm_ffn, w_router, route_ids, expert_gate, expert_up, expert_down, shared_gate, shared_up, shared_down):
    f32 = jnp.float32
    bf16 = jnp.bfloat16
    per_dev = PAGES // N_TP
    pool_size = REQ * per_dev
    replicas = jnp.arange(N_REP, dtype=jnp.int32)
    partner = (replicas + N_REP // 2) % N_REP
    slot_row = (replicas * REQ + move_slot).astype(jnp.int32)
    source_row = slot_row[partner]
    served = jnp.arange(REQS, dtype=jnp.int32).at[slot_row].set(source_row)
    page_ids = jnp.arange(PAGES, dtype=jnp.int32)

    def global_pages(rows):
        owner = rows // REQ
        return ((owner[:, None] * N_TP + page_ids[None, :] // per_dev) * pool_size + page_table[rows]).astype(jnp.int32)
    target_pages = global_pages(slot_row).reshape(-1)
    source_pages = global_pages(source_row).reshape(-1)
    moved_lat = lat_pool.at[target_pages].set(lat_pool[source_pages])
    moved_rope = rope_pool.at[target_pages].set(rope_pool[source_pages])
    x_rows = hidden[served]
    lens = lengths[served]
    xn = rms_norm(x_rows, norm_attn).astype(bf16)
    query = jnp.dot(xn, w_query, preferred_element_type=f32).astype(bf16).reshape(REQS, H, NOPE + ROPE)
    q_lat = jnp.einsum('rhn,hnl->rhl', query[..., :NOPE].astype(f32), w_key_up.astype(f32)).astype(bf16)
    q_pos = query[..., NOPE:]
    latent_full = jnp.dot(xn, w_latent, preferred_element_type=f32)
    c_new = rms_norm(latent_full[:, :LAT], latent_gain).astype(bf16)
    p_new = latent_full[:, LAT:].astype(bf16)
    scale = (NOPE + ROPE) ** (-0.5)
    all_pages = global_pages(jnp.arange(REQS, dtype=jnp.int32))
    positions = page_ids[:, None, None] * PAGE + jnp.arange(PAGE, dtype=jnp.int32)[None, None, :]

    def one_request(items):
        q_one, pos_one, c_one, p_one, length, pages = items
        lat_rows = moved_lat[pages].astype(f32)
        rope_rows = moved_rope[pages].astype(f32)
        scores = (jnp.einsum('hl,jcl->jhc', q_one.astype(f32), lat_rows) + jnp.einsum('he,jec->jhc', pos_one.astype(f32), rope_rows)) * scale
        allowed = (positions < length) & ((positions < SINKS) | (positions >= length + 1 - WIN))
        page_max = lax.optimization_barrier(jnp.max(jnp.where(allowed, scores, NEG), axis=2))
        weights = jnp.where(allowed, jnp.exp(scores - page_max[..., None]), 0.0).astype(bf16)
        totals = lax.optimization_barrier(jnp.sum(weights.astype(f32), axis=2))
        sums = jnp.einsum('jhc,jcl->jhl', weights.astype(f32), lat_rows)
        new_score = (lax.optimization_barrier(jnp.sum(q_one.astype(f32) * c_one.astype(f32)[None, :], -1)) + lax.optimization_barrier(jnp.sum(pos_one.astype(f32) * p_one.astype(f32)[None, :], -1))) * scale
        peak = jnp.maximum(lax.optimization_barrier(jnp.max(page_max, axis=0)), new_score)
        factor = jnp.exp(page_max - peak[None, :])
        new_factor = jnp.exp(new_score - peak)
        denom = lax.optimization_barrier(jnp.sum(factor * totals, axis=0)) + new_factor
        numer = lax.optimization_barrier(jnp.sum(factor[..., None] * sums, axis=0)) + new_factor[:, None] * c_one.astype(f32)[None, :]
        return (numer / denom[:, None]).astype(bf16)
    o_lat = lax.map(one_request, (q_lat, q_pos, c_new, p_new, lens, all_pages))
    o_val = jnp.einsum('rhl,hlv->rhv', o_lat.astype(f32), w_value_up.astype(f32)).astype(bf16).reshape(REQS, H * VDIM)
    h_one = (x_rows.astype(f32) + jnp.dot(o_val, w_output, preferred_element_type=f32)).astype(bf16)
    xm = rms_norm(h_one, norm_ffn).astype(bf16)
    gates = jax.nn.sigmoid(jnp.dot(xm, w_router, preferred_element_type=f32))
    chosen = jnp.take_along_axis(gates, route_ids, axis=1)
    route_weight = chosen / lax.optimization_barrier(jnp.sum(chosen, axis=1, keepdims=True)) * ROUTE_SCALE

    def expert_term(carry, expert):
        gate_val = jnp.dot(xm, expert_gate[expert], preferred_element_type=f32)
        up_val = jnp.dot(xm, expert_up[expert], preferred_element_type=f32)
        hid = (jax.nn.silu(gate_val) * up_val).astype(bf16)
        output = jnp.dot(hid, expert_down[expert], preferred_element_type=f32)
        coef = lax.optimization_barrier(jnp.sum(jnp.where(route_ids == expert, route_weight, 0.0), axis=1))
        return (carry + coef[:, None] * output, None)
    routed, _ = lax.scan(expert_term, jnp.zeros((REQS, D), f32), jnp.arange(E, dtype=jnp.int32))
    shared_hid = (jax.nn.silu(jnp.dot(xm, shared_gate, preferred_element_type=f32)) * jnp.dot(xm, shared_up, preferred_element_type=f32)).astype(bf16)
    shared = jnp.dot(shared_hid, shared_down, preferred_element_type=f32)
    mixed = (h_one.astype(f32) + routed + shared).astype(bf16)
    page_of = (lens // PAGE).astype(jnp.int32)
    row_in = (lens % PAGE).astype(jnp.int32)
    target = jnp.take_along_axis(all_pages, page_of[:, None], axis=1)[:, 0]
    lat_cache = moved_lat.at[target, row_in].set(c_new)
    rope_cache = moved_rope.at[target, :, row_in].set(p_new)
    return (mixed, lat_cache, rope_cache)
```

```python
import functools

import jax
import jax.numpy as jnp
from jax import lax
from jax.experimental import pallas as pl
from jax.experimental.pallas import tpu as pltpu
from jax.sharding import PartitionSpec as P

NOPE = 128
ROPE = 64
SINKS = 4
WIN = 4096
PAGE = 128
LANES = 128
ROWS = 16
EPS = 1e-06
ROUTE_SCALE = 2.446
NEG = -1e30
F32 = jnp.float32
BF16 = jnp.bfloat16
NT = (((1,), (1,)), ((), ()))

VMEM = pl.BlockSpec(memory_space=pltpu.VMEM)
SMEM = pl.BlockSpec(memory_space=pltpu.SMEM)
ANY = pl.BlockSpec(memory_space=pl.ANY)


def xored(value, axis, mask):
    pairs = [(source, source ^ mask) for source in range(lax.axis_size(axis))]
    return lax.ppermute(value, axis, pairs)


def call(kernel, out_shape, in_specs, out_specs, scratch=(), vmem=8, flops=0, nbytes=0, aliases=None):
    return pl.pallas_call(
        kernel,
        out_shape=out_shape,
        in_specs=in_specs,
        out_specs=out_specs,
        scratch_shapes=list(scratch),
        input_output_aliases=aliases or {},
        compiler_params=pltpu.CompilerParams(vmem_limit_bytes=vmem * 1024 * 1024),
        cost_estimate=pl.CostEstimate(flops=flops, bytes_accessed=nbytes, transcendentals=0),
    )


def struct(shape, dtype):
    return jax.ShapeDtypeStruct(shape, dtype)


def in_hbm(value):
    return pltpu.with_memory_space_constraint(value, pltpu.HBM)


def rms_norm(values, gain):
    return values * lax.rsqrt(jnp.mean(values * values, axis=-1, keepdims=True) + EPS) * gain


def silu(value):
    return value / (1.0 + jnp.exp(-value))


def query_kernel(
    first, table_in, slot_in, x_in, gain_in, w_in, key_in, lat, rope,
    q_out, normed_out, lat_out, rope_out,
    table, slot, x, gain, w_query, key_up, sems, in_sems,
):
    per_dev = table.shape[1]
    size = x.shape[1]
    parts = in_sems.shape[0] - 5
    step = size // parts
    small = [
        pltpu.make_async_copy(source, target, in_sems.at[i])
        for i, (source, target) in enumerate(
            [(table_in, table), (slot_in, slot), (x_in, x), (gain_in, gain)]
        )
    ]
    for copy in small:
        copy.start()
    big = []
    for i in range(parts):
        piece = pl.ds(i * step, step)
        big.append(pltpu.make_async_copy(w_in.at[piece], w_query.at[piece], in_sems.at[4 + i]))
    big.append(pltpu.make_async_copy(key_in, key_up, in_sems.at[4 + parts]))
    for copy in big:
        copy.start()
    small[0].wait()
    small[1].wait()
    copies = []
    for j in range(per_dev):
        page = table[slot[0], j]
        if j < first:
            copies.append(pltpu.make_async_copy(lat.at[page], lat_out.at[j], sems.at[0, j]))
        copies.append(pltpu.make_async_copy(rope.at[page], rope_out.at[j], sems.at[1, j]))
    for copy in copies:
        copy.start()
    small[2].wait()
    small[3].wait()
    normed = rms_norm(x[...].astype(F32), gain[...]).astype(BF16)
    normed_out[...] = normed
    heads, nope, _ = key_up.shape
    query = None
    for i in range(parts):
        big[i].wait()
        piece = slice(i * step, (i + 1) * step)
        term = jnp.dot(normed[:, piece], w_query[piece, :], preferred_element_type=F32)
        query = term if query is None else query + term
    big[parts].wait()
    wide = query.shape[1] // heads
    rows = []
    for h in range(heads):
        one = query[:, h * wide : (h + 1) * wide]
        q_lat = jnp.dot(one[:, :nope].astype(BF16), key_up[h], preferred_element_type=F32)
        rows.append(jnp.concatenate([q_lat, one[:, nope:]], axis=1))
    q_out[...] = jnp.concatenate(rows, axis=0).astype(BF16)
    for copy in copies:
        copy.wait()


def fetch_kernel(
    table, lengths, normed, gain, w_latent, lat, rope,
    lat_v, rope_v, new_out, latent_v, sems, w_sem,
):
    requests, per_dev = table.shape
    weights = pltpu.make_async_copy(w_latent, latent_v, w_sem.at[0])
    weights.start()
    copies = []
    for r in range(requests):
        for j in range(per_dev):
            n = r * per_dev + j
            page = table[r, j]
            copies.append(pltpu.make_async_copy(lat.at[page], lat_v.at[n], sems.at[0, n]))
            copies.append(pltpu.make_async_copy(rope.at[page], rope_v.at[n], sems.at[1, n]))
    for copy in copies:
        copy.start()
    size = gain.shape[1]
    weights.wait()
    latent = lax.dot_general(normed[...], latent_v[...], NT, preferred_element_type=F32)
    c_new = rms_norm(latent[:, :size], gain[...]).astype(BF16).astype(F32)
    p_new = latent[:, size:].astype(BF16).astype(F32)
    lane = lax.broadcasted_iota(jnp.int32, (1, LANES), 1)
    marks = []
    for r in range(requests):
        page = jnp.full((1, LANES), lengths[r] // PAGE, jnp.int32)
        inside = jnp.full((1, LANES), lengths[r] % PAGE, jnp.int32)
        marks.append(jnp.where(lane == 0, page, jnp.where(lane == 1, inside, 0)))
    mark = jnp.concatenate(marks, axis=0).astype(F32)
    new = jnp.concatenate([c_new, p_new, mark[:, : LANES - ROPE]], axis=1)
    new_out[...] = new
    for copy in copies:
        copy.wait()


def attention_kernel(blocks, per_dev, requests, lat_size, *refs):
    lengths, rank = refs[:2]
    queries = refs[2 : 2 + blocks]
    lat, rope, value_up, w_out = refs[2 + blocks : 6 + blocks]
    outs = refs[6 + blocks : 6 + 2 * blocks]
    value_v, out_v, q_all, result, sems = refs[6 + 2 * blocks :]
    weights_in = [
        pltpu.make_async_copy(value_up, value_v, sems.at[0]),
        pltpu.make_async_copy(w_out, out_v, sems.at[1]),
    ]
    for copy in weights_in:
        copy.start()
    rows = queries[0].shape[0]
    heads = blocks * rows // requests
    scale = (NOPE + ROPE) ** (-0.5)
    tiles = lat_size // LANES
    for k in range(blocks):
        block = queries[k][...].astype(F32)
        for i in range(tiles + 1):
            piece = block[:, i * LANES : (i + 1) * LANES]
            q_all[i, k * rows : (k + 1) * rows, : piece.shape[1]] = piece
    base = rank[0] * (per_dev * PAGE)
    side = lax.broadcasted_iota(jnp.int32, (heads, LANES), 1)

    def attend(r, count):
        mine = pl.ds(r, heads, stride=requests)
        length = lengths[r]
        q_lat = jnp.concatenate([q_all[i, mine, :] for i in range(tiles)], axis=1).astype(BF16)
        q_pos = q_all[tiles, mine, :][:, :ROPE].astype(BF16)
        start = r * per_dev
        latents = lat[start : start + count].reshape(count * PAGE, lat_size)
        scores = lax.dot_general(q_lat, latents, NT, preferred_element_type=F32)
        scores += jnp.concatenate(
            [
                jnp.dot(q_pos, rope[start + j], preferred_element_type=F32)
                for j in range(count)
            ],
            axis=1,
        )
        scores *= scale
        position = base + lax.broadcasted_iota(jnp.int32, scores.shape, 1)
        allowed = (position < length) & ((position < SINKS) | (position >= length + 1 - WIN))
        peak = jnp.max(jnp.where(allowed, scores, NEG), axis=1, keepdims=True)
        weights = jnp.where(allowed, jnp.exp(scores - peak), 0.0).astype(BF16)
        total = jnp.sum(weights.astype(F32), axis=1, keepdims=True)
        sums = jnp.dot(weights, latents, preferred_element_type=F32)
        for i in range(tiles):
            result[i, mine, :] = sums[:, i * LANES : (i + 1) * LANES]
        result[tiles, mine, :] = jnp.where(side < LANES // 2, peak, total)

    few = min(2, per_dev)
    for r in range(requests):
        length = lengths[r]
        past = length <= base
        short = length <= base + few * PAGE

        @pl.when(past)
        def _():
            mine = pl.ds(r, heads, stride=requests)
            for i in range(tiles):
                result[i, mine, :] = jnp.zeros((heads, LANES), F32)
            result[tiles, mine, :] = jnp.where(side < LANES // 2, NEG, 0.0)

        @pl.when(jnp.logical_not(past) & short)
        def _():
            attend(r, few)

        @pl.when(jnp.logical_not(short))
        def _():
            attend(r, per_dev)

    for k in range(blocks):
        for i in range(tiles + 1):
            outs[k][:, i * LANES : (i + 1) * LANES] = result[i, k * rows : (k + 1) * rows, :]
    for copy in weights_in:
        copy.wait()


def finish_kernel(blocks, requests, lat_size, *refs):
    parts = refs[:blocks]
    query, new, value_up, w_out, out = refs[blocks:]
    local_heads = value_up.shape[0]
    scale = (NOPE + ROPE) ** (-0.5)
    half = lat_size + LANES // 2
    fresh = jnp.concatenate([new[:, : lat_size + ROPE]] * local_heads, axis=0)
    q_own = query[...].astype(F32)
    new_score = jnp.sum(q_own * fresh, axis=1, keepdims=True) * scale
    peak = new_score
    for part in parts:
        peak = jnp.maximum(peak, part[:, lat_size : lat_size + 1])
    new_factor = jnp.exp(new_score - peak)
    denom = new_factor
    numer = new_factor * fresh[:, :lat_size]
    for part in parts:
        factor = jnp.exp(part[:, lat_size : lat_size + 1] - peak)
        denom += factor * part[:, half : half + 1]
        numer += factor * part[:, :lat_size]
    o_lat = numer / denom
    vals = []
    for h in range(local_heads):
        one = o_lat[h * requests : (h + 1) * requests, :].astype(BF16)
        vals.append(jnp.dot(one, value_up[h], preferred_element_type=F32).astype(BF16))
    o_val = jnp.concatenate(vals, axis=1)
    out[...] = jnp.dot(o_val, w_out[...], preferred_element_type=F32)


def norm_kernel(blocks, *refs):
    slot = refs[0]
    parts = refs[1 : 1 + blocks]
    x, gain = refs[1 + blocks : 3 + blocks]
    row_out, h_out = refs[-2:]
    attn = parts[0][...]
    for part in parts[1:]:
        attn += part[...]
    h_one = (x[...].astype(F32) + attn).astype(BF16)
    h_out[...] = h_one
    wide = h_one.astype(F32)
    normed = rms_norm(wide, gain[...])
    mark = jnp.full((wide.shape[0], LANES), slot[0], jnp.int32).astype(F32)
    row_out[...] = jnp.concatenate([normed, mark], axis=1).astype(BF16)


def copy_pages(table, slot, lat, lat_out, sems, first, count):
    copies = [
        pltpu.make_async_copy(
            lat.at[table[slot[0], first + j]], lat_out.at[pl.ds(j * PAGE, PAGE)], sems.at[j]
        )
        for j in range(count)
    ]
    for copy in copies:
        copy.start()
    return copies


def order_kernel(groups, requests, first, count, *refs):
    table, slot, rank, route_ids, router, lat = refs[:6]
    pieces = refs[6 : 6 + groups]
    h_one, new = refs[6 + groups : 8 + groups]
    x_out, coef_out, own_out, lat_out, sems = refs[9 + groups :]
    copies = copy_pages(table, slot, lat, lat_out, sems, first, count)
    both = jnp.concatenate([h_one[...].astype(F32), new[...]], axis=1)
    row = lax.broadcasted_iota(jnp.int32, both.shape, 0)
    both = jnp.sum(jnp.where(row == slot[0], both, 0.0), axis=0, keepdims=True)
    lat_size = lat_out.shape[1]
    lines = [both[:, b : b + lat_size] for b in range(0, both.shape[1], lat_size)]
    lines[-1] = jnp.pad(lines[-1], ((0, 0), (0, lat_size - lines[-1].shape[1])))
    lines.append(jnp.zeros((ROWS - len(lines), lat_size), F32))
    lat_out[count * PAGE :, :] = jnp.concatenate(lines, axis=0).astype(BF16)
    size = router.shape[1]
    per = pieces[0].shape[0]
    rows = groups * per
    reps = rows // requests
    wide = jnp.concatenate([p[...].astype(F32) for p in pieces], axis=0)
    moved = wide[:, size : size + 1]
    other = jnp.concatenate([moved[rows // 2 :], moved[: rows // 2]], axis=0)
    row = lax.broadcasted_iota(jnp.int32, (rows, 1), 0)
    place = row // requests
    across = ((place + reps // 2) % reps) * requests
    source = jnp.where(
        row % requests == moved.astype(jnp.int32), across + other.astype(jnp.int32), row
    )
    column = lax.broadcasted_iota(jnp.int32, (rows, rows), 1)
    picks = (column == source).astype(F32).astype(BF16)
    x = jnp.dot(picks, wide[:, :size].astype(BF16), preferred_element_type=F32)
    own_out[...] = x[:requests, :].astype(BF16)
    x = x.astype(BF16)
    x_out[...] = x
    gates = jax.nn.sigmoid(lax.dot_general(x, router[...], NT, preferred_element_type=F32))
    home = (place ^ rank[0]) * requests + row % requests
    turns = (column == home).astype(F32).astype(BF16)
    ids = jnp.dot(turns, route_ids[...].astype(F32).astype(BF16), preferred_element_type=F32)
    ids = ids.astype(jnp.int32)
    expert = lax.broadcasted_iota(jnp.int32, gates.shape, 1)
    chosen = jnp.zeros(gates.shape, F32)
    for k in range(ids.shape[1]):
        chosen += jnp.where(expert == ids[:, k : k + 1], gates, 0.0)
    coef_out[...] = chosen / jnp.sum(chosen, axis=1, keepdims=True) * ROUTE_SCALE
    for copy in copies:
        copy.wait()


def expert_kernel(
    requests, chunk, hidden, rank, x, coef, gate, up, down, kept, sent, gate_v, up_v, down_v, total, sems,
):
    units = gate.shape[0]
    pieces = [slice(b, min(b + chunk, units)) for b in range(0, units, chunk)]

    def fetch(which, source, target, i):
        piece = pl.ds(pieces[i].start, pieces[i].stop - pieces[i].start)
        return pltpu.make_async_copy(source.at[piece], target.at[piece], sems.at[which, i])

    copies = [
        [fetch(w, s, t, i) for w, (s, t) in enumerate([(gate, gate_v), (up, up_v), (down, down_v)])]
        for i in range(len(pieces))
    ]
    for trio in copies:
        for copy in trio:
            copy.start()
    count = units // hidden
    first = rank[0] * count
    weights = coef[...]
    expert = lax.broadcasted_iota(jnp.int32, weights.shape, 1)
    shares = [
        jnp.sum(jnp.where(expert == first + e, weights, 0.0), axis=1, keepdims=True)
        for e in range(count)
    ]
    rows = x.shape[0]
    for i, piece in enumerate(pieces):
        copies[i][0].wait()
        gate_val = lax.dot_general(x[...], gate_v[piece, :], NT, preferred_element_type=F32)
        copies[i][1].wait()
        up_val = lax.dot_general(x[...], up_v[piece, :], NT, preferred_element_type=F32)
        unit = piece.start + lax.broadcasted_iota(jnp.int32, gate_val.shape, 1)
        low, high = piece.start // hidden, (piece.stop - 1) // hidden
        share = jnp.broadcast_to(shares[high], gate_val.shape)
        for e in range(high - 1, low - 1, -1):
            share = jnp.where(unit < (e + 1) * hidden, shares[e], share)
        hid = (silu(gate_val) * up_val * share).astype(BF16)
        copies[i][2].wait()
        term = jnp.dot(hid, down_v[piece, :], preferred_element_type=F32)
        if i == 0:
            total[...] = term
        else:
            total[...] += term
    value = total[...]
    blocks = [value[p * requests : (p + 1) * requests] for p in range(rows // requests)]
    kept[...] = jnp.concatenate(blocks[0::2], axis=0)
    sent[...] = jnp.concatenate(blocks[1::2], axis=0).astype(BF16)


def pair_kernel(requests, kept, got, _, own, *blocks):
    total = kept[...] + got[...].astype(F32)
    own[...] = total[:requests]
    for k, block in enumerate(blocks):
        block[...] = total[(k + 1) * requests : (k + 2) * requests].astype(BF16)


def shared_kernel(x, gate, up, down, _, out, gate_v, up_v, down_v, sems):
    copies = [
        pltpu.make_async_copy(gate, gate_v, sems.at[0]),
        pltpu.make_async_copy(up, up_v, sems.at[1]),
        pltpu.make_async_copy(down, down_v, sems.at[2]),
    ]
    for copy in copies:
        copy.start()
    copies[0].wait()
    gate_val = lax.dot_general(x[...], gate_v[...], NT, preferred_element_type=F32)
    copies[1].wait()
    up_val = lax.dot_general(x[...], up_v[...], NT, preferred_element_type=F32)
    hid = (silu(gate_val) * up_val).astype(BF16)
    copies[2].wait()
    out[...] = jnp.dot(hid, down_v[...], preferred_element_type=F32)


def total_kernel(first, count, table, slot, lat, own, shared, *refs):
    others, (total, lat_out, sems) = refs[:-3], refs[-3:]
    copies = copy_pages(table, slot, lat, lat_out, sems, first, count)
    value = own[...] + shared[...]
    for other in others:
        value += other[...].astype(F32)
    total[...] = value
    for copy in copies:
        copy.wait()


def token_spot(r, table, lengths, rank):
    per_dev = table.shape[1]
    local = lengths[r] // PAGE - rank[0] * per_dev
    owned = (local >= 0) & (local < per_dev)
    local = jnp.clip(local, 0, per_dev - 1)
    inside = lengths[r] % PAGE
    return owned, local, table[r, local], inside, pl.multiple_of(inside // 16 * 16, 16)


def cache_kernel(
    first, table, slot, _, lat, rope, got_lat, got_rope,
    lat_out, rope_out, token, lat_v, rope_v, got_sems, in_sems, sems,
):
    requests, per_dev = table.shape
    moved = slot[0]
    start = moved * per_dev
    fetches = [
        pltpu.make_async_copy(got_lat, lat_v.at[pl.ds(start, first)], got_sems.at[0]),
        pltpu.make_async_copy(got_rope, rope_v.at[pl.ds(start, per_dev)], got_sems.at[1]),
    ]

    def reads(r, j):
        n = r * per_dev + j
        page = table[r, j]
        return (
            pltpu.make_async_copy(lat.at[page], lat_v.at[n], in_sems.at[0, n]),
            pltpu.make_async_copy(rope.at[page], rope_v.at[n], in_sems.at[1, n]),
        )

    def lat_write(r, j):
        n = r * per_dev + j
        return pltpu.make_async_copy(lat_v.at[n], lat_out.at[table[r, j]], sems.at[0, n])

    def rope_write(r, j):
        n = r * per_dev + j
        return pltpu.make_async_copy(rope_v.at[n], rope_out.at[table[r, j]], sems.at[1, n])

    for r in range(requests):
        @pl.when(moved != r)
        def _():
            for j in range(per_dev):
                for copy in reads(r, j):
                    copy.start()

    for copy in fetches:
        copy.start()
    token[...] = jnp.zeros_like(token)
    for r in range(requests):
        @pl.when(moved != r)
        def _():
            for j in range(per_dev):
                for copy in reads(r, j):
                    copy.wait()
                lat_write(r, j).start()
                rope_write(r, j).start()

    for copy in fetches:
        copy.wait()
    for j in range(per_dev):
        if j < first:
            lat_write(moved, j).start()
        rope_write(moved, j).start()
    for r in range(requests):
        for j in range(per_dev):
            rope_write(r, j).wait()
            if j < first:
                lat_write(r, j).wait()
            else:
                @pl.when(moved != r)
                def _():
                    lat_write(r, j).wait()


def token_kernel(
    first, last, table, slot, lengths, rank, new_lat, new_rope, got, _, lat_in, rope_in,
    lat_out, rope_out, got_v, lat_tile, rope_tile, got_sem, sems, tile_sems,
):
    requests, _ = table.shape
    moved = slot[0]
    fetch = pltpu.make_async_copy(got.at[pl.ds(0, got_v.shape[0])], got_v, got_sem.at[0])
    fetch.start()
    spots = [token_spot(r, table, lengths, rank) for r in range(requests)]

    def received(r):
        local = spots[r][1]
        return (moved == r) & (local >= first) & (local < last)

    def lat_read(r):
        _, _, page, _, group = spots[r]
        return pltpu.make_async_copy(lat_in.at[page, pl.ds(group, 16), :], lat_tile.at[r], tile_sems.at[0, r])

    def rope_read(r):
        return pltpu.make_async_copy(rope_in.at[spots[r][2]], rope_tile.at[r], tile_sems.at[1, r])

    def lat_write(r):
        _, _, page, _, group = spots[r]
        return pltpu.make_async_copy(lat_tile.at[r], lat_out.at[page, pl.ds(group, 16), :], tile_sems.at[0, r])

    def rope_write(r):
        return pltpu.make_async_copy(rope_tile.at[r], rope_out.at[spots[r][2]], tile_sems.at[1, r])

    def in_pool(r):
        owned, local = spots[r][:2]
        return owned & ((moved != r) | (local < first))

    for r in range(requests):
        @pl.when(spots[r][0])
        def _():
            rope_read(r).start()

        @pl.when(in_pool(r))
        def _():
            lat_read(r).start()

    fetch.wait()
    for r in range(requests):
        owned, local, _, inside, group = spots[r]

        @pl.when(owned & received(r))
        def _():
            index = jnp.clip(local - first, 0, last - first - 1)
            piece = pl.ds(pl.multiple_of(index * PAGE + group, 16), 16)
            tile = got_v[piece, :].astype(F32)
            row = lax.broadcasted_iota(jnp.int32, tile.shape, 0)
            got_v[piece, :] = jnp.where(
                row == inside - group, new_lat[r : r + 1, :], tile
            ).astype(BF16)

    pages = [
        pltpu.make_async_copy(
            got_v.at[pl.ds(j * PAGE, PAGE)], lat_out.at[table[moved, first + j]], sems.at[j]
        )
        for j in range(last - first)
    ]
    for copy in pages:
        copy.start()
    for r in range(requests):
        owned, local, _, inside, group = spots[r]

        @pl.when(owned)
        def _():
            rope_read(r).wait()
            lane = lax.broadcasted_iota(jnp.int32, rope_tile.shape[1:], 1)
            rope_tile[r] = jnp.where(
                lane == inside, new_rope[:, r : r + 1], rope_tile[r].astype(F32)
            ).astype(BF16)
            rope_write(r).start()

        @pl.when(in_pool(r))
        def _():
            lat_read(r).wait()
            row = lax.broadcasted_iota(jnp.int32, lat_tile.shape[1:], 0)
            lat_tile[r] = jnp.where(
                row == inside - group, new_lat[r : r + 1, :], lat_tile[r].astype(F32)
            ).astype(BF16)
            lat_write(r).start()

    for r in range(requests):
        @pl.when(spots[r][0])
        def _():
            rope_write(r).wait()

        @pl.when(in_pool(r))
        def _():
            lat_write(r).wait()
    for copy in pages:
        copy.wait()


def last_kernel(first, table, slot, lengths, rank, new_lat, got, _, lat_out, pages, in_sem, sems):
    per_dev = table.shape[1]
    moved = slot[0]
    count = per_dev - first
    fetch = pltpu.make_async_copy(got, pages, in_sem.at[0])
    fetch.start()
    fetch.wait()
    owned, local, _, inside, group = token_spot(moved, table, lengths, rank)

    @pl.when(owned & (local >= first))
    def _():
        index = jnp.maximum(local - first, 0)
        piece = pl.ds(pl.multiple_of(index * PAGE + group, 16), 16)
        tile = pages[piece, :].astype(F32)
        row = lax.broadcasted_iota(jnp.int32, tile.shape, 0)
        pages[piece, :] = jnp.where(
            row == inside - group, new_lat[pl.ds(moved, 1), :], tile
        ).astype(BF16)

    copies = [
        pltpu.make_async_copy(
            pages.at[pl.ds(j * PAGE, PAGE)], lat_out.at[table[moved, first + j]], sems.at[j]
        )
        for j in range(count)
    ]
    for copy in copies:
        copy.start()
    for copy in copies:
        copy.wait()


def body(
    hidden,
    lengths,
    page_table,
    move_slot,
    lat_pool,
    rope_pool,
    norm_attn,
    w_query,
    w_latent,
    latent_gain,
    w_key_up,
    w_value_up,
    w_output,
    norm_ffn,
    w_router,
    route_ids,
    expert_gate,
    expert_up,
    expert_down,
    shared_gate,
    shared_up,
    shared_down,
):
    requests, size = hidden.shape
    per_dev = page_table.shape[1]
    local_heads, nope_size, lat_size = w_key_up.shape
    local_experts, _, units = expert_gate.shape
    n_tp, n_rep = lax.axis_size("tp"), lax.axis_size("rep")
    groups = n_rep // 2
    half = n_rep // 2
    rows = local_heads * requests
    everyone = n_rep * requests
    pages = requests * per_dev
    width = lat_size + LANES
    tp_one = lax.axis_index("tp").astype(jnp.int32)[None]
    rep_one = lax.axis_index("rep").astype(jnp.int32)[None]
    page_bytes = PAGE * (lat_size + ROPE) * 2
    dma = pltpu.SemaphoreType.DMA
    cuts = (per_dev * 6 // 10, per_dev * 8 // 10)
    first_span, second_span, third_span = cuts[0], cuts[1] - cuts[0], per_dev - cuts[1]
    lat_page = lat_pool.shape[1:]
    rope_page = rope_pool.shape[1:]
    lat_hbm, rope_hbm = in_hbm(lat_pool), in_hbm(rope_pool)
    gate_t = jnp.swapaxes(expert_gate, 1, 2).reshape(-1, size)
    up_t = jnp.swapaxes(expert_up, 1, 2).reshape(-1, size)

    q_own, normed, out_first, out_rope = call(
        functools.partial(query_kernel, first_span),
        (
            struct((rows, lat_size + ROPE), BF16),
            struct((requests, size), BF16),
            struct((first_span,) + lat_page, BF16),
            struct((per_dev,) + rope_page, BF16),
        ),
        [ANY] * 8,
        (VMEM,) * 4,
        [
            pltpu.SMEM(page_table.shape, jnp.int32),
            pltpu.SMEM((1,), jnp.int32),
            pltpu.VMEM(hidden.shape, BF16),
            pltpu.VMEM((1, size), F32),
            pltpu.VMEM(w_query.shape, BF16),
            pltpu.VMEM(w_key_up.shape, BF16),
            dma((2, per_dev)),
            dma((9,)),
        ],
        vmem=8,
        flops=2 * requests * w_query.size,
        nbytes=2 * w_query.size,
    )(
        page_table, move_slot, in_hbm(hidden), in_hbm(norm_attn[None, :]),
        in_hbm(w_query), in_hbm(w_key_up), lat_hbm, rope_hbm,
    )
    got_first = xored(out_first, "rep", half)
    got_rope = xored(out_rope, "rep", half)
    q_blocks = [q_own] + [xored(q_own, "tp", k) for k in range(1, n_tp)]

    lat_v, rope_v, new = call(
        fetch_kernel,
        (
            pltpu.VMEM((pages,) + lat_page, BF16),
            pltpu.VMEM((pages,) + rope_page, BF16),
            struct((requests, width), F32),
        ),
        [SMEM] * 2 + [VMEM] * 2 + [ANY] * 3,
        (VMEM,) * 3,
        [pltpu.VMEM((w_latent.shape[1], size), BF16), dma((2, pages)), dma((1,))],
        vmem=6,
        flops=2 * requests * w_latent.size,
        nbytes=pages * page_bytes + 2 * w_latent.size,
    )(page_table, lengths, normed, latent_gain[None, :], in_hbm(w_latent.T), lat_hbm, rope_hbm)

    *partial, value_v, out_v = call(
        functools.partial(attention_kernel, n_tp, per_dev, requests, lat_size),
        tuple(struct((rows, width), F32) for _ in range(n_tp))
        + (pltpu.VMEM(w_value_up.shape, BF16), pltpu.VMEM(w_output.shape, BF16)),
        [SMEM, SMEM] + [VMEM] * (n_tp + 2) + [ANY, ANY],
        (VMEM,) * (n_tp + 2),
        [pltpu.VMEM((width // LANES, n_tp * rows, LANES), F32)] * 2 + [dma((2,))],
        vmem=6,
        flops=4 * n_tp * rows * per_dev * PAGE * lat_size,
        nbytes=pages * page_bytes,
    )(lengths, tp_one, *q_blocks, lat_v, rope_v, in_hbm(w_value_up), in_hbm(w_output))
    parts = [partial[0]] + [xored(partial[k], "tp", k) for k in range(1, n_tp)]

    out_part = call(
        functools.partial(finish_kernel, n_tp, requests, lat_size),
        struct((requests, size), F32),
        [VMEM] * (n_tp + 4),
        VMEM,
        vmem=4,
        flops=2 * requests * size * w_output.shape[0],
        nbytes=2 * w_output.size + 2 * w_value_up.size,
    )(*parts, q_own, new, value_v, out_v)
    out_parts = [out_part] + [xored(out_part, "tp", k) for k in range(1, n_tp)]

    ffn_row, h_one = call(
        functools.partial(norm_kernel, n_tp),
        (
            struct((requests, size + LANES), BF16),
            struct((requests, size), BF16),
        ),
        [SMEM] + [VMEM] * (n_tp + 2) + [ANY] * 2,
        (VMEM,) * 2,
        vmem=4,
        nbytes=8 * n_tp * requests * size,
    )(move_slot, *out_parts, hidden, norm_ffn[None, :], got_first, got_rope)

    pair = jnp.concatenate([ffn_row, xored(ffn_row, "rep", 1)], axis=0)
    pieces = [pair] + [xored(pair, "rep", 2 * k) for k in range(1, groups)]

    lat_most, rope_most, cache_token = call(
        functools.partial(cache_kernel, first_span),
        (struct(lat_pool.shape, BF16), struct(rope_pool.shape, BF16), struct((8, LANES), F32)),
        [SMEM] * 2 + [VMEM] + [ANY] * 4,
        (ANY, ANY, VMEM),
        [
            pltpu.VMEM((pages,) + lat_page, BF16),
            pltpu.VMEM((pages,) + rope_page, BF16),
            dma((2,)),
            dma((2, pages)),
            dma((2, pages)),
        ],
        vmem=8,
        nbytes=2 * pages * page_bytes,
    )(page_table, move_slot, pair, lat_hbm, rope_hbm, got_first, got_rope)

    x_all, coef, x_own, out_second = call(
        functools.partial(order_kernel, groups, requests, cuts[0], second_span),
        (
            struct((everyone, size), BF16),
            struct((everyone, w_router.shape[1]), F32),
            struct((requests, size), BF16),
            struct((second_span * PAGE + ROWS, lat_size), BF16),
        ),
        [SMEM] * 3 + [VMEM] * 2 + [ANY] + [VMEM] * (groups + 3),
        (VMEM,) * 4,
        [dma((second_span,))],
        vmem=6,
        flops=4 * everyone * size * everyone,
        nbytes=4 * everyone * size,
    )(page_table, move_slot, rep_one, route_ids, w_router.T, lat_hbm, *pieces, h_one, new, cache_token)
    got_second = xored(out_second, "rep", half)
    got_row = got_second[second_span * PAGE :].reshape(1, -1)[:, : size + width]

    kept, sent = call(
        functools.partial(expert_kernel, requests, 256, units),
        (struct((groups * requests, size), F32), struct((groups * requests, size), BF16)),
        [SMEM] + [VMEM] * 2 + [ANY] * 3,
        (VMEM, VMEM),
        [pltpu.VMEM((local_experts * units, size), BF16)] * 3
        + [pltpu.VMEM((everyone, size), F32), dma((3, pl.cdiv(local_experts * units, 256)))],
        vmem=40,
        flops=6 * everyone * expert_gate.size,
        nbytes=6 * expert_gate.size,
    )(
        rep_one, x_all, coef,
        in_hbm(gate_t),
        in_hbm(up_t),
        in_hbm(expert_down.reshape(-1, size)),
    )
    summed = call(
        functools.partial(pair_kernel, requests),
        (struct((requests, size), F32),) + (struct((requests, size), BF16),) * (groups - 1),
        [VMEM, VMEM, ANY],
        (VMEM,) * groups,
        vmem=4,
        nbytes=8 * everyone * size,
    )(kept, xored(sent, "rep", 1), got_second)
    others = [xored(summed[k], "rep", 2 * k) for k in range(1, groups)]
    shared_part = call(
        shared_kernel,
        struct((requests, size), F32),
        [VMEM] + [ANY] * 4,
        VMEM,
        [
            pltpu.VMEM((shared_gate.shape[1], size), BF16),
            pltpu.VMEM((shared_gate.shape[1], size), BF16),
            pltpu.VMEM(shared_down.shape, BF16),
            dma((3,)),
        ],
        vmem=12,
        flops=6 * requests * shared_gate.size,
        nbytes=6 * shared_gate.size,
    )(x_own, in_hbm(shared_gate.T), in_hbm(shared_up.T), in_hbm(shared_down), summed[0])
    total, out_third = call(
        functools.partial(total_kernel, cuts[1], third_span),
        (struct((requests, size), F32), struct((third_span * PAGE, lat_size), BF16)),
        [SMEM, SMEM, ANY] + [VMEM] * (groups + 1),
        (VMEM, VMEM),
        [dma((third_span,))],
        vmem=4,
        nbytes=8 * everyone * size,
    )(page_table, move_slot, lat_hbm, summed[0], shared_part, *others)
    got_third = xored(out_third, "rep", half)

    is_moved = (jnp.arange(requests, dtype=jnp.int32) == move_slot[0])[:, None]
    new_served = jnp.where(is_moved, got_row[:, size:].astype(F32), new)
    marks = new_served[:, lat_size + ROPE : lat_size + ROPE + 2].astype(jnp.int32)
    len_served = marks[:, 0] * PAGE + marks[:, 1]
    lat_new = new_served[:, :lat_size]
    rope_new = new_served[:, lat_size : lat_size + ROPE].T
    lat_most, rope_cache = call(
        functools.partial(token_kernel, cuts[0], cuts[1]),
        (struct(lat_pool.shape, BF16), struct(rope_pool.shape, BF16)),
        [SMEM] * 4 + [VMEM] * 2 + [ANY, VMEM] + [ANY] * 2,
        (ANY, ANY),
        [
            pltpu.VMEM((second_span * PAGE, lat_size), BF16),
            pltpu.VMEM((requests, 16, lat_size), BF16),
            pltpu.VMEM((requests,) + rope_page, BF16),
            dma((1,)),
            dma((second_span,)),
            dma((2, requests)),
        ],
        vmem=2,
        nbytes=2 * second_span * page_bytes,
        aliases={8: 0, 9: 1},
    )(
        page_table, move_slot, len_served, tp_one, lat_new, rope_new, got_second, total,
        lat_most, rope_most,
    )

    total_all = total
    for other in [xored(total, "tp", k) for k in range(1, n_tp)]:
        total_all = total_all + other
    h_served = jnp.where(is_moved, got_row[:, :size], h_one)
    mixed = (h_served.astype(F32) + total_all).astype(BF16)

    lat_cache = call(
        functools.partial(last_kernel, cuts[1]),
        struct(lat_pool.shape, BF16),
        [SMEM] * 4 + [VMEM] + [ANY] * 2,
        ANY,
        [pltpu.VMEM((third_span * PAGE, lat_size), BF16), dma((1,)), dma((third_span,))],
        vmem=2,
        nbytes=2 * third_span * page_bytes,
        aliases={6: 0},
    )(page_table, move_slot, len_served, tp_one, lat_new, got_third, lat_most)
    return (mixed, lat_cache, rope_cache)


def solution(mesh):
    in_specs = (
        P("rep", None),
        P("rep"),
        P("rep", "tp"),
        P("rep"),
        P(("rep", "tp"), None, None),
        P(("rep", "tp"), None, None),
        P(),
        P(None, "tp"),
        P(),
        P(),
        P("tp", None, None),
        P("tp", None, None),
        P("tp", None),
        P(),
        P(),
        P(),
        P("rep", None, "tp"),
        P("rep", None, "tp"),
        P("rep", "tp", None),
        P(None, "tp"),
        P(None, "tp"),
        P("tp", None),
    )
    out_specs = (P("rep", None), P(("rep", "tp"), None, None), P(("rep", "tp"), None, None))
    return jax.shard_map(body, mesh=mesh, in_specs=in_specs, out_specs=out_specs, check_vma=False)
```

```python
import functools

import jax
import jax.numpy as jnp
from jax import lax
from jax.experimental import pallas as pl
from jax.experimental.pallas import tpu as pltpu
from jax.sharding import PartitionSpec as P

NOPE = 128
ROPE = 64
SINKS = 4
WIN = 4096
PAGE = 128
LANES = 128
ROWS = 16
EPS = 1e-06
ROUTE_SCALE = 2.446
NEG = -1e30
F32 = jnp.float32
BF16 = jnp.bfloat16
NT = (((1,), (1,)), ((), ()))

VMEM = pl.BlockSpec(memory_space=pltpu.VMEM)
SMEM = pl.BlockSpec(memory_space=pltpu.SMEM)
ANY = pl.BlockSpec(memory_space=pl.ANY)


def xored(value, axis, mask):
    pairs = [(source, source ^ mask) for source in range(lax.axis_size(axis))]
    return lax.ppermute(value, axis, pairs)


def call(kernel, out_shape, in_specs, out_specs, scratch=(), vmem=8, flops=0, nbytes=0, aliases=None):
    return pl.pallas_call(
        kernel,
        out_shape=out_shape,
        in_specs=in_specs,
        out_specs=out_specs,
        scratch_shapes=list(scratch),
        input_output_aliases=aliases or {},
        compiler_params=pltpu.CompilerParams(vmem_limit_bytes=vmem * 1024 * 1024),
        cost_estimate=pl.CostEstimate(flops=flops, bytes_accessed=nbytes, transcendentals=0),
    )


def struct(shape, dtype):
    return jax.ShapeDtypeStruct(shape, dtype)


def in_hbm(value):
    return pltpu.with_memory_space_constraint(value, pltpu.HBM)


def rms_norm(values, gain):
    return values * lax.rsqrt(jnp.mean(values * values, axis=-1, keepdims=True) + EPS) * gain


def silu(value):
    return value / (1.0 + jnp.exp(-value))


def query_kernel(
    first, table_in, slot_in, x_in, gain_in, w_in, key_in, lat, rope,
    q_out, normed_out, lat_out, rope_out,
    table, slot, x, gain, w_query, key_up, sems, in_sems,
):
    per_dev = table.shape[1]
    size = x.shape[1]
    parts = in_sems.shape[0] - 5
    step = size // parts
    small = [
        pltpu.make_async_copy(source, target, in_sems.at[i])
        for i, (source, target) in enumerate(
            [(table_in, table), (slot_in, slot), (x_in, x), (gain_in, gain)]
        )
    ]
    for copy in small:
        copy.start()
    big = []
    for i in range(parts):
        piece = pl.ds(i * step, step)
        big.append(pltpu.make_async_copy(w_in.at[piece], w_query.at[piece], in_sems.at[4 + i]))
    big.append(pltpu.make_async_copy(key_in, key_up, in_sems.at[4 + parts]))
    for copy in big:
        copy.start()
    small[0].wait()
    small[1].wait()
    copies = []
    for j in range(per_dev):
        page = table[slot[0], j]
        if j < first:
            copies.append(pltpu.make_async_copy(lat.at[page], lat_out.at[j], sems.at[0, j]))
        copies.append(pltpu.make_async_copy(rope.at[page], rope_out.at[j], sems.at[1, j]))
    for copy in copies:
        copy.start()
    small[2].wait()
    small[3].wait()
    normed = rms_norm(x[...].astype(F32), gain[...]).astype(BF16)
    normed_out[...] = normed
    heads, nope, _ = key_up.shape
    query = None
    for i in range(parts):
        big[i].wait()
        piece = slice(i * step, (i + 1) * step)
        term = jnp.dot(normed[:, piece], w_query[piece, :], preferred_element_type=F32)
        query = term if query is None else query + term
    big[parts].wait()
    wide = query.shape[1] // heads
    rows = []
    for h in range(heads):
        one = query[:, h * wide : (h + 1) * wide]
        q_lat = jnp.dot(one[:, :nope].astype(BF16), key_up[h], preferred_element_type=F32)
        rows.append(jnp.concatenate([q_lat, one[:, nope:]], axis=1))
    q_out[...] = jnp.concatenate(rows, axis=0).astype(BF16)
    for copy in copies:
        copy.wait()


def fetch_kernel(table, _, lat, rope, lat_v, rope_v, token, sems):
    token[...] = jnp.zeros_like(token)
    requests, per_dev = table.shape
    copies = []
    for r in range(requests):
        for j in range(per_dev):
            n = r * per_dev + j
            page = table[r, j]
            copies.append(pltpu.make_async_copy(lat.at[page], lat_v.at[n], sems.at[0, n]))
            copies.append(pltpu.make_async_copy(rope.at[page], rope_v.at[n], sems.at[1, n]))
    for copy in copies:
        copy.start()
    for copy in copies:
        copy.wait()


def token_weights_kernel(
    lengths, normed, gain, _, w_latent, value_up, w_out, value_v, out_v, new_out, latent_v, sems,
):
    copies = [
        pltpu.make_async_copy(w_latent, latent_v, sems.at[0]),
        pltpu.make_async_copy(value_up, value_v, sems.at[1]),
        pltpu.make_async_copy(w_out, out_v, sems.at[2]),
    ]
    for copy in copies:
        copy.start()
    size = gain.shape[1]
    copies[0].wait()
    latent = lax.dot_general(normed[...], latent_v[...], NT, preferred_element_type=F32)
    c_new = rms_norm(latent[:, :size], gain[...]).astype(BF16).astype(F32)
    p_new = latent[:, size:].astype(BF16).astype(F32)
    lane = lax.broadcasted_iota(jnp.int32, (1, LANES), 1)
    marks = []
    for r in range(normed.shape[0]):
        page = jnp.full((1, LANES), lengths[r] // PAGE, jnp.int32)
        inside = jnp.full((1, LANES), lengths[r] % PAGE, jnp.int32)
        marks.append(jnp.where(lane == 0, page, jnp.where(lane == 1, inside, 0)))
    mark = jnp.concatenate(marks, axis=0).astype(F32)
    new_out[...] = jnp.concatenate([c_new, p_new, mark[:, : LANES - ROPE]], axis=1)
    copies[1].wait()
    copies[2].wait()


def attention_kernel(blocks, per_dev, requests, lat_size, *refs):
    table, slot, lengths, rank = refs[:4]
    queries = refs[4 : 4 + blocks]
    lat, rope = refs[4 + blocks : 6 + blocks]
    outs = refs[6 + blocks : 6 + 2 * blocks]
    lat_out, rope_out, q_all, result, sems = refs[6 + 2 * blocks :]

    def own_pages(r):
        copies = []
        for j in range(per_dev):
            n = r * per_dev + j
            page = table[r, j]
            copies.append(pltpu.make_async_copy(lat.at[n], lat_out.at[page], sems.at[0, n]))
            copies.append(pltpu.make_async_copy(rope.at[n], rope_out.at[page], sems.at[1, n]))
        return copies

    for r in range(requests):
        @pl.when(slot[0] != r)
        def _():
            for copy in own_pages(r):
                copy.start()

    rows = queries[0].shape[0]
    heads = blocks * rows // requests
    scale = (NOPE + ROPE) ** (-0.5)
    tiles = lat_size // LANES
    for k in range(blocks):
        block = queries[k][...].astype(F32)
        for i in range(tiles + 1):
            piece = block[:, i * LANES : (i + 1) * LANES]
            q_all[i, k * rows : (k + 1) * rows, : piece.shape[1]] = piece
    base = rank[0] * (per_dev * PAGE)
    side = lax.broadcasted_iota(jnp.int32, (heads, LANES), 1)

    def attend(r, count):
        mine = pl.ds(r, heads, stride=requests)
        length = lengths[r]
        q_lat = jnp.concatenate([q_all[i, mine, :] for i in range(tiles)], axis=1).astype(BF16)
        q_pos = q_all[tiles, mine, :][:, :ROPE].astype(BF16)
        start = r * per_dev
        latents = lat[start : start + count].reshape(count * PAGE, lat_size)
        scores = lax.dot_general(q_lat, latents, NT, preferred_element_type=F32)
        scores += jnp.concatenate(
            [
                jnp.dot(q_pos, rope[start + j], preferred_element_type=F32)
                for j in range(count)
            ],
            axis=1,
        )
        scores *= scale
        position = base + lax.broadcasted_iota(jnp.int32, scores.shape, 1)
        allowed = (position < length) & ((position < SINKS) | (position >= length + 1 - WIN))
        peak = jnp.max(jnp.where(allowed, scores, NEG), axis=1, keepdims=True)
        weights = jnp.where(allowed, jnp.exp(scores - peak), 0.0).astype(BF16)
        total = jnp.sum(weights.astype(F32), axis=1, keepdims=True)
        sums = jnp.dot(weights, latents, preferred_element_type=F32)
        for i in range(tiles):
            result[i, mine, :] = sums[:, i * LANES : (i + 1) * LANES]
        result[tiles, mine, :] = jnp.where(side < LANES // 2, peak, total)

    few = min(2, per_dev)
    for r in range(requests):
        length = lengths[r]
        past = length <= base
        short = length <= base + few * PAGE

        @pl.when(past)
        def _():
            mine = pl.ds(r, heads, stride=requests)
            for i in range(tiles):
                result[i, mine, :] = jnp.zeros((heads, LANES), F32)
            result[tiles, mine, :] = jnp.where(side < LANES // 2, NEG, 0.0)

        @pl.when(jnp.logical_not(past) & short)
        def _():
            attend(r, few)

        @pl.when(jnp.logical_not(short))
        def _():
            attend(r, per_dev)

    for k in range(blocks):
        block = pl.ds(k * rows, rows)
        marks = result[tiles, block, :]
        peak, total = marks[:, :1], marks[:, LANES // 2 : LANES // 2 + 1]
        some = total > 0.0
        safe = jnp.where(some, total, 1.0)
        level = jnp.where(some, peak + jnp.log(safe), NEG)
        high = level.astype(BF16).astype(F32)
        middle = (level - high).astype(BF16).astype(F32)
        low = level - high - middle
        lane = lax.broadcasted_iota(jnp.int32, marks.shape, 1)
        split = jnp.where(lane == 0, high, jnp.where(lane == 1, middle, low))
        share = 1.0 / safe
        pieces = [result[i, block, :] * share for i in range(tiles)] + [split]
        outs[k][...] = jnp.concatenate(pieces, axis=1).astype(BF16)
    for r in range(requests):
        @pl.when(slot[0] != r)
        def _():
            for copy in own_pages(r):
                copy.wait()


def finish_kernel(blocks, requests, lat_size, *refs):
    parts = refs[:blocks]
    query, new, value_up, w_out, out, sent = refs[blocks:]
    local_heads = value_up.shape[0]
    scale = (NOPE + ROPE) ** (-0.5)
    fresh = jnp.concatenate([new[:, : lat_size + ROPE]] * local_heads, axis=0)
    q_own = query[...].astype(F32)
    new_score = jnp.sum(q_own * fresh, axis=1, keepdims=True) * scale
    peak = new_score
    means = []
    for part in parts:
        wide = part[...].astype(F32)
        marks = wide[:, lat_size:]
        level = marks[:, 0:1] + marks[:, 1:2] + marks[:, 2:3]
        means.append((level, wide[:, :lat_size]))
        peak = jnp.maximum(peak, level)
    new_factor = jnp.exp(new_score - peak)
    denom = new_factor
    numer = new_factor * fresh[:, :lat_size]
    for level, mean in means:
        factor = jnp.exp(level - peak)
        denom += factor
        numer += factor * mean
    o_lat = numer / denom
    vals = []
    for h in range(local_heads):
        one = o_lat[h * requests : (h + 1) * requests, :].astype(BF16)
        vals.append(jnp.dot(one, value_up[h], preferred_element_type=F32).astype(BF16))
    o_val = jnp.concatenate(vals, axis=1)
    value = jnp.dot(o_val, w_out[...], preferred_element_type=F32)
    out[...] = value
    sent[...] = value.astype(BF16)


def norm_kernel(blocks, *refs):
    slot = refs[0]
    parts = refs[1 : 1 + blocks]
    x, gain = refs[1 + blocks : 3 + blocks]
    row_out, h_out = refs[-2:]
    attn = parts[0][...]
    for part in parts[1:]:
        attn += part[...].astype(F32)
    h_one = (x[...].astype(F32) + attn).astype(BF16)
    h_out[...] = h_one
    wide = h_one.astype(F32)
    normed = rms_norm(wide, gain[...])
    mark = jnp.full((wide.shape[0], LANES), slot[0], jnp.int32).astype(F32)
    row_out[...] = jnp.concatenate([normed, mark], axis=1).astype(BF16)


def copy_pages(table, slot, lat, lat_out, sems, first, count):
    copies = [
        pltpu.make_async_copy(
            lat.at[table[slot[0], first + j]], lat_out.at[pl.ds(j * PAGE, PAGE)], sems.at[j]
        )
        for j in range(count)
    ]
    for copy in copies:
        copy.start()
    return copies


def order_kernel(groups, requests, rank, route_ids, router, *refs):
    pieces = refs[:groups]
    x_out, coef_out, own_out, _ = refs[groups + 1 :]
    size = router.shape[1]
    wide = jnp.concatenate([p[...].astype(F32) for p in pieces], axis=0)
    rows = wide.shape[0]
    reps = rows // requests
    moved = wide[:, size : size + 1]
    other = jnp.concatenate([moved[rows // 2 :], moved[: rows // 2]], axis=0)
    row = lax.broadcasted_iota(jnp.int32, (rows, 1), 0)
    place = row // requests
    across = ((place + reps // 2) % reps) * requests
    source = jnp.where(
        row % requests == moved.astype(jnp.int32), across + other.astype(jnp.int32), row
    )
    column = lax.broadcasted_iota(jnp.int32, (rows, rows), 1)
    picks = (column == source).astype(F32).astype(BF16)
    x = jnp.dot(picks, wide[:, :size].astype(BF16), preferred_element_type=F32)
    own_out[...] = x[:requests, :].astype(BF16)
    x = x.astype(BF16)
    x_out[...] = x
    gates = jax.nn.sigmoid(lax.dot_general(x, router[...], NT, preferred_element_type=F32))
    home = (place ^ rank[0]) * requests + row % requests
    turns = (column == home).astype(F32).astype(BF16)
    ids = jnp.dot(turns, route_ids[...].astype(F32).astype(BF16), preferred_element_type=F32)
    ids = ids.astype(jnp.int32)
    expert = lax.broadcasted_iota(jnp.int32, gates.shape, 1)
    chosen = jnp.zeros(gates.shape, F32)
    for k in range(ids.shape[1]):
        chosen += jnp.where(expert == ids[:, k : k + 1], gates, 0.0)
    coef_out[...] = chosen / jnp.sum(chosen, axis=1, keepdims=True) * ROUTE_SCALE


def expert_kernel(
    requests, chunk, hidden, rank, x, coef, gate, up, down, kept, sent, gate_v, up_v, down_v, total, sems,
):
    units = gate.shape[0]
    pieces = [slice(b, min(b + chunk, units)) for b in range(0, units, chunk)]

    def fetch(which, source, target, i):
        piece = pl.ds(pieces[i].start, pieces[i].stop - pieces[i].start)
        return pltpu.make_async_copy(source.at[piece], target.at[piece], sems.at[which, i])

    copies = [
        [fetch(w, s, t, i) for w, (s, t) in enumerate([(gate, gate_v), (up, up_v), (down, down_v)])]
        for i in range(len(pieces))
    ]
    for trio in copies:
        for copy in trio:
            copy.start()
    count = units // hidden
    first = rank[0] * count
    weights = coef[...]
    expert = lax.broadcasted_iota(jnp.int32, weights.shape, 1)
    shares = [
        jnp.sum(jnp.where(expert == first + e, weights, 0.0), axis=1, keepdims=True)
        for e in range(count)
    ]
    rows = x.shape[0]
    for i, piece in enumerate(pieces):
        copies[i][0].wait()
        gate_val = lax.dot_general(x[...], gate_v[piece, :], NT, preferred_element_type=F32)
        copies[i][1].wait()
        up_val = lax.dot_general(x[...], up_v[piece, :], NT, preferred_element_type=F32)
        unit = piece.start + lax.broadcasted_iota(jnp.int32, gate_val.shape, 1)
        low, high = piece.start // hidden, (piece.stop - 1) // hidden
        share = jnp.broadcast_to(shares[high], gate_val.shape)
        for e in range(high - 1, low - 1, -1):
            share = jnp.where(unit < (e + 1) * hidden, shares[e], share)
        hid = (silu(gate_val) * up_val * share).astype(BF16)
        copies[i][2].wait()
        term = jnp.dot(hid, down_v[piece, :], preferred_element_type=F32)
        if i == 0:
            total[...] = term
        else:
            total[...] += term
    value = total[...]
    blocks = [value[p * requests : (p + 1) * requests] for p in range(rows // requests)]
    kept[...] = jnp.concatenate(blocks[0::2], axis=0)
    sent[...] = jnp.concatenate(blocks[1::2], axis=0).astype(BF16)


def pair_kernel(requests, kept, got, _, own, *blocks):
    total = kept[...] + got[...].astype(F32)
    own[...] = total[:requests]
    for k, block in enumerate(blocks):
        block[...] = total[(k + 1) * requests : (k + 2) * requests].astype(BF16)


def shared_kernel(
    first, count, table, slot, x, gate, up, down, lat, _, out, lat_out, gate_v, up_v, down_v, sems, page_sems,
):
    copies = [
        pltpu.make_async_copy(gate, gate_v, sems.at[0]),
        pltpu.make_async_copy(up, up_v, sems.at[1]),
        pltpu.make_async_copy(down, down_v, sems.at[2]),
    ]
    for copy in copies:
        copy.start()
    pages = copy_pages(table, slot, lat, lat_out, page_sems, first, count)
    copies[0].wait()
    gate_val = lax.dot_general(x[...], gate_v[...], NT, preferred_element_type=F32)
    copies[1].wait()
    up_val = lax.dot_general(x[...], up_v[...], NT, preferred_element_type=F32)
    hid = (silu(gate_val) * up_val).astype(BF16)
    copies[2].wait()
    for copy in pages:
        copy.wait()
    out[...] = jnp.dot(hid, down_v[...], preferred_element_type=F32)


def total_kernel(own, shared, *refs):
    others, (total, sent) = refs[:-2], refs[-2:]
    value = own[...] + shared[...]
    for other in others:
        value += other[...].astype(F32)
    total[...] = value
    sent[...] = value.astype(BF16)


def token_spot(r, table, lengths, rank):
    per_dev = table.shape[1]
    local = lengths[r] // PAGE - rank[0] * per_dev
    owned = (local >= 0) & (local < per_dev)
    local = jnp.clip(local, 0, per_dev - 1)
    inside = lengths[r] % PAGE
    return owned, local, table[r, local], inside, pl.multiple_of(inside // 16 * 16, 16)


def cache_kernel(
    first, count, table, slot, _, h_one, new, lat, got_lat, got_rope, lat_in, rope_in,
    next_out, lat_out, rope_out, lat_v, rope_v, page_sems, got_sems, sems,
):
    del lat_in, rope_in
    per_dev = table.shape[1]
    moved = slot[0]
    fetches = [
        pltpu.make_async_copy(got_lat, lat_v, got_sems.at[0]),
        pltpu.make_async_copy(got_rope, rope_v, got_sems.at[1]),
    ]
    for copy in fetches:
        copy.start()
    copies = copy_pages(table, slot, lat, next_out, page_sems, first, count)
    both = jnp.concatenate([h_one[...].astype(F32), new[...]], axis=1)
    row = lax.broadcasted_iota(jnp.int32, both.shape, 0)
    both = jnp.sum(jnp.where(row == moved, both, 0.0), axis=0, keepdims=True)
    lat_size = next_out.shape[1]
    lines = [both[:, b : b + lat_size] for b in range(0, both.shape[1], lat_size)]
    lines[-1] = jnp.pad(lines[-1], ((0, 0), (0, lat_size - lines[-1].shape[1])))
    lines.append(jnp.zeros((ROWS - len(lines), lat_size), F32))
    next_out[count * PAGE :, :] = jnp.concatenate(lines, axis=0).astype(BF16)
    for copy in fetches:
        copy.wait()
    for j in range(per_dev):
        page = table[moved, j]
        if j < first:
            copies.append(pltpu.make_async_copy(lat_v.at[j], lat_out.at[page], sems.at[0, j]))
            copies[-1].start()
        copies.append(pltpu.make_async_copy(rope_v.at[j], rope_out.at[page], sems.at[1, j]))
        copies[-1].start()
    for copy in copies:
        copy.wait()


def token_kernel(
    first, last, table, slot, lengths, rank, new_lat, new_rope, got, _, lat_in, rope_in,
    lat_out, rope_out, got_v, lat_tile, rope_tile, got_sem, sems, tile_sems,
):
    requests, _ = table.shape
    moved = slot[0]
    fetch = pltpu.make_async_copy(got.at[pl.ds(0, got_v.shape[0])], got_v, got_sem.at[0])
    fetch.start()
    spots = [token_spot(r, table, lengths, rank) for r in range(requests)]

    def received(r):
        local = spots[r][1]
        return (moved == r) & (local >= first) & (local < last)

    def lat_read(r):
        _, _, page, _, group = spots[r]
        return pltpu.make_async_copy(lat_in.at[page, pl.ds(group, 16), :], lat_tile.at[r], tile_sems.at[0, r])

    def rope_read(r):
        return pltpu.make_async_copy(rope_in.at[spots[r][2]], rope_tile.at[r], tile_sems.at[1, r])

    def lat_write(r):
        _, _, page, _, group = spots[r]
        return pltpu.make_async_copy(lat_tile.at[r], lat_out.at[page, pl.ds(group, 16), :], tile_sems.at[0, r])

    def rope_write(r):
        return pltpu.make_async_copy(rope_tile.at[r], rope_out.at[spots[r][2]], tile_sems.at[1, r])

    def in_pool(r):
        owned, local = spots[r][:2]
        return owned & ((moved != r) | (local < first))

    for r in range(requests):
        @pl.when(spots[r][0])
        def _():
            rope_read(r).start()

        @pl.when(in_pool(r))
        def _():
            lat_read(r).start()

    fetch.wait()
    for r in range(requests):
        owned, local, _, inside, group = spots[r]

        @pl.when(owned & received(r))
        def _():
            index = jnp.clip(local - first, 0, last - first - 1)
            piece = pl.ds(pl.multiple_of(index * PAGE + group, 16), 16)
            tile = got_v[piece, :].astype(F32)
            row = lax.broadcasted_iota(jnp.int32, tile.shape, 0)
            got_v[piece, :] = jnp.where(
                row == inside - group, new_lat[r : r + 1, :], tile
            ).astype(BF16)

    pages = [
        pltpu.make_async_copy(
            got_v.at[pl.ds(j * PAGE, PAGE)], lat_out.at[table[moved, first + j]], sems.at[j]
        )
        for j in range(last - first)
    ]
    for copy in pages:
        copy.start()
    for r in range(requests):
        owned, local, _, inside, group = spots[r]

        @pl.when(owned)
        def _():
            rope_read(r).wait()
            lane = lax.broadcasted_iota(jnp.int32, rope_tile.shape[1:], 1)
            rope_tile[r] = jnp.where(
                lane == inside, new_rope[:, r : r + 1], rope_tile[r].astype(F32)
            ).astype(BF16)
            rope_write(r).start()

        @pl.when(in_pool(r))
        def _():
            lat_read(r).wait()
            row = lax.broadcasted_iota(jnp.int32, lat_tile.shape[1:], 0)
            lat_tile[r] = jnp.where(
                row == inside - group, new_lat[r : r + 1, :], lat_tile[r].astype(F32)
            ).astype(BF16)
            lat_write(r).start()

    for r in range(requests):
        @pl.when(spots[r][0])
        def _():
            rope_write(r).wait()

        @pl.when(in_pool(r))
        def _():
            lat_write(r).wait()
    for copy in pages:
        copy.wait()


def last_kernel(first, table, slot, lengths, rank, new_lat, got, _, lat_out, pages, in_sem, sems):
    per_dev = table.shape[1]
    moved = slot[0]
    count = per_dev - first
    fetch = pltpu.make_async_copy(got, pages, in_sem.at[0])
    fetch.start()
    fetch.wait()
    owned, local, _, inside, group = token_spot(moved, table, lengths, rank)

    @pl.when(owned & (local >= first))
    def _():
        index = jnp.maximum(local - first, 0)
        piece = pl.ds(pl.multiple_of(index * PAGE + group, 16), 16)
        tile = pages[piece, :].astype(F32)
        row = lax.broadcasted_iota(jnp.int32, tile.shape, 0)
        pages[piece, :] = jnp.where(
            row == inside - group, new_lat[pl.ds(moved, 1), :], tile
        ).astype(BF16)

    copies = [
        pltpu.make_async_copy(
            pages.at[pl.ds(j * PAGE, PAGE)], lat_out.at[table[moved, first + j]], sems.at[j]
        )
        for j in range(count)
    ]
    for copy in copies:
        copy.start()
    for copy in copies:
        copy.wait()


def body(
    hidden,
    lengths,
    page_table,
    move_slot,
    lat_pool,
    rope_pool,
    norm_attn,
    w_query,
    w_latent,
    latent_gain,
    w_key_up,
    w_value_up,
    w_output,
    norm_ffn,
    w_router,
    route_ids,
    expert_gate,
    expert_up,
    expert_down,
    shared_gate,
    shared_up,
    shared_down,
):
    requests, size = hidden.shape
    per_dev = page_table.shape[1]
    local_heads, nope_size, lat_size = w_key_up.shape
    local_experts, _, units = expert_gate.shape
    n_tp, n_rep = lax.axis_size("tp"), lax.axis_size("rep")
    groups = n_rep // 2
    half = n_rep // 2
    rows = local_heads * requests
    everyone = n_rep * requests
    pages = requests * per_dev
    width = lat_size + LANES
    tp_one = lax.axis_index("tp").astype(jnp.int32)[None]
    rep_one = lax.axis_index("rep").astype(jnp.int32)[None]
    page_bytes = PAGE * (lat_size + ROPE) * 2
    dma = pltpu.SemaphoreType.DMA
    cuts = (per_dev * 6 // 10, per_dev * 8 // 10)
    first_span, second_span, third_span = cuts[0], cuts[1] - cuts[0], per_dev - cuts[1]
    lat_page = lat_pool.shape[1:]
    rope_page = rope_pool.shape[1:]
    lat_hbm, rope_hbm = in_hbm(lat_pool), in_hbm(rope_pool)
    gate_t = jnp.swapaxes(expert_gate, 1, 2).reshape(-1, size)
    up_t = jnp.swapaxes(expert_up, 1, 2).reshape(-1, size)

    q_own, normed, out_first, out_rope = call(
        functools.partial(query_kernel, first_span),
        (
            struct((rows, lat_size + ROPE), BF16),
            struct((requests, size), BF16),
            struct((first_span,) + lat_page, BF16),
            struct((per_dev,) + rope_page, BF16),
        ),
        [ANY] * 8,
        (VMEM,) * 4,
        [
            pltpu.SMEM(page_table.shape, jnp.int32),
            pltpu.SMEM((1,), jnp.int32),
            pltpu.VMEM(hidden.shape, BF16),
            pltpu.VMEM((1, size), F32),
            pltpu.VMEM(w_query.shape, BF16),
            pltpu.VMEM(w_key_up.shape, BF16),
            dma((2, per_dev)),
            dma((9,)),
        ],
        vmem=8,
        flops=2 * requests * w_query.size,
        nbytes=2 * w_query.size,
    )(
        page_table, move_slot, in_hbm(hidden), in_hbm(norm_attn[None, :]),
        in_hbm(w_query), in_hbm(w_key_up), lat_hbm, rope_hbm,
    )
    got_first = xored(out_first, "rep", half)
    got_rope = xored(out_rope, "rep", half)
    q_blocks = [q_own] + [xored(q_own, "tp", k) for k in range(1, n_tp)]

    lat_v, rope_v, _ = call(
        fetch_kernel,
        (
            pltpu.VMEM((pages,) + lat_page, BF16),
            pltpu.VMEM((pages,) + rope_page, BF16),
            struct((8, LANES), F32),
        ),
        [SMEM, VMEM, ANY, ANY],
        (VMEM,) * 3,
        [dma((2, pages))],
        vmem=6,
        flops=2 * requests * w_latent.size,
        nbytes=pages * page_bytes + 2 * (w_latent.size + w_output.size + w_value_up.size),
    )(page_table, q_own, lat_hbm, rope_hbm)

    *partial, lat_most, rope_most = call(
        functools.partial(attention_kernel, n_tp, per_dev, requests, lat_size),
        tuple(struct((rows, width), BF16) for _ in range(n_tp))
        + (struct(lat_pool.shape, BF16), struct(rope_pool.shape, BF16)),
        [SMEM] * 4 + [VMEM] * (n_tp + 2),
        (VMEM,) * n_tp + (ANY, ANY),
        [pltpu.VMEM((width // LANES, n_tp * rows, LANES), F32)] * 2 + [dma((2, pages))],
        vmem=6,
        flops=4 * n_tp * rows * per_dev * PAGE * lat_size,
        nbytes=pages * page_bytes,
    )(page_table, move_slot, lengths, tp_one, *q_blocks, lat_v, rope_v)
    parts = [partial[0]] + [xored(partial[k], "tp", k) for k in range(1, n_tp)]
    value_v, out_v, new = call(
        token_weights_kernel,
        (
            pltpu.VMEM(w_value_up.shape, BF16),
            pltpu.VMEM(w_output.shape, BF16),
            struct((requests, width), F32),
        ),
        [SMEM] + [VMEM] * 3 + [ANY] * 3,
        (VMEM,) * 3,
        [pltpu.VMEM((w_latent.shape[1], size), BF16), dma((3,))],
        vmem=6,
        flops=2 * requests * w_latent.size,
        nbytes=2 * (w_latent.size + w_output.size + w_value_up.size),
    )(
        lengths, normed, latent_gain[None, :], partial[0], in_hbm(w_latent.T),
        in_hbm(w_value_up), in_hbm(w_output),
    )

    out_part, out_sent = call(
        functools.partial(finish_kernel, n_tp, requests, lat_size),
        (struct((requests, size), F32), struct((requests, size), BF16)),
        [VMEM] * (n_tp + 4),
        (VMEM, VMEM),
        vmem=4,
        flops=2 * requests * size * w_output.shape[0],
        nbytes=2 * w_output.size + 2 * w_value_up.size,
    )(*parts, q_own, new, value_v, out_v)
    out_parts = [out_part] + [xored(out_sent, "tp", k) for k in range(1, n_tp)]

    ffn_row, h_one = call(
        functools.partial(norm_kernel, n_tp),
        (
            struct((requests, size + LANES), BF16),
            struct((requests, size), BF16),
        ),
        [SMEM] + [VMEM] * (n_tp + 2) + [ANY] * 2,
        (VMEM,) * 2,
        vmem=4,
        nbytes=8 * n_tp * requests * size,
    )(move_slot, *out_parts, hidden, norm_ffn[None, :], got_first, got_rope)

    pair = jnp.concatenate([ffn_row, xored(ffn_row, "rep", 1)], axis=0)
    pieces = [pair] + [xored(pair, "rep", 2 * k) for k in range(1, groups)]

    out_second, lat_most, rope_most = call(
        functools.partial(cache_kernel, first_span, second_span),
        (
            struct((second_span * PAGE + ROWS, lat_size), BF16),
            struct(lat_pool.shape, BF16),
            struct(rope_pool.shape, BF16),
        ),
        [SMEM] * 2 + [VMEM] * 3 + [ANY] * 5,
        (VMEM, ANY, ANY),
        [
            pltpu.VMEM((first_span,) + lat_page, BF16),
            pltpu.VMEM((per_dev,) + rope_page, BF16),
            dma((second_span,)),
            dma((2,)),
            dma((2, per_dev)),
        ],
        vmem=4,
        nbytes=2 * first_span * page_bytes,
        aliases={8: 1, 9: 2},
    )(
        page_table, move_slot, pair, h_one, new, lat_hbm, got_first, got_rope,
        lat_most, rope_most,
    )
    x_all, coef, x_own, out_second = call(
        functools.partial(order_kernel, groups, requests),
        (
            struct((everyone, size), BF16),
            struct((everyone, w_router.shape[1]), F32),
            struct((requests, size), BF16),
            struct(out_second.shape, BF16),
        ),
        [SMEM] + [VMEM] * (groups + 3),
        (VMEM,) * 4,
        vmem=6,
        flops=4 * everyone * size * everyone,
        nbytes=4 * everyone * size,
        aliases={3 + groups: 3},
    )(rep_one, route_ids, w_router.T, *pieces, out_second)
    got_second = xored(out_second, "rep", half)
    got_row = got_second[second_span * PAGE :].reshape(1, -1)[:, : size + width]

    kept, sent = call(
        functools.partial(expert_kernel, requests, 256, units),
        (
            struct((groups * requests, size), F32),
            struct((groups * requests, size), BF16),
        ),
        [SMEM] + [VMEM] * 2 + [ANY] * 3,
        (VMEM, VMEM),
        [pltpu.VMEM((local_experts * units, size), BF16)] * 3
        + [pltpu.VMEM((everyone, size), F32), dma((3, pl.cdiv(local_experts * units, 256)))],
        vmem=42,
        flops=6 * everyone * expert_gate.size,
        nbytes=6 * expert_gate.size,
    )(
        rep_one, x_all, coef, in_hbm(gate_t), in_hbm(up_t), in_hbm(expert_down.reshape(-1, size)),
    )
    summed = call(
        functools.partial(pair_kernel, requests),
        (struct((requests, size), F32),) + (struct((requests, size), BF16),) * (groups - 1),
        [VMEM, VMEM, ANY],
        (VMEM,) * groups,
        vmem=4,
        nbytes=8 * everyone * size,
    )(kept, xored(sent, "rep", 1), got_second)
    others = [xored(summed[k], "rep", 2 * k) for k in range(1, groups)]
    shared_part, out_third = call(
        functools.partial(shared_kernel, cuts[1], third_span),
        (struct((requests, size), F32), struct((third_span * PAGE, lat_size), BF16)),
        [SMEM, SMEM, VMEM] + [ANY] * 5,
        (VMEM, VMEM),
        [
            pltpu.VMEM((shared_gate.shape[1], size), BF16),
            pltpu.VMEM((shared_gate.shape[1], size), BF16),
            pltpu.VMEM(shared_down.shape, BF16),
            dma((3,)),
            dma((third_span,)),
        ],
        vmem=12,
        flops=6 * requests * shared_gate.size,
        nbytes=6 * shared_gate.size,
    )(
        page_table, move_slot, x_own, in_hbm(shared_gate.T), in_hbm(shared_up.T),
        in_hbm(shared_down), lat_hbm, summed[0],
    )
    total, total_sent = call(
        total_kernel,
        (struct((requests, size), F32), struct((requests, size), BF16)),
        [VMEM] * (groups + 1),
        (VMEM, VMEM),
        vmem=4,
        nbytes=8 * everyone * size,
    )(summed[0], shared_part, *others)
    got_third = xored(out_third, "rep", half)

    is_moved = (jnp.arange(requests, dtype=jnp.int32) == move_slot[0])[:, None]
    new_served = jnp.where(is_moved, got_row[:, size:].astype(F32), new)
    marks = new_served[:, lat_size + ROPE : lat_size + ROPE + 2].astype(jnp.int32)
    len_served = marks[:, 0] * PAGE + marks[:, 1]
    lat_new = new_served[:, :lat_size]
    rope_new = new_served[:, lat_size : lat_size + ROPE].T
    lat_most, rope_cache = call(
        functools.partial(token_kernel, cuts[0], cuts[1]),
        (struct(lat_pool.shape, BF16), struct(rope_pool.shape, BF16)),
        [SMEM] * 4 + [VMEM] * 2 + [ANY, VMEM] + [ANY] * 2,
        (ANY, ANY),
        [
            pltpu.VMEM((second_span * PAGE, lat_size), BF16),
            pltpu.VMEM((requests, 16, lat_size), BF16),
            pltpu.VMEM((requests,) + rope_page, BF16),
            dma((1,)),
            dma((second_span,)),
            dma((2, requests)),
        ],
        vmem=2,
        nbytes=2 * second_span * page_bytes,
        aliases={8: 0, 9: 1},
    )(
        page_table, move_slot, len_served, tp_one, lat_new, rope_new, got_second, total,
        lat_most, rope_most,
    )

    total_all = total
    for other in [xored(total_sent, "tp", k) for k in range(1, n_tp)]:
        total_all = total_all + other.astype(F32)
    h_served = jnp.where(is_moved, got_row[:, :size], h_one)
    mixed = (h_served.astype(F32) + total_all).astype(BF16)

    lat_cache = call(
        functools.partial(last_kernel, cuts[1]),
        struct(lat_pool.shape, BF16),
        [SMEM] * 4 + [VMEM] + [ANY] * 2,
        ANY,
        [pltpu.VMEM((third_span * PAGE, lat_size), BF16), dma((1,)), dma((third_span,))],
        vmem=2,
        nbytes=2 * third_span * page_bytes,
        aliases={6: 0},
    )(page_table, move_slot, len_served, tp_one, lat_new, got_third, lat_most)
    return (mixed, lat_cache, rope_cache)


def solution(mesh):
    in_specs = (
        P("rep", None),
        P("rep"),
        P("rep", "tp"),
        P("rep"),
        P(("rep", "tp"), None, None),
        P(("rep", "tp"), None, None),
        P(),
        P(None, "tp"),
        P(),
        P(),
        P("tp", None, None),
        P("tp", None, None),
        P("tp", None),
        P(),
        P(),
        P(),
        P("rep", None, "tp"),
        P("rep", None, "tp"),
        P("rep", "tp", None),
        P(None, "tp"),
        P(None, "tp"),
        P("tp", None),
    )
    out_specs = (P("rep", None), P(("rep", "tp"), None, None), P(("rep", "tp"), None, None))
    return jax.shard_map(body, mesh=mesh, in_specs=in_specs, out_specs=out_specs, check_vma=False)
```

```python
import functools

import jax
import jax.numpy as jnp
from jax import lax
from jax.experimental import pallas as pl
from jax.experimental.pallas import tpu as pltpu
from jax.sharding import PartitionSpec as P

NOPE = 128
ROPE = 64
SINKS = 4
WIN = 4096
PAGE = 128
LANES = 128
ROWS = 16
EPS = 1e-06
ROUTE_SCALE = 2.446
NEG = -1e30
F32 = jnp.float32
BF16 = jnp.bfloat16
NT = (((1,), (1,)), ((), ()))

VMEM = pl.BlockSpec(memory_space=pltpu.VMEM)
SMEM = pl.BlockSpec(memory_space=pltpu.SMEM)
ANY = pl.BlockSpec(memory_space=pl.ANY)


def xored(value, axis, mask):
    pairs = [(source, source ^ mask) for source in range(lax.axis_size(axis))]
    return lax.ppermute(value, axis, pairs)


def call(kernel, out_shape, in_specs, out_specs, scratch=(), vmem=8, flops=0, nbytes=0, aliases=None):
    return pl.pallas_call(
        kernel,
        out_shape=out_shape,
        in_specs=in_specs,
        out_specs=out_specs,
        scratch_shapes=list(scratch),
        input_output_aliases=aliases or {},
        compiler_params=pltpu.CompilerParams(vmem_limit_bytes=vmem * 1024 * 1024),
        cost_estimate=pl.CostEstimate(flops=flops, bytes_accessed=nbytes, transcendentals=0),
    )


def struct(shape, dtype):
    return jax.ShapeDtypeStruct(shape, dtype)


def in_hbm(value):
    return pltpu.with_memory_space_constraint(value, pltpu.HBM)


def rms_norm(values, gain):
    return values * lax.rsqrt(jnp.mean(values * values, axis=-1, keepdims=True) + EPS) * gain


def silu(value):
    return value / (1.0 + jnp.exp(-value))


def query_kernel(
    first, table_in, slot_in, x_in, gain_in, w_in, key_in, lat, rope,
    q_out, normed_out, lat_out, rope_out,
    table, slot, x, gain, w_query, key_up, sems, in_sems,
):
    per_dev = table.shape[1]
    size = x.shape[1]
    parts = in_sems.shape[0] - 5
    step = size // parts
    small = [
        pltpu.make_async_copy(source, target, in_sems.at[i])
        for i, (source, target) in enumerate(
            [(table_in, table), (slot_in, slot), (x_in, x), (gain_in, gain)]
        )
    ]
    for copy in small:
        copy.start()
    big = []
    for i in range(parts):
        piece = pl.ds(i * step, step)
        big.append(pltpu.make_async_copy(w_in.at[piece], w_query.at[piece], in_sems.at[4 + i]))
    big.append(pltpu.make_async_copy(key_in, key_up, in_sems.at[4 + parts]))
    for copy in big:
        copy.start()
    small[0].wait()
    small[1].wait()
    copies = []
    for j in range(per_dev):
        page = table[slot[0], j]
        if j < first:
            copies.append(pltpu.make_async_copy(lat.at[page], lat_out.at[j], sems.at[0, j]))
        copies.append(pltpu.make_async_copy(rope.at[page], rope_out.at[j], sems.at[1, j]))
    for copy in copies:
        copy.start()
    small[2].wait()
    small[3].wait()
    normed = rms_norm(x[...].astype(F32), gain[...]).astype(BF16)
    normed_out[...] = normed
    heads, nope, _ = key_up.shape
    query = None
    for i in range(parts):
        big[i].wait()
        piece = slice(i * step, (i + 1) * step)
        term = jnp.dot(normed[:, piece], w_query[piece, :], preferred_element_type=F32)
        query = term if query is None else query + term
    big[parts].wait()
    wide = query.shape[1] // heads
    rows = []
    for h in range(heads):
        one = query[:, h * wide : (h + 1) * wide]
        q_lat = jnp.dot(one[:, :nope].astype(BF16), key_up[h], preferred_element_type=F32)
        rows.append(jnp.concatenate([q_lat, one[:, nope:]], axis=1))
    q_out[...] = jnp.concatenate(rows, axis=0).astype(BF16)
    for copy in copies:
        copy.wait()


def fetch_kernel(table, _, lat, rope, lat_v, rope_v, token, sems):
    token[...] = jnp.zeros_like(token)
    requests, per_dev = table.shape
    copies = []
    for r in range(requests):
        for j in range(per_dev):
            n = r * per_dev + j
            page = table[r, j]
            copies.append(pltpu.make_async_copy(lat.at[page], lat_v.at[n], sems.at[0, n]))
            copies.append(pltpu.make_async_copy(rope.at[page], rope_v.at[n], sems.at[1, n]))
    for copy in copies:
        copy.start()
    for copy in copies:
        copy.wait()


def token_weights_kernel(
    lengths, normed, gain, _, w_latent, value_up, w_out, value_v, out_v, new_out, latent_v, sems,
):
    copies = [
        pltpu.make_async_copy(w_latent, latent_v, sems.at[0]),
        pltpu.make_async_copy(value_up, value_v, sems.at[1]),
        pltpu.make_async_copy(w_out, out_v, sems.at[2]),
    ]
    for copy in copies:
        copy.start()
    size = gain.shape[1]
    copies[0].wait()
    latent = lax.dot_general(normed[...], latent_v[...], NT, preferred_element_type=F32)
    c_new = rms_norm(latent[:, :size], gain[...]).astype(BF16).astype(F32)
    p_new = latent[:, size:].astype(BF16).astype(F32)
    lane = lax.broadcasted_iota(jnp.int32, (1, LANES), 1)
    marks = []
    for r in range(normed.shape[0]):
        page = jnp.full((1, LANES), lengths[r] // PAGE, jnp.int32)
        inside = jnp.full((1, LANES), lengths[r] % PAGE, jnp.int32)
        marks.append(jnp.where(lane == 0, page, jnp.where(lane == 1, inside, 0)))
    mark = jnp.concatenate(marks, axis=0).astype(F32)
    new_out[...] = jnp.concatenate([c_new, p_new, mark[:, : LANES - ROPE]], axis=1)
    copies[1].wait()
    copies[2].wait()


def attention_kernel(blocks, per_dev, requests, lat_size, *refs):
    table, slot, lengths, rank = refs[:4]
    queries = refs[4 : 4 + blocks]
    lat, rope = refs[4 + blocks : 6 + blocks]
    outs = refs[6 + blocks : 6 + 2 * blocks]
    lat_out, rope_out, q_all, result, sems = refs[6 + 2 * blocks :]

    def own_pages(r):
        copies = []
        for j in range(per_dev):
            n = r * per_dev + j
            page = table[r, j]
            copies.append(pltpu.make_async_copy(lat.at[n], lat_out.at[page], sems.at[0, n]))
            copies.append(pltpu.make_async_copy(rope.at[n], rope_out.at[page], sems.at[1, n]))
        return copies

    for r in range(requests):
        @pl.when(slot[0] != r)
        def _():
            for copy in own_pages(r):
                copy.start()

    rows = queries[0].shape[0]
    heads = blocks * rows // requests
    scale = (NOPE + ROPE) ** (-0.5)
    tiles = lat_size // LANES
    for k in range(blocks):
        block = queries[k][...].astype(F32)
        for i in range(tiles + 1):
            piece = block[:, i * LANES : (i + 1) * LANES]
            q_all[i, k * rows : (k + 1) * rows, : piece.shape[1]] = piece
    base = rank[0] * (per_dev * PAGE)
    side = lax.broadcasted_iota(jnp.int32, (heads, LANES), 1)

    def attend(r, count):
        mine = pl.ds(r, heads, stride=requests)
        length = lengths[r]
        q_lat = jnp.concatenate([q_all[i, mine, :] for i in range(tiles)], axis=1).astype(BF16)
        q_pos = q_all[tiles, mine, :][:, :ROPE].astype(BF16)
        start = r * per_dev
        latents = lat[start : start + count].reshape(count * PAGE, lat_size)
        scores = lax.dot_general(q_lat, latents, NT, preferred_element_type=F32)
        scores += jnp.concatenate(
            [
                jnp.dot(q_pos, rope[start + j], preferred_element_type=F32)
                for j in range(count)
            ],
            axis=1,
        )
        scores *= scale
        position = base + lax.broadcasted_iota(jnp.int32, scores.shape, 1)
        allowed = (position < length) & ((position < SINKS) | (position >= length + 1 - WIN))
        peak = jnp.max(jnp.where(allowed, scores, NEG), axis=1, keepdims=True)
        weights = jnp.where(allowed, jnp.exp(scores - peak), 0.0).astype(BF16)
        total = jnp.sum(weights.astype(F32), axis=1, keepdims=True)
        sums = jnp.dot(weights, latents, preferred_element_type=F32)
        for i in range(tiles):
            result[i, mine, :] = sums[:, i * LANES : (i + 1) * LANES]
        result[tiles, mine, :] = jnp.where(side < LANES // 2, peak, total)

    few = min(2, per_dev)
    for r in range(requests):
        length = lengths[r]
        past = length <= base
        short = length <= base + few * PAGE

        @pl.when(past)
        def _():
            mine = pl.ds(r, heads, stride=requests)
            for i in range(tiles):
                result[i, mine, :] = jnp.zeros((heads, LANES), F32)
            result[tiles, mine, :] = jnp.where(side < LANES // 2, NEG, 0.0)

        @pl.when(jnp.logical_not(past) & short)
        def _():
            attend(r, few)

        @pl.when(jnp.logical_not(short))
        def _():
            attend(r, per_dev)

    for k in range(blocks):
        block = pl.ds(k * rows, rows)
        marks = result[tiles, block, :]
        peak, total = marks[:, :1], marks[:, LANES // 2 : LANES // 2 + 1]
        some = total > 0.0
        safe = jnp.where(some, total, 1.0)
        level = jnp.where(some, peak + jnp.log(safe), NEG)
        high = level.astype(BF16).astype(F32)
        middle = (level - high).astype(BF16).astype(F32)
        low = level - high - middle
        lane = lax.broadcasted_iota(jnp.int32, marks.shape, 1)
        split = jnp.where(lane == 0, high, jnp.where(lane == 1, middle, low))
        share = 1.0 / safe
        pieces = [result[i, block, :] * share for i in range(tiles)] + [split]
        outs[k][...] = jnp.concatenate(pieces, axis=1).astype(BF16)
    for r in range(requests):
        @pl.when(slot[0] != r)
        def _():
            for copy in own_pages(r):
                copy.wait()


def finish_kernel(blocks, requests, lat_size, *refs):
    parts = refs[:blocks]
    query, new, value_up, w_out, out, sent = refs[blocks:]
    local_heads = value_up.shape[0]
    scale = (NOPE + ROPE) ** (-0.5)
    fresh = jnp.concatenate([new[:, : lat_size + ROPE]] * local_heads, axis=0)
    q_own = query[...].astype(F32)
    new_score = jnp.sum(q_own * fresh, axis=1, keepdims=True) * scale
    peak = new_score
    means = []
    for part in parts:
        wide = part[...].astype(F32)
        marks = wide[:, lat_size:]
        level = marks[:, 0:1] + marks[:, 1:2] + marks[:, 2:3]
        means.append((level, wide[:, :lat_size]))
        peak = jnp.maximum(peak, level)
    new_factor = jnp.exp(new_score - peak)
    denom = new_factor
    numer = new_factor * fresh[:, :lat_size]
    for level, mean in means:
        factor = jnp.exp(level - peak)
        denom += factor
        numer += factor * mean
    o_lat = numer / denom
    vals = []
    for h in range(local_heads):
        one = o_lat[h * requests : (h + 1) * requests, :].astype(BF16)
        vals.append(jnp.dot(one, value_up[h], preferred_element_type=F32).astype(BF16))
    o_val = jnp.concatenate(vals, axis=1)
    value = jnp.dot(o_val, w_out[...], preferred_element_type=F32)
    out[...] = value
    sent[...] = value.astype(BF16)


def norm_kernel(blocks, *refs):
    slot = refs[0]
    parts = refs[1 : 1 + blocks]
    x, gain = refs[1 + blocks : 3 + blocks]
    row_out, h_out = refs[-2:]
    attn = parts[0][...]
    for part in parts[1:]:
        attn += part[...].astype(F32)
    h_one = (x[...].astype(F32) + attn).astype(BF16)
    h_out[...] = h_one
    wide = h_one.astype(F32)
    normed = rms_norm(wide, gain[...])
    mark = jnp.full((wide.shape[0], LANES), slot[0], jnp.int32).astype(F32)
    row_out[...] = jnp.concatenate([normed, mark], axis=1).astype(BF16)


def copy_pages(table, slot, lat, lat_out, sems, first, count):
    copies = [
        pltpu.make_async_copy(
            lat.at[table[slot[0], first + j]], lat_out.at[pl.ds(j * PAGE, PAGE)], sems.at[j]
        )
        for j in range(count)
    ]
    for copy in copies:
        copy.start()
    return copies


def order_kernel(groups, requests, rank, route_ids, router, *refs):
    pieces = refs[:groups]
    x_out, coef_out, _ = refs[groups + 1 :]
    size = router.shape[1]
    wide = jnp.concatenate([p[...].astype(F32) for p in pieces], axis=0)
    rows = wide.shape[0]
    reps = rows // requests
    moved = wide[:, size : size + 1]
    other = jnp.concatenate([moved[rows // 2 :], moved[: rows // 2]], axis=0)
    row = lax.broadcasted_iota(jnp.int32, (rows, 1), 0)
    place = row // requests
    across = ((place + reps // 2) % reps) * requests
    source = jnp.where(
        row % requests == moved.astype(jnp.int32), across + other.astype(jnp.int32), row
    )
    column = lax.broadcasted_iota(jnp.int32, (rows, rows), 1)
    picks = (column == source).astype(F32).astype(BF16)
    x = jnp.dot(picks, wide[:, :size].astype(BF16), preferred_element_type=F32).astype(BF16)
    x_out[...] = x
    gates = jax.nn.sigmoid(lax.dot_general(x, router[...], NT, preferred_element_type=F32))
    home = (place ^ rank[0]) * requests + row % requests
    turns = (column == home).astype(F32).astype(BF16)
    ids = jnp.dot(turns, route_ids[...].astype(F32).astype(BF16), preferred_element_type=F32)
    ids = ids.astype(jnp.int32)
    expert = lax.broadcasted_iota(jnp.int32, gates.shape, 1)
    chosen = jnp.zeros(gates.shape, F32)
    for k in range(ids.shape[1]):
        chosen += jnp.where(expert == ids[:, k : k + 1], gates, 0.0)
    coef_out[...] = chosen / jnp.sum(chosen, axis=1, keepdims=True) * ROUTE_SCALE


def expert_kernel(
    requests, chunk, hidden, rank, x, coef, gate, up, down, kept, sent, gate_v, up_v, down_v, total, sems,
):
    units = gate.shape[0]
    pieces = [slice(b, min(b + chunk, units)) for b in range(0, units, chunk)]

    def fetch(which, source, target, i):
        piece = pl.ds(pieces[i].start, pieces[i].stop - pieces[i].start)
        return pltpu.make_async_copy(source.at[piece], target.at[piece], sems.at[which, i])

    copies = [
        [fetch(w, s, t, i) for w, (s, t) in enumerate([(gate, gate_v), (up, up_v), (down, down_v)])]
        for i in range(len(pieces))
    ]
    for trio in copies:
        for copy in trio:
            copy.start()
    count = units // hidden
    first = rank[0] * count
    weights = coef[...]
    expert = lax.broadcasted_iota(jnp.int32, weights.shape, 1)
    shares = [
        jnp.sum(jnp.where(expert == first + e, weights, 0.0), axis=1, keepdims=True)
        for e in range(count)
    ]
    rows = x.shape[0]
    for i, piece in enumerate(pieces):
        copies[i][0].wait()
        gate_val = lax.dot_general(x[...], gate_v[piece, :], NT, preferred_element_type=F32)
        copies[i][1].wait()
        up_val = lax.dot_general(x[...], up_v[piece, :], NT, preferred_element_type=F32)
        unit = piece.start + lax.broadcasted_iota(jnp.int32, gate_val.shape, 1)
        low, high = piece.start // hidden, (piece.stop - 1) // hidden
        share = jnp.broadcast_to(shares[high], gate_val.shape)
        for e in range(high - 1, low - 1, -1):
            share = jnp.where(unit < (e + 1) * hidden, shares[e], share)
        hid = (silu(gate_val) * up_val * share).astype(BF16)
        copies[i][2].wait()
        term = jnp.dot(hid, down_v[piece, :], preferred_element_type=F32)
        if i == 0:
            total[...] = term
        else:
            total[...] += term
    value = total[...]
    blocks = [value[p * requests : (p + 1) * requests] for p in range(rows // requests)]
    kept[...] = jnp.concatenate(blocks[0::2], axis=0)
    sent[...] = jnp.concatenate(blocks[1::2], axis=0).astype(BF16)


def pair_kernel(requests, kept, got, _, own, *blocks):
    total = kept[...] + got[...].astype(F32)
    own[...] = total[:requests]
    for k, block in enumerate(blocks):
        block[...] = total[(k + 1) * requests : (k + 2) * requests].astype(BF16)


def shared_kernel(
    first, count, table, slot, rows, h_one, new, _, gate, up, down, lat,
    out, next_out, gate_v, up_v, down_v, sems, page_sems,
):
    copies = [
        pltpu.make_async_copy(gate, gate_v, sems.at[0]),
        pltpu.make_async_copy(up, up_v, sems.at[1]),
        pltpu.make_async_copy(down, down_v, sems.at[2]),
    ]
    for copy in copies:
        copy.start()
    pages = copy_pages(table, slot, lat, next_out, page_sems, first, count)
    x = rows[:, : gate.shape[1]]
    copies[0].wait()
    gate_val = lax.dot_general(x, gate_v[...], NT, preferred_element_type=F32)
    copies[1].wait()
    up_val = lax.dot_general(x, up_v[...], NT, preferred_element_type=F32)
    hid = (silu(gate_val) * up_val).astype(BF16)
    copies[2].wait()
    shared = jnp.dot(hid, down_v[...], preferred_element_type=F32)
    out[...] = shared
    every = jnp.concatenate([h_one[...].astype(F32), new[...], shared], axis=1)
    row = lax.broadcasted_iota(jnp.int32, every.shape, 0)
    every = jnp.sum(jnp.where(row == slot[0], every, 0.0), axis=0, keepdims=True)
    lat_size = next_out.shape[1]
    lines = [every[:, b : b + lat_size] for b in range(0, every.shape[1], lat_size)]
    lines[-1] = jnp.pad(lines[-1], ((0, 0), (0, lat_size - lines[-1].shape[1])))
    lines.append(jnp.zeros((ROWS - len(lines), lat_size), F32))
    next_out[count * PAGE :, :] = jnp.concatenate(lines, axis=0).astype(BF16)
    for copy in pages:
        copy.wait()


def total_kernel(slot, got, own, shared, _, *refs):
    others, (total, sent) = refs[:-2], refs[-2:]
    row = lax.broadcasted_iota(jnp.int32, own.shape, 0)
    value = own[...] + jnp.where(row == slot[0], got[...].astype(F32), shared[...])
    for other in others:
        value += other[...].astype(F32)
    total[...] = value
    sent[...] = value.astype(BF16)


def token_spot(r, table, lengths, rank):
    per_dev = table.shape[1]
    local = lengths[r] // PAGE - rank[0] * per_dev
    owned = (local >= 0) & (local < per_dev)
    local = jnp.clip(local, 0, per_dev - 1)
    inside = lengths[r] % PAGE
    return owned, local, table[r, local], inside, pl.multiple_of(inside // 16 * 16, 16)


def cache_kernel(
    first, table, slot, _, got_lat, got_rope, lat_in, rope_in,
    lat_out, rope_out, token, lat_v, rope_v, got_sems, sems,
):
    del lat_in, rope_in
    per_dev = table.shape[1]
    moved = slot[0]
    token[...] = jnp.zeros_like(token)
    fetches = [
        pltpu.make_async_copy(got_rope, rope_v, got_sems.at[0]),
        pltpu.make_async_copy(got_lat, lat_v, got_sems.at[1]),
    ]
    for copy in fetches:
        copy.start()
    for copy in fetches:
        copy.wait()
    copies = []
    for j in range(per_dev):
        page = table[moved, j]
        if j < first:
            copies.append(pltpu.make_async_copy(lat_v.at[j], lat_out.at[page], sems.at[0, j]))
        copies.append(pltpu.make_async_copy(rope_v.at[j], rope_out.at[page], sems.at[1, j]))
    for copy in copies:
        copy.start()
    for copy in copies:
        copy.wait()


def token_kernel(
    first, last, table, slot, lengths, rank, new_lat, new_rope, got, _, lat_in, rope_in,
    lat_out, rope_out, got_v, lat_tile, rope_tile, got_sem, sems, tile_sems,
):
    requests, _ = table.shape
    moved = slot[0]
    fetch = pltpu.make_async_copy(got.at[pl.ds(0, got_v.shape[0])], got_v, got_sem.at[0])
    fetch.start()
    spots = [token_spot(r, table, lengths, rank) for r in range(requests)]

    def received(r):
        local = spots[r][1]
        return (moved == r) & (local >= first) & (local < last)

    def lat_read(r):
        _, _, page, _, group = spots[r]
        return pltpu.make_async_copy(lat_in.at[page, pl.ds(group, 16), :], lat_tile.at[r], tile_sems.at[0, r])

    def rope_read(r):
        return pltpu.make_async_copy(rope_in.at[spots[r][2]], rope_tile.at[r], tile_sems.at[1, r])

    def lat_write(r):
        _, _, page, _, group = spots[r]
        return pltpu.make_async_copy(lat_tile.at[r], lat_out.at[page, pl.ds(group, 16), :], tile_sems.at[0, r])

    def rope_write(r):
        return pltpu.make_async_copy(rope_tile.at[r], rope_out.at[spots[r][2]], tile_sems.at[1, r])

    def in_pool(r):
        owned, local = spots[r][:2]
        return owned & ((moved != r) | (local < first))

    for r in range(requests):
        @pl.when(spots[r][0])
        def _():
            rope_read(r).start()

        @pl.when(in_pool(r))
        def _():
            lat_read(r).start()

    fetch.wait()
    for r in range(requests):
        owned, local, _, inside, group = spots[r]

        @pl.when(owned & received(r))
        def _():
            index = jnp.clip(local - first, 0, last - first - 1)
            piece = pl.ds(pl.multiple_of(index * PAGE + group, 16), 16)
            tile = got_v[piece, :].astype(F32)
            row = lax.broadcasted_iota(jnp.int32, tile.shape, 0)
            got_v[piece, :] = jnp.where(
                row == inside - group, new_lat[r : r + 1, :], tile
            ).astype(BF16)

    pages = [
        pltpu.make_async_copy(
            got_v.at[pl.ds(j * PAGE, PAGE)], lat_out.at[table[moved, first + j]], sems.at[j]
        )
        for j in range(last - first)
    ]
    for copy in pages:
        copy.start()
    for r in range(requests):
        owned, local, _, inside, group = spots[r]

        @pl.when(owned)
        def _():
            rope_read(r).wait()
            lane = lax.broadcasted_iota(jnp.int32, rope_tile.shape[1:], 1)
            rope_tile[r] = jnp.where(
                lane == inside, new_rope[:, r : r + 1], rope_tile[r].astype(F32)
            ).astype(BF16)
            rope_write(r).start()

        @pl.when(in_pool(r))
        def _():
            lat_read(r).wait()
            row = lax.broadcasted_iota(jnp.int32, lat_tile.shape[1:], 0)
            lat_tile[r] = jnp.where(
                row == inside - group, new_lat[r : r + 1, :], lat_tile[r].astype(F32)
            ).astype(BF16)
            lat_write(r).start()

    for r in range(requests):
        @pl.when(spots[r][0])
        def _():
            rope_write(r).wait()

        @pl.when(in_pool(r))
        def _():
            lat_write(r).wait()
    for copy in pages:
        copy.wait()


def body(
    hidden,
    lengths,
    page_table,
    move_slot,
    lat_pool,
    rope_pool,
    norm_attn,
    w_query,
    w_latent,
    latent_gain,
    w_key_up,
    w_value_up,
    w_output,
    norm_ffn,
    w_router,
    route_ids,
    expert_gate,
    expert_up,
    expert_down,
    shared_gate,
    shared_up,
    shared_down,
):
    requests, size = hidden.shape
    per_dev = page_table.shape[1]
    local_heads, nope_size, lat_size = w_key_up.shape
    local_experts, _, units = expert_gate.shape
    n_tp, n_rep = lax.axis_size("tp"), lax.axis_size("rep")
    groups = n_rep // 2
    half = n_rep // 2
    rows = local_heads * requests
    everyone = n_rep * requests
    pages = requests * per_dev
    width = lat_size + LANES
    tp_one = lax.axis_index("tp").astype(jnp.int32)[None]
    rep_one = lax.axis_index("rep").astype(jnp.int32)[None]
    page_bytes = PAGE * (lat_size + ROPE) * 2
    dma = pltpu.SemaphoreType.DMA
    first_span = per_dev * 6 // 10
    second_span = per_dev - first_span
    lat_page = lat_pool.shape[1:]
    rope_page = rope_pool.shape[1:]
    lat_hbm, rope_hbm = in_hbm(lat_pool), in_hbm(rope_pool)
    gate_t = jnp.swapaxes(expert_gate, 1, 2).reshape(-1, size)
    up_t = jnp.swapaxes(expert_up, 1, 2).reshape(-1, size)

    q_own, normed, out_first, out_rope = call(
        functools.partial(query_kernel, first_span),
        (
            struct((rows, lat_size + ROPE), BF16),
            struct((requests, size), BF16),
            struct((first_span,) + lat_page, BF16),
            struct((per_dev,) + rope_page, BF16),
        ),
        [ANY] * 8,
        (VMEM,) * 4,
        [
            pltpu.SMEM(page_table.shape, jnp.int32),
            pltpu.SMEM((1,), jnp.int32),
            pltpu.VMEM(hidden.shape, BF16),
            pltpu.VMEM((1, size), F32),
            pltpu.VMEM(w_query.shape, BF16),
            pltpu.VMEM(w_key_up.shape, BF16),
            dma((2, per_dev)),
            dma((9,)),
        ],
        vmem=8,
        flops=2 * requests * w_query.size,
        nbytes=2 * w_query.size,
    )(
        page_table, move_slot, in_hbm(hidden), in_hbm(norm_attn[None, :]),
        in_hbm(w_query), in_hbm(w_key_up), lat_hbm, rope_hbm,
    )
    got_first = xored(out_first, "rep", half)
    got_rope = xored(out_rope, "rep", half)
    q_blocks = [q_own] + [xored(q_own, "tp", k) for k in range(1, n_tp)]

    lat_v, rope_v, _ = call(
        fetch_kernel,
        (
            pltpu.VMEM((pages,) + lat_page, BF16),
            pltpu.VMEM((pages,) + rope_page, BF16),
            struct((8, LANES), F32),
        ),
        [SMEM, VMEM, ANY, ANY],
        (VMEM,) * 3,
        [dma((2, pages))],
        vmem=6,
        flops=2 * requests * w_latent.size,
        nbytes=pages * page_bytes + 2 * (w_latent.size + w_output.size + w_value_up.size),
    )(page_table, q_own, lat_hbm, rope_hbm)

    *partial, lat_most, rope_most = call(
        functools.partial(attention_kernel, n_tp, per_dev, requests, lat_size),
        tuple(struct((rows, width), BF16) for _ in range(n_tp))
        + (struct(lat_pool.shape, BF16), struct(rope_pool.shape, BF16)),
        [SMEM] * 4 + [VMEM] * (n_tp + 2),
        (VMEM,) * n_tp + (ANY, ANY),
        [pltpu.VMEM((width // LANES, n_tp * rows, LANES), F32)] * 2 + [dma((2, pages))],
        vmem=6,
        flops=4 * n_tp * rows * per_dev * PAGE * lat_size,
        nbytes=pages * page_bytes,
    )(page_table, move_slot, lengths, tp_one, *q_blocks, lat_v, rope_v)
    parts = [partial[0]] + [xored(partial[k], "tp", k) for k in range(1, n_tp)]
    value_v, out_v, new = call(
        token_weights_kernel,
        (
            pltpu.VMEM(w_value_up.shape, BF16),
            pltpu.VMEM(w_output.shape, BF16),
            struct((requests, width), F32),
        ),
        [SMEM] + [VMEM] * 3 + [ANY] * 3,
        (VMEM,) * 3,
        [pltpu.VMEM((w_latent.shape[1], size), BF16), dma((3,))],
        vmem=6,
        flops=2 * requests * w_latent.size,
        nbytes=2 * (w_latent.size + w_output.size + w_value_up.size),
    )(
        lengths, normed, latent_gain[None, :], partial[0], in_hbm(w_latent.T),
        in_hbm(w_value_up), in_hbm(w_output),
    )

    out_part, out_sent = call(
        functools.partial(finish_kernel, n_tp, requests, lat_size),
        (struct((requests, size), F32), struct((requests, size), BF16)),
        [VMEM] * (n_tp + 4),
        (VMEM, VMEM),
        vmem=4,
        flops=2 * requests * size * w_output.shape[0],
        nbytes=2 * w_output.size + 2 * w_value_up.size,
    )(*parts, q_own, new, value_v, out_v)
    out_parts = [out_part] + [xored(out_sent, "tp", k) for k in range(1, n_tp)]

    ffn_row, h_one = call(
        functools.partial(norm_kernel, n_tp),
        (
            struct((requests, size + LANES), BF16),
            struct((requests, size), BF16),
        ),
        [SMEM] + [VMEM] * (n_tp + 2) + [ANY] * 2,
        (VMEM,) * 2,
        vmem=4,
        nbytes=8 * n_tp * requests * size,
    )(move_slot, *out_parts, hidden, norm_ffn[None, :], got_first, got_rope)

    pair = jnp.concatenate([ffn_row, xored(ffn_row, "rep", 1)], axis=0)
    pieces = [pair] + [xored(pair, "rep", 2 * k) for k in range(1, groups)]

    shared_part, out_second = call(
        functools.partial(shared_kernel, first_span, second_span),
        (
            struct((requests, size), F32),
            struct((second_span * PAGE + ROWS, lat_size), BF16),
        ),
        [SMEM, SMEM] + [VMEM] * 4 + [ANY] * 4,
        (VMEM, VMEM),
        [
            pltpu.VMEM((shared_gate.shape[1], size), BF16),
            pltpu.VMEM((shared_gate.shape[1], size), BF16),
            pltpu.VMEM(shared_down.shape, BF16),
            dma((3,)),
            dma((second_span,)),
        ],
        vmem=12,
        flops=6 * requests * shared_gate.size,
        nbytes=6 * shared_gate.size,
    )(
        page_table, move_slot, ffn_row, h_one, new, pair, in_hbm(shared_gate.T),
        in_hbm(shared_up.T), in_hbm(shared_down), lat_hbm,
    )
    x_all, coef, out_second = call(
        functools.partial(order_kernel, groups, requests),
        (
            struct((everyone, size), BF16),
            struct((everyone, w_router.shape[1]), F32),
            struct(out_second.shape, BF16),
        ),
        [SMEM] + [VMEM] * (groups + 3),
        (VMEM,) * 3,
        vmem=6,
        flops=4 * everyone * size * everyone,
        nbytes=4 * everyone * size,
        aliases={3 + groups: 2},
    )(rep_one, route_ids, w_router.T, *pieces, out_second)
    got_second = xored(out_second, "rep", half)
    got_row = got_second[second_span * PAGE :].reshape(1, -1)[:, : size + width + size]

    kept, sent = call(
        functools.partial(expert_kernel, requests, 512, units),
        (
            struct((groups * requests, size), F32),
            struct((groups * requests, size), BF16),
        ),
        [SMEM] + [VMEM] * 2 + [ANY] * 3,
        (VMEM, VMEM),
        [pltpu.VMEM((local_experts * units, size), BF16)] * 3
        + [pltpu.VMEM((everyone, size), F32), dma((3, pl.cdiv(local_experts * units, 512)))],
        vmem=42,
        flops=6 * everyone * expert_gate.size,
        nbytes=6 * expert_gate.size,
    )(
        rep_one, x_all, coef, in_hbm(gate_t), in_hbm(up_t), in_hbm(expert_down.reshape(-1, size)),
    )
    summed = call(
        functools.partial(pair_kernel, requests),
        (struct((requests, size), F32),) + (struct((requests, size), BF16),) * (groups - 1),
        [VMEM, VMEM, ANY],
        (VMEM,) * groups,
        vmem=4,
        nbytes=8 * everyone * size,
    )(kept, xored(sent, "rep", 1), got_second)
    others = [xored(summed[k], "rep", 2 * k) for k in range(1, groups)]
    lat_most, rope_most, cache_token = call(
        functools.partial(cache_kernel, first_span),
        (struct(lat_pool.shape, BF16), struct(rope_pool.shape, BF16), struct((8, LANES), F32)),
        [SMEM] * 2 + [VMEM] + [ANY] * 4,
        (ANY, ANY, VMEM),
        [
            pltpu.VMEM((first_span,) + lat_page, BF16),
            pltpu.VMEM((per_dev,) + rope_page, BF16),
            dma((2,)),
            dma((2, per_dev)),
        ],
        vmem=4,
        nbytes=2 * first_span * page_bytes,
        aliases={5: 0, 6: 1},
    )(page_table, move_slot, summed[0], got_first, got_rope, lat_most, rope_most)
    total, total_sent = call(
        total_kernel,
        (struct((requests, size), F32), struct((requests, size), BF16)),
        [SMEM] + [VMEM] * (groups + 3),
        (VMEM, VMEM),
        vmem=4,
        nbytes=8 * everyone * size,
    )(move_slot, got_row[:, size + width :], summed[0], shared_part, cache_token, *others)

    is_moved = (jnp.arange(requests, dtype=jnp.int32) == move_slot[0])[:, None]
    new_served = jnp.where(is_moved, got_row[:, size : size + width].astype(F32), new)
    marks = new_served[:, lat_size + ROPE : lat_size + ROPE + 2].astype(jnp.int32)
    len_served = marks[:, 0] * PAGE + marks[:, 1]
    lat_new = new_served[:, :lat_size]
    rope_new = new_served[:, lat_size : lat_size + ROPE].T
    lat_cache, rope_cache = call(
        functools.partial(token_kernel, first_span, per_dev),
        (struct(lat_pool.shape, BF16), struct(rope_pool.shape, BF16)),
        [SMEM] * 4 + [VMEM] * 2 + [ANY, VMEM] + [ANY] * 2,
        (ANY, ANY),
        [
            pltpu.VMEM((second_span * PAGE, lat_size), BF16),
            pltpu.VMEM((requests, 16, lat_size), BF16),
            pltpu.VMEM((requests,) + rope_page, BF16),
            dma((1,)),
            dma((second_span,)),
            dma((2, requests)),
        ],
        vmem=2,
        nbytes=2 * second_span * page_bytes,
        aliases={8: 0, 9: 1},
    )(
        page_table, move_slot, len_served, tp_one, lat_new, rope_new, got_second, total,
        lat_most, rope_most,
    )

    total_all = total
    for other in [xored(total_sent, "tp", k) for k in range(1, n_tp)]:
        total_all = total_all + other.astype(F32)
    h_served = jnp.where(is_moved, got_row[:, :size], h_one)
    mixed = (h_served.astype(F32) + total_all).astype(BF16)
    return (mixed, lat_cache, rope_cache)


def solution(mesh):
    in_specs = (
        P("rep", None),
        P("rep"),
        P("rep", "tp"),
        P("rep"),
        P(("rep", "tp"), None, None),
        P(("rep", "tp"), None, None),
        P(),
        P(None, "tp"),
        P(),
        P(),
        P("tp", None, None),
        P("tp", None, None),
        P("tp", None),
        P(),
        P(),
        P(),
        P("rep", None, "tp"),
        P("rep", None, "tp"),
        P("rep", "tp", None),
        P(None, "tp"),
        P(None, "tp"),
        P("tp", None),
    )
    out_specs = (P("rep", None), P(("rep", "tp"), None, None), P(("rep", "tp"), None, None))
    return jax.shard_map(body, mesh=mesh, in_specs=in_specs, out_specs=out_specs, check_vma=False)
```

```python
import functools

import jax
import jax.numpy as jnp
from jax import lax
from jax.experimental import pallas as pl
from jax.experimental.pallas import tpu as pltpu
from jax.sharding import PartitionSpec as P

NOPE = 128
ROPE = 64
SINKS = 4
WIN = 4096
PAGE = 128
LANES = 128
ROWS = 16
EPS = 1e-06
ROUTE_SCALE = 2.446
NEG = -1e30
F32 = jnp.float32
BF16 = jnp.bfloat16
NT = (((1,), (1,)), ((), ()))

VMEM = pl.BlockSpec(memory_space=pltpu.VMEM)
SMEM = pl.BlockSpec(memory_space=pltpu.SMEM)
ANY = pl.BlockSpec(memory_space=pl.ANY)


def xored(value, axis, mask):
    pairs = [(source, source ^ mask) for source in range(lax.axis_size(axis))]
    return lax.ppermute(value, axis, pairs)


def call(kernel, out_shape, in_specs, out_specs, scratch=(), vmem=8, flops=0, nbytes=0, aliases=None):
    return pl.pallas_call(
        kernel,
        out_shape=out_shape,
        in_specs=in_specs,
        out_specs=out_specs,
        scratch_shapes=list(scratch),
        input_output_aliases=aliases or {},
        compiler_params=pltpu.CompilerParams(vmem_limit_bytes=vmem * 1024 * 1024),
        cost_estimate=pl.CostEstimate(flops=flops, bytes_accessed=nbytes, transcendentals=0),
    )


def struct(shape, dtype):
    return jax.ShapeDtypeStruct(shape, dtype)


def in_hbm(value):
    return pltpu.with_memory_space_constraint(value, pltpu.HBM)


def rms_norm(values, gain):
    return values * lax.rsqrt(jnp.mean(values * values, axis=-1, keepdims=True) + EPS) * gain


def silu(value):
    return value / (1.0 + jnp.exp(-value))


def query_kernel(
    first, table_in, slot_in, x_in, gain_in, w_in, key_in, lat, rope,
    q_out, normed_out, lat_out, rope_out,
    table, slot, x, gain, w_query, key_up, sems, in_sems,
):
    per_dev = table.shape[1]
    size = x.shape[1]
    parts = in_sems.shape[0] - 5
    step = size // parts
    small = [
        pltpu.make_async_copy(source, target, in_sems.at[i])
        for i, (source, target) in enumerate(
            [(table_in, table), (slot_in, slot), (x_in, x), (gain_in, gain)]
        )
    ]
    for copy in small:
        copy.start()
    big = []
    for i in range(parts):
        piece = pl.ds(i * step, step)
        big.append(pltpu.make_async_copy(w_in.at[piece], w_query.at[piece], in_sems.at[4 + i]))
    big.append(pltpu.make_async_copy(key_in, key_up, in_sems.at[4 + parts]))
    for copy in big:
        copy.start()
    small[0].wait()
    small[1].wait()
    copies = []
    for j in range(per_dev):
        page = table[slot[0], j]
        if j < first:
            copies.append(pltpu.make_async_copy(lat.at[page], lat_out.at[j], sems.at[0, j]))
        copies.append(pltpu.make_async_copy(rope.at[page], rope_out.at[j], sems.at[1, j]))
    for copy in copies:
        copy.start()
    small[2].wait()
    small[3].wait()
    normed = rms_norm(x[...].astype(F32), gain[...]).astype(BF16)
    normed_out[...] = normed
    heads, nope, _ = key_up.shape
    query = None
    for i in range(parts):
        big[i].wait()
        piece = slice(i * step, (i + 1) * step)
        term = jnp.dot(normed[:, piece], w_query[piece, :], preferred_element_type=F32)
        query = term if query is None else query + term
    big[parts].wait()
    wide = query.shape[1] // heads
    rows = []
    for h in range(heads):
        one = query[:, h * wide : (h + 1) * wide]
        q_lat = jnp.dot(one[:, :nope].astype(BF16), key_up[h], preferred_element_type=F32)
        rows.append(jnp.concatenate([q_lat, one[:, nope:]], axis=1))
    q_out[...] = jnp.concatenate(rows, axis=0).astype(BF16)
    for copy in copies:
        copy.wait()


def fetch_kernel(parts, _, lat, rope, lat_v, rope_v, token, sems):
    token[...] = jnp.zeros_like(token)
    step = lat.shape[0] // parts
    copies = []
    for i in range(parts):
        piece = pl.ds(i * step, step)
        copies.append(pltpu.make_async_copy(lat.at[piece], lat_v.at[piece], sems.at[i]))
    copies.append(pltpu.make_async_copy(rope, rope_v, sems.at[parts]))
    for copy in copies:
        copy.start()
    for copy in copies:
        copy.wait()


def token_weights_kernel(
    lengths, normed, gain, _, w_latent, value_up, w_out, value_v, out_v, new_out, latent_v, sems,
):
    copies = [
        pltpu.make_async_copy(w_latent, latent_v, sems.at[0]),
        pltpu.make_async_copy(value_up, value_v, sems.at[1]),
        pltpu.make_async_copy(w_out, out_v, sems.at[2]),
    ]
    for copy in copies:
        copy.start()
    size = gain.shape[1]
    copies[0].wait()
    latent = lax.dot_general(normed[...], latent_v[...], NT, preferred_element_type=F32)
    c_new = rms_norm(latent[:, :size], gain[...]).astype(BF16).astype(F32)
    p_new = latent[:, size:].astype(BF16).astype(F32)
    lane = lax.broadcasted_iota(jnp.int32, (1, LANES), 1)
    marks = []
    for r in range(normed.shape[0]):
        page = jnp.full((1, LANES), lengths[r] // PAGE, jnp.int32)
        inside = jnp.full((1, LANES), lengths[r] % PAGE, jnp.int32)
        marks.append(jnp.where(lane == 0, page, jnp.where(lane == 1, inside, 0)))
    mark = jnp.concatenate(marks, axis=0).astype(F32)
    new_out[...] = jnp.concatenate([c_new, p_new, mark[:, : LANES - ROPE]], axis=1)
    copies[1].wait()
    copies[2].wait()


def attention_kernel(blocks, per_dev, requests, lat_size, *refs):
    table, lengths, rank = refs[:3]
    queries = refs[3 : 3 + blocks]
    lat, rope = refs[3 + blocks : 5 + blocks]
    outs = refs[5 + blocks : 5 + 2 * blocks]
    lat_out, rope_out, q_all, result, sems = refs[5 + 2 * blocks :]
    copies = []
    for r in range(requests):
        piece = pl.ds(r * per_dev, per_dev)
        copies.append(pltpu.make_async_copy(lat.at[piece], lat_out.at[piece], sems.at[r]))
    copies.append(pltpu.make_async_copy(rope, rope_out, sems.at[requests]))
    for copy in copies:
        copy.start()
    rows = queries[0].shape[0]
    heads = blocks * rows // requests
    scale = (NOPE + ROPE) ** (-0.5)
    tiles = lat_size // LANES
    for k in range(blocks):
        block = queries[k][...].astype(F32)
        for i in range(tiles + 1):
            piece = block[:, i * LANES : (i + 1) * LANES]
            q_all[i, k * rows : (k + 1) * rows, : piece.shape[1]] = piece
    base = rank[0] * (per_dev * PAGE)
    side = lax.broadcasted_iota(jnp.int32, (heads, LANES), 1)

    def attend(r, count):
        mine = pl.ds(r, heads, stride=requests)
        length = lengths[r]
        q_lat = jnp.concatenate([q_all[i, mine, :] for i in range(tiles)], axis=1).astype(BF16)
        q_pos = q_all[tiles, mine, :][:, :ROPE].astype(BF16)
        latents = jnp.concatenate([lat[table[r, j]] for j in range(count)], axis=0)
        scores = lax.dot_general(q_lat, latents, NT, preferred_element_type=F32)
        scores += jnp.concatenate(
            [
                jnp.dot(q_pos, rope[table[r, j]], preferred_element_type=F32)
                for j in range(count)
            ],
            axis=1,
        )
        scores *= scale
        position = base + lax.broadcasted_iota(jnp.int32, scores.shape, 1)
        allowed = (position < length) & ((position < SINKS) | (position >= length + 1 - WIN))
        peak = jnp.max(jnp.where(allowed, scores, NEG), axis=1, keepdims=True)
        weights = jnp.where(allowed, jnp.exp(scores - peak), 0.0).astype(BF16)
        total = jnp.sum(weights.astype(F32), axis=1, keepdims=True)
        sums = jnp.dot(weights, latents, preferred_element_type=F32)
        for i in range(tiles):
            result[i, mine, :] = sums[:, i * LANES : (i + 1) * LANES]
        result[tiles, mine, :] = jnp.where(side < LANES // 2, peak, total)

    few = min(2, per_dev)
    for r in range(requests):
        length = lengths[r]
        past = length <= base
        short = length <= base + few * PAGE

        @pl.when(past)
        def _():
            mine = pl.ds(r, heads, stride=requests)
            for i in range(tiles):
                result[i, mine, :] = jnp.zeros((heads, LANES), F32)
            result[tiles, mine, :] = jnp.where(side < LANES // 2, NEG, 0.0)

        @pl.when(jnp.logical_not(past) & short)
        def _():
            attend(r, few)

        @pl.when(jnp.logical_not(short))
        def _():
            attend(r, per_dev)

    for k in range(blocks):
        block = pl.ds(k * rows, rows)
        marks = result[tiles, block, :]
        peak, total = marks[:, :1], marks[:, LANES // 2 : LANES // 2 + 1]
        some = total > 0.0
        safe = jnp.where(some, total, 1.0)
        level = jnp.where(some, peak + jnp.log(safe), NEG)
        high = level.astype(BF16).astype(F32)
        middle = (level - high).astype(BF16).astype(F32)
        low = level - high - middle
        lane = lax.broadcasted_iota(jnp.int32, marks.shape, 1)
        split = jnp.where(lane == 0, high, jnp.where(lane == 1, middle, low))
        share = 1.0 / safe
        pieces = [result[i, block, :] * share for i in range(tiles)] + [split]
        outs[k][...] = jnp.concatenate(pieces, axis=1).astype(BF16)
    for copy in copies:
        copy.wait()


def finish_kernel(blocks, requests, lat_size, *refs):
    parts = refs[:blocks]
    query, new, value_up, w_out, out, sent = refs[blocks:]
    local_heads = value_up.shape[0]
    scale = (NOPE + ROPE) ** (-0.5)
    fresh = jnp.concatenate([new[:, : lat_size + ROPE]] * local_heads, axis=0)
    q_own = query[...].astype(F32)
    new_score = jnp.sum(q_own * fresh, axis=1, keepdims=True) * scale
    peak = new_score
    means = []
    for part in parts:
        wide = part[...].astype(F32)
        marks = wide[:, lat_size:]
        level = marks[:, 0:1] + marks[:, 1:2] + marks[:, 2:3]
        means.append((level, wide[:, :lat_size]))
        peak = jnp.maximum(peak, level)
    new_factor = jnp.exp(new_score - peak)
    denom = new_factor
    numer = new_factor * fresh[:, :lat_size]
    for level, mean in means:
        factor = jnp.exp(level - peak)
        denom += factor
        numer += factor * mean
    o_lat = numer / denom
    vals = []
    for h in range(local_heads):
        one = o_lat[h * requests : (h + 1) * requests, :].astype(BF16)
        vals.append(jnp.dot(one, value_up[h], preferred_element_type=F32).astype(BF16))
    o_val = jnp.concatenate(vals, axis=1)
    value = jnp.dot(o_val, w_out[...], preferred_element_type=F32)
    out[...] = value
    sent[...] = value.astype(BF16)


def norm_kernel(blocks, *refs):
    slot = refs[0]
    parts = refs[1 : 1 + blocks]
    x, gain = refs[1 + blocks : 3 + blocks]
    row_out, h_out = refs[-2:]
    attn = parts[0][...]
    for part in parts[1:]:
        attn += part[...].astype(F32)
    h_one = (x[...].astype(F32) + attn).astype(BF16)
    h_out[...] = h_one
    wide = h_one.astype(F32)
    normed = rms_norm(wide, gain[...])
    mark = jnp.full((wide.shape[0], LANES), slot[0], jnp.int32).astype(F32)
    row_out[...] = jnp.concatenate([normed, mark], axis=1).astype(BF16)


def copy_pages(table, slot, lat, lat_out, sems, first, count):
    copies = [
        pltpu.make_async_copy(
            lat.at[table[slot[0], first + j]], lat_out.at[pl.ds(j * PAGE, PAGE)], sems.at[j]
        )
        for j in range(count)
    ]
    for copy in copies:
        copy.start()
    return copies


def order_kernel(groups, requests, rank, route_ids, router, *refs):
    pieces = refs[:groups]
    x_out, coef_out, _ = refs[groups + 1 :]
    size = router.shape[1]
    wide = jnp.concatenate([p[...].astype(F32) for p in pieces], axis=0)
    rows = wide.shape[0]
    reps = rows // requests
    moved = wide[:, size : size + 1]
    other = jnp.concatenate([moved[rows // 2 :], moved[: rows // 2]], axis=0)
    row = lax.broadcasted_iota(jnp.int32, (rows, 1), 0)
    place = row // requests
    across = ((place + reps // 2) % reps) * requests
    source = jnp.where(
        row % requests == moved.astype(jnp.int32), across + other.astype(jnp.int32), row
    )
    column = lax.broadcasted_iota(jnp.int32, (rows, rows), 1)
    picks = (column == source).astype(F32).astype(BF16)
    x = jnp.dot(picks, wide[:, :size].astype(BF16), preferred_element_type=F32).astype(BF16)
    x_out[...] = x
    gates = jax.nn.sigmoid(lax.dot_general(x, router[...], NT, preferred_element_type=F32))
    home = (place ^ rank[0]) * requests + row % requests
    turns = (column == home).astype(F32).astype(BF16)
    ids = jnp.dot(turns, route_ids[...].astype(F32).astype(BF16), preferred_element_type=F32)
    ids = ids.astype(jnp.int32)
    expert = lax.broadcasted_iota(jnp.int32, gates.shape, 1)
    chosen = jnp.zeros(gates.shape, F32)
    for k in range(ids.shape[1]):
        chosen += jnp.where(expert == ids[:, k : k + 1], gates, 0.0)
    coef_out[...] = chosen / jnp.sum(chosen, axis=1, keepdims=True) * ROUTE_SCALE


def expert_kernel(
    requests, chunk, hidden, rank, x, coef, gate, up, down, kept, sent, gate_v, up_v, down_v, total, sems,
):
    units = gate.shape[0]
    pieces = [slice(b, min(b + chunk, units)) for b in range(0, units, chunk)]

    def fetch(which, source, target, i):
        piece = pl.ds(pieces[i].start, pieces[i].stop - pieces[i].start)
        return pltpu.make_async_copy(source.at[piece], target.at[piece], sems.at[which, i])

    copies = [
        [fetch(w, s, t, i) for w, (s, t) in enumerate([(gate, gate_v), (up, up_v), (down, down_v)])]
        for i in range(len(pieces))
    ]
    for trio in copies:
        for copy in trio:
            copy.start()
    count = units // hidden
    first = rank[0] * count
    weights = coef[...]
    expert = lax.broadcasted_iota(jnp.int32, weights.shape, 1)
    shares = [
        jnp.sum(jnp.where(expert == first + e, weights, 0.0), axis=1, keepdims=True)
        for e in range(count)
    ]
    rows = x.shape[0]
    for i, piece in enumerate(pieces):
        copies[i][0].wait()
        gate_val = lax.dot_general(x[...], gate_v[piece, :], NT, preferred_element_type=F32)
        copies[i][1].wait()
        up_val = lax.dot_general(x[...], up_v[piece, :], NT, preferred_element_type=F32)
        unit = piece.start + lax.broadcasted_iota(jnp.int32, gate_val.shape, 1)
        low, high = piece.start // hidden, (piece.stop - 1) // hidden
        share = jnp.broadcast_to(shares[high], gate_val.shape)
        for e in range(high - 1, low - 1, -1):
            share = jnp.where(unit < (e + 1) * hidden, shares[e], share)
        hid = (silu(gate_val) * up_val * share).astype(BF16)
        copies[i][2].wait()
        term = jnp.dot(hid, down_v[piece, :], preferred_element_type=F32)
        if i == 0:
            total[...] = term
        else:
            total[...] += term
    value = total[...]
    blocks = [value[p * requests : (p + 1) * requests] for p in range(rows // requests)]
    kept[...] = jnp.concatenate(blocks[0::2], axis=0)
    sent[...] = jnp.concatenate(blocks[1::2], axis=0).astype(BF16)


def pair_kernel(requests, kept, got, _, own, *blocks):
    total = kept[...] + got[...].astype(F32)
    own[...] = total[:requests]
    for k, block in enumerate(blocks):
        block[...] = total[(k + 1) * requests : (k + 2) * requests].astype(BF16)


def shared_kernel(
    first, count, table, slot, rows, h_one, new, _, gate, up, down, lat,
    out, next_out, gate_v, up_v, down_v, sems, page_sems,
):
    copies = [
        pltpu.make_async_copy(gate, gate_v, sems.at[0]),
        pltpu.make_async_copy(up, up_v, sems.at[1]),
        pltpu.make_async_copy(down, down_v, sems.at[2]),
    ]
    for copy in copies:
        copy.start()
    pages = copy_pages(table, slot, lat, next_out, page_sems, first, count)
    x = rows[:, : gate.shape[1]]
    copies[0].wait()
    gate_val = lax.dot_general(x, gate_v[...], NT, preferred_element_type=F32)
    copies[1].wait()
    up_val = lax.dot_general(x, up_v[...], NT, preferred_element_type=F32)
    hid = (silu(gate_val) * up_val).astype(BF16)
    copies[2].wait()
    shared = jnp.dot(hid, down_v[...], preferred_element_type=F32)
    out[...] = shared
    every = jnp.concatenate([h_one[...].astype(F32), new[...], shared], axis=1)
    row = lax.broadcasted_iota(jnp.int32, every.shape, 0)
    every = jnp.sum(jnp.where(row == slot[0], every, 0.0), axis=0, keepdims=True)
    lat_size = next_out.shape[1]
    lines = [every[:, b : b + lat_size] for b in range(0, every.shape[1], lat_size)]
    lines[-1] = jnp.pad(lines[-1], ((0, 0), (0, lat_size - lines[-1].shape[1])))
    lines.append(jnp.zeros((ROWS - len(lines), lat_size), F32))
    next_out[count * PAGE :, :] = jnp.concatenate(lines, axis=0).astype(BF16)
    for copy in pages:
        copy.wait()


def total_kernel(slot, got, own, shared, _, *refs):
    others, (total, sent) = refs[:-2], refs[-2:]
    row = lax.broadcasted_iota(jnp.int32, own.shape, 0)
    value = own[...] + jnp.where(row == slot[0], got[...].astype(F32), shared[...])
    for other in others:
        value += other[...].astype(F32)
    total[...] = value
    sent[...] = value.astype(BF16)


def token_spot(r, table, lengths, rank):
    per_dev = table.shape[1]
    local = lengths[r] // PAGE - rank[0] * per_dev
    owned = (local >= 0) & (local < per_dev)
    local = jnp.clip(local, 0, per_dev - 1)
    inside = lengths[r] % PAGE
    return owned, local, table[r, local], inside, pl.multiple_of(inside // 16 * 16, 16)


def cache_kernel(
    first, table, slot, _, got_lat, got_rope, lat_in, rope_in,
    lat_out, rope_out, token, lat_v, rope_v, got_sems, sems,
):
    del lat_in, rope_in
    per_dev = table.shape[1]
    moved = slot[0]
    token[...] = jnp.zeros_like(token)
    fetches = [
        pltpu.make_async_copy(got_rope, rope_v, got_sems.at[0]),
        pltpu.make_async_copy(got_lat, lat_v, got_sems.at[1]),
    ]
    for copy in fetches:
        copy.start()
    for copy in fetches:
        copy.wait()
    copies = []
    for j in range(per_dev):
        page = table[moved, j]
        if j < first:
            copies.append(pltpu.make_async_copy(lat_v.at[j], lat_out.at[page], sems.at[0, j]))
        copies.append(pltpu.make_async_copy(rope_v.at[j], rope_out.at[page], sems.at[1, j]))
    for copy in copies:
        copy.start()
    for copy in copies:
        copy.wait()


def token_kernel(
    first, last, table, slot, lengths, rank, new_lat, new_rope, got, _, lat_in, rope_in,
    lat_out, rope_out, got_v, lat_tile, rope_tile, got_sem, sems, tile_sems,
):
    requests, _ = table.shape
    moved = slot[0]
    fetch = pltpu.make_async_copy(got.at[pl.ds(0, got_v.shape[0])], got_v, got_sem.at[0])
    fetch.start()
    spots = [token_spot(r, table, lengths, rank) for r in range(requests)]

    def received(r):
        local = spots[r][1]
        return (moved == r) & (local >= first) & (local < last)

    def lat_read(r):
        _, _, page, _, group = spots[r]
        return pltpu.make_async_copy(lat_in.at[page, pl.ds(group, 16), :], lat_tile.at[r], tile_sems.at[0, r])

    def rope_read(r):
        return pltpu.make_async_copy(rope_in.at[spots[r][2]], rope_tile.at[r], tile_sems.at[1, r])

    def lat_write(r):
        _, _, page, _, group = spots[r]
        return pltpu.make_async_copy(lat_tile.at[r], lat_out.at[page, pl.ds(group, 16), :], tile_sems.at[0, r])

    def rope_write(r):
        return pltpu.make_async_copy(rope_tile.at[r], rope_out.at[spots[r][2]], tile_sems.at[1, r])

    def in_pool(r):
        owned, local = spots[r][:2]
        return owned & ((moved != r) | (local < first))

    for r in range(requests):
        @pl.when(spots[r][0])
        def _():
            rope_read(r).start()

        @pl.when(in_pool(r))
        def _():
            lat_read(r).start()

    fetch.wait()
    for r in range(requests):
        owned, local, _, inside, group = spots[r]

        @pl.when(owned & received(r))
        def _():
            index = jnp.clip(local - first, 0, last - first - 1)
            piece = pl.ds(pl.multiple_of(index * PAGE + group, 16), 16)
            tile = got_v[piece, :].astype(F32)
            row = lax.broadcasted_iota(jnp.int32, tile.shape, 0)
            got_v[piece, :] = jnp.where(
                row == inside - group, new_lat[r : r + 1, :], tile
            ).astype(BF16)

    pages = [
        pltpu.make_async_copy(
            got_v.at[pl.ds(j * PAGE, PAGE)], lat_out.at[table[moved, first + j]], sems.at[j]
        )
        for j in range(last - first)
    ]
    for copy in pages:
        copy.start()
    for r in range(requests):
        owned, local, _, inside, group = spots[r]

        @pl.when(owned)
        def _():
            rope_read(r).wait()
            lane = lax.broadcasted_iota(jnp.int32, rope_tile.shape[1:], 1)
            rope_tile[r] = jnp.where(
                lane == inside, new_rope[:, r : r + 1], rope_tile[r].astype(F32)
            ).astype(BF16)
            rope_write(r).start()

        @pl.when(in_pool(r))
        def _():
            lat_read(r).wait()
            row = lax.broadcasted_iota(jnp.int32, lat_tile.shape[1:], 0)
            lat_tile[r] = jnp.where(
                row == inside - group, new_lat[r : r + 1, :], lat_tile[r].astype(F32)
            ).astype(BF16)
            lat_write(r).start()

    for r in range(requests):
        @pl.when(spots[r][0])
        def _():
            rope_write(r).wait()

        @pl.when(in_pool(r))
        def _():
            lat_write(r).wait()
    for copy in pages:
        copy.wait()


def body(
    hidden,
    lengths,
    page_table,
    move_slot,
    lat_pool,
    rope_pool,
    norm_attn,
    w_query,
    w_latent,
    latent_gain,
    w_key_up,
    w_value_up,
    w_output,
    norm_ffn,
    w_router,
    route_ids,
    expert_gate,
    expert_up,
    expert_down,
    shared_gate,
    shared_up,
    shared_down,
):
    requests, size = hidden.shape
    per_dev = page_table.shape[1]
    local_heads, nope_size, lat_size = w_key_up.shape
    local_experts, _, units = expert_gate.shape
    n_tp, n_rep = lax.axis_size("tp"), lax.axis_size("rep")
    groups = n_rep // 2
    half = n_rep // 2
    rows = local_heads * requests
    everyone = n_rep * requests
    pages = requests * per_dev
    width = lat_size + LANES
    tp_one = lax.axis_index("tp").astype(jnp.int32)[None]
    rep_one = lax.axis_index("rep").astype(jnp.int32)[None]
    page_bytes = PAGE * (lat_size + ROPE) * 2
    dma = pltpu.SemaphoreType.DMA
    first_span = per_dev * 6 // 10
    second_span = per_dev - first_span
    lat_page = lat_pool.shape[1:]
    rope_page = rope_pool.shape[1:]
    lat_hbm, rope_hbm = in_hbm(lat_pool), in_hbm(rope_pool)
    gate_t = jnp.swapaxes(expert_gate, 1, 2).reshape(-1, size)
    up_t = jnp.swapaxes(expert_up, 1, 2).reshape(-1, size)

    q_own, normed, out_first, out_rope = call(
        functools.partial(query_kernel, first_span),
        (
            struct((rows, lat_size + ROPE), BF16),
            struct((requests, size), BF16),
            struct((first_span,) + lat_page, BF16),
            struct((per_dev,) + rope_page, BF16),
        ),
        [ANY] * 8,
        (VMEM,) * 4,
        [
            pltpu.SMEM(page_table.shape, jnp.int32),
            pltpu.SMEM((1,), jnp.int32),
            pltpu.VMEM(hidden.shape, BF16),
            pltpu.VMEM((1, size), F32),
            pltpu.VMEM(w_query.shape, BF16),
            pltpu.VMEM(w_key_up.shape, BF16),
            dma((2, per_dev)),
            dma((9,)),
        ],
        vmem=8,
        flops=2 * requests * w_query.size,
        nbytes=2 * w_query.size,
    )(
        page_table, move_slot, in_hbm(hidden), in_hbm(norm_attn[None, :]),
        in_hbm(w_query), in_hbm(w_key_up), lat_hbm, rope_hbm,
    )
    got_first = xored(out_first, "rep", half)
    got_rope = xored(out_rope, "rep", half)
    q_blocks = [q_own] + [xored(q_own, "tp", k) for k in range(1, n_tp)]

    lat_v, rope_v, _ = call(
        functools.partial(fetch_kernel, requests),
        (
            pltpu.VMEM((pages,) + lat_page, BF16),
            pltpu.VMEM((pages,) + rope_page, BF16),
            struct((8, LANES), F32),
        ),
        [VMEM, ANY, ANY],
        (VMEM,) * 3,
        [dma((requests + 1,))],
        vmem=6,
        flops=2 * requests * w_latent.size,
        nbytes=pages * page_bytes + 2 * (w_latent.size + w_output.size + w_value_up.size),
    )(q_own, lat_hbm, rope_hbm)

    *partial, lat_most, rope_most = call(
        functools.partial(attention_kernel, n_tp, per_dev, requests, lat_size),
        tuple(struct((rows, width), BF16) for _ in range(n_tp))
        + (struct(lat_pool.shape, BF16), struct(rope_pool.shape, BF16)),
        [SMEM] * 3 + [VMEM] * (n_tp + 2),
        (VMEM,) * n_tp + (ANY, ANY),
        [pltpu.VMEM((width // LANES, n_tp * rows, LANES), F32)] * 2 + [dma((requests + 1,))],
        vmem=6,
        flops=4 * n_tp * rows * per_dev * PAGE * lat_size,
        nbytes=pages * page_bytes,
    )(page_table, lengths, tp_one, *q_blocks, lat_v, rope_v)
    parts = [partial[0]] + [xored(partial[k], "tp", k) for k in range(1, n_tp)]
    value_v, out_v, new = call(
        token_weights_kernel,
        (
            pltpu.VMEM(w_value_up.shape, BF16),
            pltpu.VMEM(w_output.shape, BF16),
            struct((requests, width), F32),
        ),
        [SMEM] + [VMEM] * 3 + [ANY] * 3,
        (VMEM,) * 3,
        [pltpu.VMEM((w_latent.shape[1], size), BF16), dma((3,))],
        vmem=6,
        flops=2 * requests * w_latent.size,
        nbytes=2 * (w_latent.size + w_output.size + w_value_up.size),
    )(
        lengths, normed, latent_gain[None, :], partial[0], in_hbm(w_latent.T),
        in_hbm(w_value_up), in_hbm(w_output),
    )

    out_part, out_sent = call(
        functools.partial(finish_kernel, n_tp, requests, lat_size),
        (struct((requests, size), F32), struct((requests, size), BF16)),
        [VMEM] * (n_tp + 4),
        (VMEM, VMEM),
        vmem=4,
        flops=2 * requests * size * w_output.shape[0],
        nbytes=2 * w_output.size + 2 * w_value_up.size,
    )(*parts, q_own, new, value_v, out_v)
    out_parts = [out_part] + [xored(out_sent, "tp", k) for k in range(1, n_tp)]

    ffn_row, h_one = call(
        functools.partial(norm_kernel, n_tp),
        (
            struct((requests, size + LANES), BF16),
            struct((requests, size), BF16),
        ),
        [SMEM] + [VMEM] * (n_tp + 2) + [ANY] * 2,
        (VMEM,) * 2,
        vmem=4,
        nbytes=8 * n_tp * requests * size,
    )(move_slot, *out_parts, hidden, norm_ffn[None, :], got_first, got_rope)

    pair = jnp.concatenate([ffn_row, xored(ffn_row, "rep", 1)], axis=0)
    pieces = [pair] + [xored(pair, "rep", 2 * k) for k in range(1, groups)]

    shared_part, out_second = call(
        functools.partial(shared_kernel, first_span, second_span),
        (
            struct((requests, size), F32),
            struct((second_span * PAGE + ROWS, lat_size), BF16),
        ),
        [SMEM, SMEM] + [VMEM] * 4 + [ANY] * 4,
        (VMEM, VMEM),
        [
            pltpu.VMEM((shared_gate.shape[1], size), BF16),
            pltpu.VMEM((shared_gate.shape[1], size), BF16),
            pltpu.VMEM(shared_down.shape, BF16),
            dma((3,)),
            dma((second_span,)),
        ],
        vmem=12,
        flops=6 * requests * shared_gate.size,
        nbytes=6 * shared_gate.size,
    )(
        page_table, move_slot, ffn_row, h_one, new, pair, in_hbm(shared_gate.T),
        in_hbm(shared_up.T), in_hbm(shared_down), lat_hbm,
    )
    x_all, coef, out_second = call(
        functools.partial(order_kernel, groups, requests),
        (
            struct((everyone, size), BF16),
            struct((everyone, w_router.shape[1]), F32),
            struct(out_second.shape, BF16),
        ),
        [SMEM] + [VMEM] * (groups + 3),
        (VMEM,) * 3,
        vmem=6,
        flops=4 * everyone * size * everyone,
        nbytes=4 * everyone * size,
        aliases={3 + groups: 2},
    )(rep_one, route_ids, w_router.T, *pieces, out_second)
    got_second = xored(out_second, "rep", half)
    got_row = got_second[second_span * PAGE :].reshape(1, -1)[:, : size + width + size]

    kept, sent = call(
        functools.partial(expert_kernel, requests, 512, units),
        (
            struct((groups * requests, size), F32),
            struct((groups * requests, size), BF16),
        ),
        [SMEM] + [VMEM] * 2 + [ANY] * 3,
        (VMEM, VMEM),
        [pltpu.VMEM((local_experts * units, size), BF16)] * 3
        + [pltpu.VMEM((everyone, size), F32), dma((3, pl.cdiv(local_experts * units, 512)))],
        vmem=42,
        flops=6 * everyone * expert_gate.size,
        nbytes=6 * expert_gate.size,
    )(
        rep_one, x_all, coef, in_hbm(gate_t), in_hbm(up_t), in_hbm(expert_down.reshape(-1, size)),
    )
    summed = call(
        functools.partial(pair_kernel, requests),
        (struct((requests, size), F32),) + (struct((requests, size), BF16),) * (groups - 1),
        [VMEM, VMEM, ANY],
        (VMEM,) * groups,
        vmem=4,
        nbytes=8 * everyone * size,
    )(kept, xored(sent, "rep", 1), got_second)
    others = [xored(summed[k], "rep", 2 * k) for k in range(1, groups)]
    lat_most, rope_most, cache_token = call(
        functools.partial(cache_kernel, first_span),
        (struct(lat_pool.shape, BF16), struct(rope_pool.shape, BF16), struct((8, LANES), F32)),
        [SMEM] * 2 + [VMEM] + [ANY] * 4,
        (ANY, ANY, VMEM),
        [
            pltpu.VMEM((first_span,) + lat_page, BF16),
            pltpu.VMEM((per_dev,) + rope_page, BF16),
            dma((2,)),
            dma((2, per_dev)),
        ],
        vmem=4,
        nbytes=2 * first_span * page_bytes,
        aliases={5: 0, 6: 1},
    )(page_table, move_slot, summed[0], got_first, got_rope, lat_most, rope_most)
    total, total_sent = call(
        total_kernel,
        (struct((requests, size), F32), struct((requests, size), BF16)),
        [SMEM] + [VMEM] * (groups + 3),
        (VMEM, VMEM),
        vmem=4,
        nbytes=8 * everyone * size,
    )(move_slot, got_row[:, size + width :], summed[0], shared_part, cache_token, *others)

    is_moved = (jnp.arange(requests, dtype=jnp.int32) == move_slot[0])[:, None]
    new_served = jnp.where(is_moved, got_row[:, size : size + width].astype(F32), new)
    marks = new_served[:, lat_size + ROPE : lat_size + ROPE + 2].astype(jnp.int32)
    len_served = marks[:, 0] * PAGE + marks[:, 1]
    lat_new = new_served[:, :lat_size]
    rope_new = new_served[:, lat_size : lat_size + ROPE].T
    lat_cache, rope_cache = call(
        functools.partial(token_kernel, first_span, per_dev),
        (struct(lat_pool.shape, BF16), struct(rope_pool.shape, BF16)),
        [SMEM] * 4 + [VMEM] * 2 + [ANY, VMEM] + [ANY] * 2,
        (ANY, ANY),
        [
            pltpu.VMEM((second_span * PAGE, lat_size), BF16),
            pltpu.VMEM((requests, 16, lat_size), BF16),
            pltpu.VMEM((requests,) + rope_page, BF16),
            dma((1,)),
            dma((second_span,)),
            dma((2, requests)),
        ],
        vmem=2,
        nbytes=2 * second_span * page_bytes,
        aliases={8: 0, 9: 1},
    )(
        page_table, move_slot, len_served, tp_one, lat_new, rope_new, got_second, total,
        lat_most, rope_most,
    )

    total_all = total
    for other in [xored(total_sent, "tp", k) for k in range(1, n_tp)]:
        total_all = total_all + other.astype(F32)
    h_served = jnp.where(is_moved, got_row[:, :size], h_one)
    mixed = (h_served.astype(F32) + total_all).astype(BF16)
    return (mixed, lat_cache, rope_cache)


def solution(mesh):
    in_specs = (
        P("rep", None),
        P("rep"),
        P("rep", "tp"),
        P("rep"),
        P(("rep", "tp"), None, None),
        P(("rep", "tp"), None, None),
        P(),
        P(None, "tp"),
        P(),
        P(),
        P("tp", None, None),
        P("tp", None, None),
        P("tp", None),
        P(),
        P(),
        P(),
        P("rep", None, "tp"),
        P("rep", None, "tp"),
        P("rep", "tp", None),
        P(None, "tp"),
        P(None, "tp"),
        P("tp", None),
    )
    out_specs = (P("rep", None), P(("rep", "tp"), None, None), P(("rep", "tp"), None, None))
    return jax.shard_map(body, mesh=mesh, in_specs=in_specs, out_specs=out_specs, check_vma=False)
```

```python
import functools

import jax
import jax.numpy as jnp
from jax import lax
from jax.experimental import pallas as pl
from jax.experimental.pallas import tpu as pltpu
from jax.sharding import PartitionSpec as P

NOPE = 128
ROPE = 64
SINKS = 4
WIN = 4096
PAGE = 128
LANES = 128
ROWS = 16
EPS = 1e-06
ROUTE_SCALE = 2.446
NEG = -1e30
F32 = jnp.float32
BF16 = jnp.bfloat16
NT = (((1,), (1,)), ((), ()))

VMEM = pl.BlockSpec(memory_space=pltpu.VMEM)
SMEM = pl.BlockSpec(memory_space=pltpu.SMEM)
ANY = pl.BlockSpec(memory_space=pl.ANY)


def xored(value, axis, mask):
    pairs = [(source, source ^ mask) for source in range(lax.axis_size(axis))]
    return lax.ppermute(value, axis, pairs)


def call(kernel, out_shape, in_specs, out_specs, scratch=(), vmem=8, flops=0, nbytes=0, aliases=None):
    return pl.pallas_call(
        kernel,
        out_shape=out_shape,
        in_specs=in_specs,
        out_specs=out_specs,
        scratch_shapes=list(scratch),
        input_output_aliases=aliases or {},
        compiler_params=pltpu.CompilerParams(vmem_limit_bytes=vmem * 1024 * 1024),
        cost_estimate=pl.CostEstimate(flops=flops, bytes_accessed=nbytes, transcendentals=0),
    )


def struct(shape, dtype):
    return jax.ShapeDtypeStruct(shape, dtype)


def in_hbm(value):
    return pltpu.with_memory_space_constraint(value, pltpu.HBM)


def rms_norm(values, gain):
    return values * lax.rsqrt(jnp.mean(values * values, axis=-1, keepdims=True) + EPS) * gain


def silu(value):
    return value / (1.0 + jnp.exp(-value))


def query_kernel(
    first, table_in, slot_in, x_in, gain_in, w_in, key_in, lat, rope,
    q_out, normed_out, lat_out, rope_out,
    table, slot, x, gain, w_query, key_up, sems, in_sems,
):
    per_dev = table.shape[1]
    size = x.shape[1]
    parts = in_sems.shape[0] - 5
    step = size // parts
    small = [
        pltpu.make_async_copy(source, target, in_sems.at[i])
        for i, (source, target) in enumerate(
            [(table_in, table), (slot_in, slot), (x_in, x), (gain_in, gain)]
        )
    ]
    for copy in small:
        copy.start()
    big = []
    for i in range(parts):
        piece = pl.ds(i * step, step)
        big.append(pltpu.make_async_copy(w_in.at[piece], w_query.at[piece], in_sems.at[4 + i]))
    big.append(pltpu.make_async_copy(key_in, key_up, in_sems.at[4 + parts]))
    for copy in big:
        copy.start()
    small[0].wait()
    small[1].wait()
    copies = []
    for j in range(per_dev):
        page = table[slot[0], j]
        if j < first:
            copies.append(pltpu.make_async_copy(lat.at[page], lat_out.at[j], sems.at[0, j]))
        copies.append(pltpu.make_async_copy(rope.at[page], rope_out.at[j], sems.at[1, j]))
    for copy in copies:
        copy.start()
    small[2].wait()
    small[3].wait()
    normed = rms_norm(x[...].astype(F32), gain[...]).astype(BF16)
    normed_out[...] = normed
    heads, nope, _ = key_up.shape
    query = None
    for i in range(parts):
        big[i].wait()
        piece = slice(i * step, (i + 1) * step)
        term = jnp.dot(normed[:, piece], w_query[piece, :], preferred_element_type=F32)
        query = term if query is None else query + term
    big[parts].wait()
    wide = query.shape[1] // heads
    rows = []
    for h in range(heads):
        one = query[:, h * wide : (h + 1) * wide]
        q_lat = jnp.dot(one[:, :nope].astype(BF16), key_up[h], preferred_element_type=F32)
        rows.append(jnp.concatenate([q_lat, one[:, nope:]], axis=1))
    q_out[...] = jnp.concatenate(rows, axis=0).astype(BF16)
    for copy in copies:
        copy.wait()


def fetch_kernel(parts, _, lat, rope, lat_v, rope_v, token, sems):
    token[...] = jnp.zeros_like(token)
    step = lat.shape[0] // parts
    copies = []
    for i in range(parts):
        piece = pl.ds(i * step, step)
        copies.append(pltpu.make_async_copy(lat.at[piece], lat_v.at[piece], sems.at[i]))
    copies.append(pltpu.make_async_copy(rope, rope_v, sems.at[parts]))
    for copy in copies:
        copy.start()
    for copy in copies:
        copy.wait()


def token_weights_kernel(
    lengths, normed, gain, _, w_latent, value_up, w_out, value_v, out_v, new_out, latent_v, sems,
):
    copies = [
        pltpu.make_async_copy(w_latent, latent_v, sems.at[0]),
        pltpu.make_async_copy(value_up, value_v, sems.at[1]),
        pltpu.make_async_copy(w_out, out_v, sems.at[2]),
    ]
    for copy in copies:
        copy.start()
    size = gain.shape[1]
    copies[0].wait()
    latent = lax.dot_general(normed[...], latent_v[...], NT, preferred_element_type=F32)
    c_new = rms_norm(latent[:, :size], gain[...]).astype(BF16).astype(F32)
    p_new = latent[:, size:].astype(BF16).astype(F32)
    lane = lax.broadcasted_iota(jnp.int32, (1, LANES), 1)
    marks = []
    for r in range(normed.shape[0]):
        page = jnp.full((1, LANES), lengths[r] // PAGE, jnp.int32)
        inside = jnp.full((1, LANES), lengths[r] % PAGE, jnp.int32)
        marks.append(jnp.where(lane == 0, page, jnp.where(lane == 1, inside, 0)))
    mark = jnp.concatenate(marks, axis=0).astype(F32)
    new_out[...] = jnp.concatenate([c_new, p_new, mark[:, : LANES - ROPE]], axis=1)
    copies[1].wait()
    copies[2].wait()


def attention_kernel(blocks, per_dev, requests, lat_size, *refs):
    table, lengths, rank = refs[:3]
    queries = refs[3 : 3 + blocks]
    lat, rope = refs[3 + blocks : 5 + blocks]
    outs = refs[5 + blocks : 5 + 2 * blocks]
    lat_out, rope_out, q_all, result, sems = refs[5 + 2 * blocks :]
    copies = []
    for r in range(requests):
        piece = pl.ds(r * per_dev, per_dev)
        copies.append(pltpu.make_async_copy(lat.at[piece], lat_out.at[piece], sems.at[r]))
    copies.append(pltpu.make_async_copy(rope, rope_out, sems.at[requests]))
    for copy in copies:
        copy.start()
    rows = queries[0].shape[0]
    heads = blocks * rows // requests
    scale = (NOPE + ROPE) ** (-0.5)
    tiles = lat_size // LANES
    for k in range(blocks):
        block = queries[k][...].astype(F32)
        for i in range(tiles + 1):
            piece = block[:, i * LANES : (i + 1) * LANES]
            q_all[i, k * rows : (k + 1) * rows, : piece.shape[1]] = piece
    base = rank[0] * (per_dev * PAGE)
    side = lax.broadcasted_iota(jnp.int32, (heads, LANES), 1)

    def attend(r, count):
        mine = pl.ds(r, heads, stride=requests)
        length = lengths[r]
        q_lat = jnp.concatenate([q_all[i, mine, :] for i in range(tiles)], axis=1).astype(BF16)
        q_pos = q_all[tiles, mine, :][:, :ROPE].astype(BF16)
        latents = jnp.concatenate([lat[table[r, j]] for j in range(count)], axis=0)
        scores = lax.dot_general(q_lat, latents, NT, preferred_element_type=F32)
        scores += jnp.concatenate(
            [
                jnp.dot(q_pos, rope[table[r, j]], preferred_element_type=F32)
                for j in range(count)
            ],
            axis=1,
        )
        scores *= scale
        position = base + lax.broadcasted_iota(jnp.int32, scores.shape, 1)
        allowed = (position < length) & ((position < SINKS) | (position >= length + 1 - WIN))
        peak = jnp.max(jnp.where(allowed, scores, NEG), axis=1, keepdims=True)
        weights = jnp.where(allowed, jnp.exp(scores - peak), 0.0).astype(BF16)
        total = jnp.sum(weights.astype(F32), axis=1, keepdims=True)
        sums = jnp.dot(weights, latents, preferred_element_type=F32)
        for i in range(tiles):
            result[i, mine, :] = sums[:, i * LANES : (i + 1) * LANES]
        result[tiles, mine, :] = jnp.where(side < LANES // 2, peak, total)

    few = min(2, per_dev)
    for r in range(requests):
        length = lengths[r]
        past = length <= base
        short = length <= base + few * PAGE

        @pl.when(past)
        def _():
            mine = pl.ds(r, heads, stride=requests)
            for i in range(tiles):
                result[i, mine, :] = jnp.zeros((heads, LANES), F32)
            result[tiles, mine, :] = jnp.where(side < LANES // 2, NEG, 0.0)

        @pl.when(jnp.logical_not(past) & short)
        def _():
            attend(r, few)

        @pl.when(jnp.logical_not(short))
        def _():
            attend(r, per_dev)

    for k in range(blocks):
        block = pl.ds(k * rows, rows)
        marks = result[tiles, block, :]
        peak, total = marks[:, :1], marks[:, LANES // 2 : LANES // 2 + 1]
        some = total > 0.0
        safe = jnp.where(some, total, 1.0)
        level = jnp.where(some, peak + jnp.log(safe), NEG)
        high = level.astype(BF16).astype(F32)
        middle = (level - high).astype(BF16).astype(F32)
        low = level - high - middle
        lane = lax.broadcasted_iota(jnp.int32, marks.shape, 1)
        split = jnp.where(lane == 0, high, jnp.where(lane == 1, middle, low))
        share = 1.0 / safe
        pieces = [result[i, block, :] * share for i in range(tiles)] + [split]
        outs[k][...] = jnp.concatenate(pieces, axis=1).astype(BF16)
    for copy in copies:
        copy.wait()


def finish_kernel(blocks, requests, lat_size, *refs):
    parts = refs[:blocks]
    query, new, value_up, w_out, out, sent = refs[blocks:]
    local_heads = value_up.shape[0]
    scale = (NOPE + ROPE) ** (-0.5)
    fresh = jnp.concatenate([new[:, : lat_size + ROPE]] * local_heads, axis=0)
    q_own = query[...].astype(F32)
    new_score = jnp.sum(q_own * fresh, axis=1, keepdims=True) * scale
    peak = new_score
    means = []
    for part in parts:
        wide = part[...].astype(F32)
        marks = wide[:, lat_size:]
        level = marks[:, 0:1] + marks[:, 1:2] + marks[:, 2:3]
        means.append((level, wide[:, :lat_size]))
        peak = jnp.maximum(peak, level)
    new_factor = jnp.exp(new_score - peak)
    denom = new_factor
    numer = new_factor * fresh[:, :lat_size]
    for level, mean in means:
        factor = jnp.exp(level - peak)
        denom += factor
        numer += factor * mean
    o_lat = numer / denom
    vals = []
    for h in range(local_heads):
        one = o_lat[h * requests : (h + 1) * requests, :].astype(BF16)
        vals.append(jnp.dot(one, value_up[h], preferred_element_type=F32).astype(BF16))
    o_val = jnp.concatenate(vals, axis=1)
    value = jnp.dot(o_val, w_out[...], preferred_element_type=F32)
    out[...] = value
    sent[...] = value.astype(BF16)


def norm_kernel(blocks, *refs):
    slot = refs[0]
    parts = refs[1 : 1 + blocks]
    x, gain = refs[1 + blocks : 3 + blocks]
    row_out, h_out = refs[-2:]
    attn = parts[0][...]
    for part in parts[1:]:
        attn += part[...].astype(F32)
    h_one = (x[...].astype(F32) + attn).astype(BF16)
    h_out[...] = h_one
    wide = h_one.astype(F32)
    normed = rms_norm(wide, gain[...])
    mark = jnp.full((wide.shape[0], LANES), slot[0], jnp.int32).astype(F32)
    row_out[...] = jnp.concatenate([normed, mark], axis=1).astype(BF16)


def copy_pages(table, slot, lat, lat_out, sems, first, count):
    copies = [
        pltpu.make_async_copy(
            lat.at[table[slot[0], first + j]], lat_out.at[pl.ds(j * PAGE, PAGE)], sems.at[j]
        )
        for j in range(count)
    ]
    for copy in copies:
        copy.start()
    return copies


def order_kernel(groups, requests, rank, route_ids, router, *refs):
    pieces = refs[:groups]
    x_out, coef_out, _ = refs[groups + 1 :]
    size = router.shape[1]
    wide = jnp.concatenate([p[...].astype(F32) for p in pieces], axis=0)
    rows = wide.shape[0]
    reps = rows // requests
    moved = wide[:, size : size + 1]
    other = jnp.concatenate([moved[rows // 2 :], moved[: rows // 2]], axis=0)
    row = lax.broadcasted_iota(jnp.int32, (rows, 1), 0)
    place = row // requests
    across = ((place + reps // 2) % reps) * requests
    source = jnp.where(
        row % requests == moved.astype(jnp.int32), across + other.astype(jnp.int32), row
    )
    column = lax.broadcasted_iota(jnp.int32, (rows, rows), 1)
    picks = (column == source).astype(F32).astype(BF16)
    x = jnp.dot(picks, wide[:, :size].astype(BF16), preferred_element_type=F32).astype(BF16)
    x_out[...] = x
    gates = jax.nn.sigmoid(lax.dot_general(x, router[...], NT, preferred_element_type=F32))
    home = (place ^ rank[0]) * requests + row % requests
    turns = (column == home).astype(F32).astype(BF16)
    ids = jnp.dot(turns, route_ids[...].astype(F32).astype(BF16), preferred_element_type=F32)
    ids = ids.astype(jnp.int32)
    expert = lax.broadcasted_iota(jnp.int32, gates.shape, 1)
    chosen = jnp.zeros(gates.shape, F32)
    for k in range(ids.shape[1]):
        chosen += jnp.where(expert == ids[:, k : k + 1], gates, 0.0)
    coef_out[...] = chosen / jnp.sum(chosen, axis=1, keepdims=True) * ROUTE_SCALE


def expert_kernel(
    requests, chunk, hidden, rank, x, coef, gate, up, down, kept, sent, gate_v, up_v, down_v, total, sems,
):
    units = gate.shape[0]
    pieces = [slice(b, min(b + chunk, units)) for b in range(0, units, chunk)]

    def fetch(which, source, target, i):
        piece = pl.ds(pieces[i].start, pieces[i].stop - pieces[i].start)
        return pltpu.make_async_copy(source.at[piece], target.at[piece], sems.at[which, i])

    copies = [
        [fetch(w, s, t, i) for w, (s, t) in enumerate([(gate, gate_v), (up, up_v), (down, down_v)])]
        for i in range(len(pieces))
    ]
    for trio in copies:
        for copy in trio:
            copy.start()
    count = units // hidden
    first = rank[0] * count
    weights = coef[...]
    expert = lax.broadcasted_iota(jnp.int32, weights.shape, 1)
    shares = [
        jnp.sum(jnp.where(expert == first + e, weights, 0.0), axis=1, keepdims=True)
        for e in range(count)
    ]
    rows = x.shape[0]
    for i, piece in enumerate(pieces):
        copies[i][0].wait()
        gate_val = lax.dot_general(x[...], gate_v[piece, :], NT, preferred_element_type=F32)
        copies[i][1].wait()
        up_val = lax.dot_general(x[...], up_v[piece, :], NT, preferred_element_type=F32)
        unit = piece.start + lax.broadcasted_iota(jnp.int32, gate_val.shape, 1)
        low, high = piece.start // hidden, (piece.stop - 1) // hidden
        share = jnp.broadcast_to(shares[high], gate_val.shape)
        for e in range(high - 1, low - 1, -1):
            share = jnp.where(unit < (e + 1) * hidden, shares[e], share)
        hid = (silu(gate_val) * up_val * share).astype(BF16)
        copies[i][2].wait()
        term = jnp.dot(hid, down_v[piece, :], preferred_element_type=F32)
        if i == 0:
            total[...] = term
        else:
            total[...] += term
    value = total[...]
    blocks = [value[p * requests : (p + 1) * requests] for p in range(rows // requests)]
    kept[...] = jnp.concatenate(blocks[0::2], axis=0)
    sent[...] = jnp.concatenate(blocks[1::2], axis=0).astype(BF16)


def pair_kernel(requests, kept, got, _, own, *blocks):
    total = kept[...] + got[...].astype(F32)
    own[...] = total[:requests]
    for k, block in enumerate(blocks):
        block[...] = total[(k + 1) * requests : (k + 2) * requests].astype(BF16)


def shared_kernel(
    first, count, table, slot, rows, h_one, new, _, gate, up, lat,
    out, next_out, gate_v, up_v, sems, page_sems,
):
    copies = [
        pltpu.make_async_copy(gate, gate_v, sems.at[0]),
        pltpu.make_async_copy(up, up_v, sems.at[1]),
    ]
    for copy in copies:
        copy.start()
    pages = copy_pages(table, slot, lat, next_out, page_sems, first, count)
    x = rows[:, : gate.shape[1]]
    copies[0].wait()
    gate_val = lax.dot_general(x, gate_v[...], NT, preferred_element_type=F32)
    copies[1].wait()
    up_val = lax.dot_general(x, up_v[...], NT, preferred_element_type=F32)
    hid = silu(gate_val) * up_val
    out[...] = hid.astype(BF16)
    every = jnp.concatenate([h_one[...].astype(F32), new[...], hid], axis=1)
    row = lax.broadcasted_iota(jnp.int32, every.shape, 0)
    every = jnp.sum(jnp.where(row == slot[0], every, 0.0), axis=0, keepdims=True)
    lat_size = next_out.shape[1]
    lines = [every[:, b : b + lat_size] for b in range(0, every.shape[1], lat_size)]
    lines[-1] = jnp.pad(lines[-1], ((0, 0), (0, lat_size - lines[-1].shape[1])))
    lines.append(jnp.zeros((ROWS - len(lines), lat_size), F32))
    next_out[count * PAGE :, :] = jnp.concatenate(lines, axis=0).astype(BF16)
    for copy in pages:
        copy.wait()


def total_kernel(own, shared, *refs):
    others, (total, sent) = refs[:-2], refs[-2:]
    value = own[...] + shared[...]
    for other in others:
        value += other[...].astype(F32)
    total[...] = value
    sent[...] = value.astype(BF16)


def token_spot(r, table, lengths, rank):
    per_dev = table.shape[1]
    local = lengths[r] // PAGE - rank[0] * per_dev
    owned = (local >= 0) & (local < per_dev)
    local = jnp.clip(local, 0, per_dev - 1)
    inside = lengths[r] % PAGE
    return owned, local, table[r, local], inside, pl.multiple_of(inside // 16 * 16, 16)


def cache_kernel(
    first, table, slot, _, hid, got_hid, down, got_lat, got_rope, lat_in, rope_in,
    lat_out, rope_out, shared, lat_v, rope_v, down_v, got_sems, sems,
):
    del lat_in, rope_in
    per_dev = table.shape[1]
    moved = slot[0]
    weights = pltpu.make_async_copy(down, down_v, got_sems.at[2])
    weights.start()
    fetches = [
        pltpu.make_async_copy(got_rope, rope_v, got_sems.at[0]),
        pltpu.make_async_copy(got_lat, lat_v, got_sems.at[1]),
    ]
    for copy in fetches:
        copy.start()
    for copy in fetches:
        copy.wait()
    copies = []
    for j in range(per_dev):
        page = table[moved, j]
        if j < first:
            copies.append(pltpu.make_async_copy(lat_v.at[j], lat_out.at[page], sems.at[0, j]))
        copies.append(pltpu.make_async_copy(rope_v.at[j], rope_out.at[page], sems.at[1, j]))
    for copy in copies:
        copy.start()
    row = lax.broadcasted_iota(jnp.int32, hid.shape, 0)
    served = jnp.where(row == moved, got_hid[...].astype(F32), hid[...].astype(F32)).astype(BF16)
    weights.wait()
    shared[...] = jnp.dot(served, down_v[...], preferred_element_type=F32)
    for copy in copies:
        copy.wait()


def token_kernel(
    first, last, table, slot, lengths, rank, new_lat, new_rope, got, _, lat_in, rope_in,
    lat_out, rope_out, got_v, lat_tile, rope_tile, got_sem, sems, tile_sems,
):
    requests, _ = table.shape
    moved = slot[0]
    fetch = pltpu.make_async_copy(got.at[pl.ds(0, got_v.shape[0])], got_v, got_sem.at[0])
    fetch.start()
    spots = [token_spot(r, table, lengths, rank) for r in range(requests)]

    def received(r):
        local = spots[r][1]
        return (moved == r) & (local >= first) & (local < last)

    def lat_read(r):
        _, _, page, _, group = spots[r]
        return pltpu.make_async_copy(lat_in.at[page, pl.ds(group, 16), :], lat_tile.at[r], tile_sems.at[0, r])

    def rope_read(r):
        return pltpu.make_async_copy(rope_in.at[spots[r][2]], rope_tile.at[r], tile_sems.at[1, r])

    def lat_write(r):
        _, _, page, _, group = spots[r]
        return pltpu.make_async_copy(lat_tile.at[r], lat_out.at[page, pl.ds(group, 16), :], tile_sems.at[0, r])

    def rope_write(r):
        return pltpu.make_async_copy(rope_tile.at[r], rope_out.at[spots[r][2]], tile_sems.at[1, r])

    def in_pool(r):
        owned, local = spots[r][:2]
        return owned & ((moved != r) | (local < first))

    for r in range(requests):
        @pl.when(spots[r][0])
        def _():
            rope_read(r).start()

        @pl.when(in_pool(r))
        def _():
            lat_read(r).start()

    fetch.wait()
    for r in range(requests):
        owned, local, _, inside, group = spots[r]

        @pl.when(owned & received(r))
        def _():
            index = jnp.clip(local - first, 0, last - first - 1)
            piece = pl.ds(pl.multiple_of(index * PAGE + group, 16), 16)
            tile = got_v[piece, :].astype(F32)
            row = lax.broadcasted_iota(jnp.int32, tile.shape, 0)
            got_v[piece, :] = jnp.where(
                row == inside - group, new_lat[r : r + 1, :], tile
            ).astype(BF16)

    pages = [
        pltpu.make_async_copy(
            got_v.at[pl.ds(j * PAGE, PAGE)], lat_out.at[table[moved, first + j]], sems.at[j]
        )
        for j in range(last - first)
    ]
    for copy in pages:
        copy.start()
    for r in range(requests):
        owned, local, _, inside, group = spots[r]

        @pl.when(owned)
        def _():
            rope_read(r).wait()
            lane = lax.broadcasted_iota(jnp.int32, rope_tile.shape[1:], 1)
            rope_tile[r] = jnp.where(
                lane == inside, new_rope[:, r : r + 1], rope_tile[r].astype(F32)
            ).astype(BF16)
            rope_write(r).start()

        @pl.when(in_pool(r))
        def _():
            lat_read(r).wait()
            row = lax.broadcasted_iota(jnp.int32, lat_tile.shape[1:], 0)
            lat_tile[r] = jnp.where(
                row == inside - group, new_lat[r : r + 1, :], lat_tile[r].astype(F32)
            ).astype(BF16)
            lat_write(r).start()

    for r in range(requests):
        @pl.when(spots[r][0])
        def _():
            rope_write(r).wait()

        @pl.when(in_pool(r))
        def _():
            lat_write(r).wait()
    for copy in pages:
        copy.wait()


def body(
    hidden,
    lengths,
    page_table,
    move_slot,
    lat_pool,
    rope_pool,
    norm_attn,
    w_query,
    w_latent,
    latent_gain,
    w_key_up,
    w_value_up,
    w_output,
    norm_ffn,
    w_router,
    route_ids,
    expert_gate,
    expert_up,
    expert_down,
    shared_gate,
    shared_up,
    shared_down,
):
    requests, size = hidden.shape
    per_dev = page_table.shape[1]
    local_heads, nope_size, lat_size = w_key_up.shape
    local_experts, _, units = expert_gate.shape
    n_tp, n_rep = lax.axis_size("tp"), lax.axis_size("rep")
    groups = n_rep // 2
    half = n_rep // 2
    rows = local_heads * requests
    everyone = n_rep * requests
    pages = requests * per_dev
    width = lat_size + LANES
    tp_one = lax.axis_index("tp").astype(jnp.int32)[None]
    rep_one = lax.axis_index("rep").astype(jnp.int32)[None]
    page_bytes = PAGE * (lat_size + ROPE) * 2
    dma = pltpu.SemaphoreType.DMA
    first_span = per_dev * 6 // 10
    second_span = per_dev - first_span
    lat_page = lat_pool.shape[1:]
    rope_page = rope_pool.shape[1:]
    lat_hbm, rope_hbm = in_hbm(lat_pool), in_hbm(rope_pool)
    gate_t = jnp.swapaxes(expert_gate, 1, 2).reshape(-1, size)
    up_t = jnp.swapaxes(expert_up, 1, 2).reshape(-1, size)

    q_own, normed, out_first, out_rope = call(
        functools.partial(query_kernel, first_span),
        (
            struct((rows, lat_size + ROPE), BF16),
            struct((requests, size), BF16),
            struct((first_span,) + lat_page, BF16),
            struct((per_dev,) + rope_page, BF16),
        ),
        [ANY] * 8,
        (VMEM,) * 4,
        [
            pltpu.SMEM(page_table.shape, jnp.int32),
            pltpu.SMEM((1,), jnp.int32),
            pltpu.VMEM(hidden.shape, BF16),
            pltpu.VMEM((1, size), F32),
            pltpu.VMEM(w_query.shape, BF16),
            pltpu.VMEM(w_key_up.shape, BF16),
            dma((2, per_dev)),
            dma((9,)),
        ],
        vmem=8,
        flops=2 * requests * w_query.size,
        nbytes=2 * w_query.size,
    )(
        page_table, move_slot, in_hbm(hidden), in_hbm(norm_attn[None, :]),
        in_hbm(w_query), in_hbm(w_key_up), lat_hbm, rope_hbm,
    )
    got_first = xored(out_first, "rep", half)
    got_rope = xored(out_rope, "rep", half)
    q_blocks = [q_own] + [xored(q_own, "tp", k) for k in range(1, n_tp)]

    lat_v, rope_v, _ = call(
        functools.partial(fetch_kernel, requests),
        (
            pltpu.VMEM((pages,) + lat_page, BF16),
            pltpu.VMEM((pages,) + rope_page, BF16),
            struct((8, LANES), F32),
        ),
        [VMEM, ANY, ANY],
        (VMEM,) * 3,
        [dma((requests + 1,))],
        vmem=6,
        flops=2 * requests * w_latent.size,
        nbytes=pages * page_bytes + 2 * (w_latent.size + w_output.size + w_value_up.size),
    )(q_own, lat_hbm, rope_hbm)

    *partial, lat_most, rope_most = call(
        functools.partial(attention_kernel, n_tp, per_dev, requests, lat_size),
        tuple(struct((rows, width), BF16) for _ in range(n_tp))
        + (struct(lat_pool.shape, BF16), struct(rope_pool.shape, BF16)),
        [SMEM] * 3 + [VMEM] * (n_tp + 2),
        (VMEM,) * n_tp + (ANY, ANY),
        [pltpu.VMEM((width // LANES, n_tp * rows, LANES), F32)] * 2 + [dma((requests + 1,))],
        vmem=6,
        flops=4 * n_tp * rows * per_dev * PAGE * lat_size,
        nbytes=pages * page_bytes,
    )(page_table, lengths, tp_one, *q_blocks, lat_v, rope_v)
    parts = [partial[0]] + [xored(partial[k], "tp", k) for k in range(1, n_tp)]
    value_v, out_v, new = call(
        token_weights_kernel,
        (
            pltpu.VMEM(w_value_up.shape, BF16),
            pltpu.VMEM(w_output.shape, BF16),
            struct((requests, width), F32),
        ),
        [SMEM] + [VMEM] * 3 + [ANY] * 3,
        (VMEM,) * 3,
        [pltpu.VMEM((w_latent.shape[1], size), BF16), dma((3,))],
        vmem=6,
        flops=2 * requests * w_latent.size,
        nbytes=2 * (w_latent.size + w_output.size + w_value_up.size),
    )(
        lengths, normed, latent_gain[None, :], partial[0], in_hbm(w_latent.T),
        in_hbm(w_value_up), in_hbm(w_output),
    )

    out_part, out_sent = call(
        functools.partial(finish_kernel, n_tp, requests, lat_size),
        (struct((requests, size), F32), struct((requests, size), BF16)),
        [VMEM] * (n_tp + 4),
        (VMEM, VMEM),
        vmem=4,
        flops=2 * requests * size * w_output.shape[0],
        nbytes=2 * w_output.size + 2 * w_value_up.size,
    )(*parts, q_own, new, value_v, out_v)
    out_parts = [out_part] + [xored(out_sent, "tp", k) for k in range(1, n_tp)]

    ffn_row, h_one = call(
        functools.partial(norm_kernel, n_tp),
        (
            struct((requests, size + LANES), BF16),
            struct((requests, size), BF16),
        ),
        [SMEM] + [VMEM] * (n_tp + 2) + [ANY] * 2,
        (VMEM,) * 2,
        vmem=4,
        nbytes=8 * n_tp * requests * size,
    )(move_slot, *out_parts, hidden, norm_ffn[None, :], got_first, got_rope)

    pair = jnp.concatenate([ffn_row, xored(ffn_row, "rep", 1)], axis=0)
    pieces = [pair] + [xored(pair, "rep", 2 * k) for k in range(1, groups)]

    shared_hid, out_second = call(
        functools.partial(shared_kernel, first_span, second_span),
        (
            struct((requests, shared_gate.shape[1]), BF16),
            struct((second_span * PAGE + ROWS, lat_size), BF16),
        ),
        [SMEM, SMEM] + [VMEM] * 4 + [ANY] * 3,
        (VMEM, VMEM),
        [
            pltpu.VMEM((shared_gate.shape[1], size), BF16),
            pltpu.VMEM((shared_gate.shape[1], size), BF16),
            dma((2,)),
            dma((second_span,)),
        ],
        vmem=12,
        flops=6 * requests * shared_gate.size,
        nbytes=6 * shared_gate.size,
    )(
        page_table, move_slot, ffn_row, h_one, new, pair, in_hbm(shared_gate.T),
        in_hbm(shared_up.T), lat_hbm,
    )
    x_all, coef, out_second = call(
        functools.partial(order_kernel, groups, requests),
        (
            struct((everyone, size), BF16),
            struct((everyone, w_router.shape[1]), F32),
            struct(out_second.shape, BF16),
        ),
        [SMEM] + [VMEM] * (groups + 3),
        (VMEM,) * 3,
        vmem=6,
        flops=4 * everyone * size * everyone,
        nbytes=4 * everyone * size,
        aliases={3 + groups: 2},
    )(rep_one, route_ids, w_router.T, *pieces, out_second)
    got_second = xored(out_second, "rep", half)
    got_row = got_second[second_span * PAGE :].reshape(1, -1)

    kept, sent = call(
        functools.partial(expert_kernel, requests, 512, units),
        (
            struct((groups * requests, size), F32),
            struct((groups * requests, size), BF16),
        ),
        [SMEM] + [VMEM] * 2 + [ANY] * 3,
        (VMEM, VMEM),
        [pltpu.VMEM((local_experts * units, size), BF16)] * 3
        + [pltpu.VMEM((everyone, size), F32), dma((3, pl.cdiv(local_experts * units, 512)))],
        vmem=42,
        flops=6 * everyone * expert_gate.size,
        nbytes=6 * expert_gate.size,
    )(
        rep_one, x_all, coef, in_hbm(gate_t), in_hbm(up_t), in_hbm(expert_down.reshape(-1, size)),
    )
    summed = call(
        functools.partial(pair_kernel, requests),
        (struct((requests, size), F32),) + (struct((requests, size), BF16),) * (groups - 1),
        [VMEM, VMEM, ANY],
        (VMEM,) * groups,
        vmem=4,
        nbytes=8 * everyone * size,
    )(kept, xored(sent, "rep", 1), got_second)
    others = [xored(summed[k], "rep", 2 * k) for k in range(1, groups)]
    lat_most, rope_most, shared_part = call(
        functools.partial(cache_kernel, first_span),
        (struct(lat_pool.shape, BF16), struct(rope_pool.shape, BF16), struct((requests, size), F32)),
        [SMEM] * 2 + [VMEM] * 3 + [ANY] * 5,
        (ANY, ANY, VMEM),
        [
            pltpu.VMEM((first_span,) + lat_page, BF16),
            pltpu.VMEM((per_dev,) + rope_page, BF16),
            pltpu.VMEM(shared_down.shape, BF16),
            dma((3,)),
            dma((2, per_dev)),
        ],
        vmem=8,
        nbytes=2 * first_span * page_bytes,
        aliases={8: 0, 9: 1},
    )(
        page_table, move_slot, summed[0], shared_hid,
        got_row[:, size + width : size + width + shared_gate.shape[1]], in_hbm(shared_down),
        got_first, got_rope, lat_most, rope_most,
    )
    total, total_sent = call(
        total_kernel,
        (struct((requests, size), F32), struct((requests, size), BF16)),
        [VMEM] * (groups + 1),
        (VMEM, VMEM),
        vmem=4,
        nbytes=8 * everyone * size,
    )(summed[0], shared_part, *others)

    is_moved = (jnp.arange(requests, dtype=jnp.int32) == move_slot[0])[:, None]
    new_served = jnp.where(is_moved, got_row[:, size : size + width].astype(F32), new)
    marks = new_served[:, lat_size + ROPE : lat_size + ROPE + 2].astype(jnp.int32)
    len_served = marks[:, 0] * PAGE + marks[:, 1]
    lat_new = new_served[:, :lat_size]
    rope_new = new_served[:, lat_size : lat_size + ROPE].T
    lat_cache, rope_cache = call(
        functools.partial(token_kernel, first_span, per_dev),
        (struct(lat_pool.shape, BF16), struct(rope_pool.shape, BF16)),
        [SMEM] * 4 + [VMEM] * 2 + [ANY, VMEM] + [ANY] * 2,
        (ANY, ANY),
        [
            pltpu.VMEM((second_span * PAGE, lat_size), BF16),
            pltpu.VMEM((requests, 16, lat_size), BF16),
            pltpu.VMEM((requests,) + rope_page, BF16),
            dma((1,)),
            dma((second_span,)),
            dma((2, requests)),
        ],
        vmem=2,
        nbytes=2 * second_span * page_bytes,
        aliases={8: 0, 9: 1},
    )(
        page_table, move_slot, len_served, tp_one, lat_new, rope_new, got_second, total,
        lat_most, rope_most,
    )

    total_all = total
    for other in [xored(total_sent, "tp", k) for k in range(1, n_tp)]:
        total_all = total_all + other.astype(F32)
    h_served = jnp.where(is_moved, got_row[:, :size], h_one)
    mixed = (h_served.astype(F32) + total_all).astype(BF16)
    return (mixed, lat_cache, rope_cache)


def solution(mesh):
    in_specs = (
        P("rep", None),
        P("rep"),
        P("rep", "tp"),
        P("rep"),
        P(("rep", "tp"), None, None),
        P(("rep", "tp"), None, None),
        P(),
        P(None, "tp"),
        P(),
        P(),
        P("tp", None, None),
        P("tp", None, None),
        P("tp", None),
        P(),
        P(),
        P(),
        P("rep", None, "tp"),
        P("rep", None, "tp"),
        P("rep", "tp", None),
        P(None, "tp"),
        P(None, "tp"),
        P("tp", None),
    )
    out_specs = (P("rep", None), P(("rep", "tp"), None, None), P(("rep", "tp"), None, None))
    return jax.shard_map(body, mesh=mesh, in_specs=in_specs, out_specs=out_specs, check_vma=False)
```

```python
import functools

import jax
import jax.numpy as jnp
from jax import lax
from jax.experimental import pallas as pl
from jax.experimental.pallas import tpu as pltpu
from jax.sharding import PartitionSpec as P

NOPE = 128
ROPE = 64
SINKS = 4
WIN = 4096
PAGE = 128
LANES = 128
ROWS = 16
EPS = 1e-06
ROUTE_SCALE = 2.446
NEG = -1e30
F32 = jnp.float32
BF16 = jnp.bfloat16
NT = (((1,), (1,)), ((), ()))

VMEM = pl.BlockSpec(memory_space=pltpu.VMEM)
SMEM = pl.BlockSpec(memory_space=pltpu.SMEM)
ANY = pl.BlockSpec(memory_space=pl.ANY)


def xored(value, axis, mask):
    pairs = [(source, source ^ mask) for source in range(lax.axis_size(axis))]
    return lax.ppermute(value, axis, pairs)


def call(kernel, out_shape, in_specs, out_specs, scratch=(), vmem=8, flops=0, nbytes=0, aliases=None):
    return pl.pallas_call(
        kernel,
        out_shape=out_shape,
        in_specs=in_specs,
        out_specs=out_specs,
        scratch_shapes=list(scratch),
        input_output_aliases=aliases or {},
        compiler_params=pltpu.CompilerParams(vmem_limit_bytes=vmem * 1024 * 1024),
        cost_estimate=pl.CostEstimate(flops=flops, bytes_accessed=nbytes, transcendentals=0),
    )


def struct(shape, dtype):
    return jax.ShapeDtypeStruct(shape, dtype)


def in_hbm(value):
    return pltpu.with_memory_space_constraint(value, pltpu.HBM)


def rms_norm(values, gain):
    return values * lax.rsqrt(jnp.mean(values * values, axis=-1, keepdims=True) + EPS) * gain


def silu(value):
    return value / (1.0 + jnp.exp(-value))


def query_kernel(
    first, table_in, slot_in, x_in, gain_in, w_in, key_in, lat, rope,
    q_out, normed_out, lat_out, rope_out,
    table, slot, x, gain, w_query, key_up, sems, in_sems,
):
    per_dev = table.shape[1]
    size = x.shape[1]
    parts = in_sems.shape[0] - 5
    step = size // parts
    small = [
        pltpu.make_async_copy(source, target, in_sems.at[i])
        for i, (source, target) in enumerate(
            [(table_in, table), (slot_in, slot), (x_in, x), (gain_in, gain)]
        )
    ]
    for copy in small:
        copy.start()
    big = []
    for i in range(parts):
        piece = pl.ds(i * step, step)
        big.append(pltpu.make_async_copy(w_in.at[piece], w_query.at[piece], in_sems.at[4 + i]))
    big.append(pltpu.make_async_copy(key_in, key_up, in_sems.at[4 + parts]))
    for copy in big:
        copy.start()
    small[0].wait()
    small[1].wait()
    copies = []
    for j in range(per_dev):
        page = table[slot[0], j]
        if j < first:
            copies.append(pltpu.make_async_copy(lat.at[page], lat_out.at[j], sems.at[0, j]))
        copies.append(pltpu.make_async_copy(rope.at[page], rope_out.at[j], sems.at[1, j]))
    for copy in copies:
        copy.start()
    small[2].wait()
    small[3].wait()
    normed = rms_norm(x[...].astype(F32), gain[...]).astype(BF16)
    normed_out[...] = normed
    heads, nope, _ = key_up.shape
    query = None
    for i in range(parts):
        big[i].wait()
        piece = slice(i * step, (i + 1) * step)
        term = jnp.dot(normed[:, piece], w_query[piece, :], preferred_element_type=F32)
        query = term if query is None else query + term
    big[parts].wait()
    wide = query.shape[1] // heads
    rows = []
    for h in range(heads):
        one = query[:, h * wide : (h + 1) * wide]
        q_lat = jnp.dot(one[:, :nope].astype(BF16), key_up[h], preferred_element_type=F32)
        rows.append(jnp.concatenate([q_lat, one[:, nope:]], axis=1))
    q_out[...] = jnp.concatenate(rows, axis=0).astype(BF16)
    for copy in copies:
        copy.wait()


def fetch_kernel(parts, _, lat, rope, lat_v, rope_v, token, sems):
    token[...] = jnp.zeros_like(token)
    step = lat.shape[0] // parts
    copies = []
    for i in range(parts):
        piece = pl.ds(i * step, step)
        copies.append(pltpu.make_async_copy(lat.at[piece], lat_v.at[piece], sems.at[i]))
    copies.append(pltpu.make_async_copy(rope, rope_v, sems.at[parts]))
    for copy in copies:
        copy.start()
    for copy in copies:
        copy.wait()


def token_weights_kernel(
    lengths, normed, gain, _, w_latent, value_up, w_out, value_v, out_v, new_out, latent_v, sems,
):
    copies = [
        pltpu.make_async_copy(w_latent, latent_v, sems.at[0]),
        pltpu.make_async_copy(value_up, value_v, sems.at[1]),
        pltpu.make_async_copy(w_out, out_v, sems.at[2]),
    ]
    for copy in copies:
        copy.start()
    size = gain.shape[1]
    copies[0].wait()
    latent = lax.dot_general(normed[...], latent_v[...], NT, preferred_element_type=F32)
    c_new = rms_norm(latent[:, :size], gain[...]).astype(BF16).astype(F32)
    p_new = latent[:, size:].astype(BF16).astype(F32)
    lane = lax.broadcasted_iota(jnp.int32, (1, LANES), 1)
    marks = []
    for r in range(normed.shape[0]):
        page = jnp.full((1, LANES), lengths[r] // PAGE, jnp.int32)
        inside = jnp.full((1, LANES), lengths[r] % PAGE, jnp.int32)
        marks.append(jnp.where(lane == 0, page, jnp.where(lane == 1, inside, 0)))
    mark = jnp.concatenate(marks, axis=0).astype(F32)
    new_out[...] = jnp.concatenate([c_new, p_new, mark[:, : LANES - ROPE]], axis=1)
    copies[1].wait()
    copies[2].wait()


def attention_kernel(blocks, per_dev, requests, lat_size, *refs):
    table, lengths, rank = refs[:3]
    queries = refs[3 : 3 + blocks]
    lat, rope = refs[3 + blocks : 5 + blocks]
    outs = refs[5 + blocks : 5 + 2 * blocks]
    lat_out, rope_out, q_all, result, sems = refs[5 + 2 * blocks :]
    copies = []
    for r in range(requests):
        piece = pl.ds(r * per_dev, per_dev)
        copies.append(pltpu.make_async_copy(lat.at[piece], lat_out.at[piece], sems.at[r]))
    copies.append(pltpu.make_async_copy(rope, rope_out, sems.at[requests]))
    for copy in copies:
        copy.start()
    rows = queries[0].shape[0]
    heads = blocks * rows // requests
    scale = (NOPE + ROPE) ** (-0.5)
    tiles = lat_size // LANES
    for k in range(blocks):
        block = queries[k][...].astype(F32)
        for i in range(tiles + 1):
            piece = block[:, i * LANES : (i + 1) * LANES]
            q_all[i, k * rows : (k + 1) * rows, : piece.shape[1]] = piece
    base = rank[0] * (per_dev * PAGE)
    side = lax.broadcasted_iota(jnp.int32, (heads, LANES), 1)

    def attend(r, count):
        mine = pl.ds(r, heads, stride=requests)
        length = lengths[r]
        q_lat = jnp.concatenate([q_all[i, mine, :] for i in range(tiles)], axis=1).astype(BF16)
        q_pos = q_all[tiles, mine, :][:, :ROPE].astype(BF16)
        latents = jnp.concatenate([lat[table[r, j]] for j in range(count)], axis=0)
        scores = lax.dot_general(q_lat, latents, NT, preferred_element_type=F32)
        scores += jnp.concatenate(
            [
                jnp.dot(q_pos, rope[table[r, j]], preferred_element_type=F32)
                for j in range(count)
            ],
            axis=1,
        )
        scores *= scale
        position = base + lax.broadcasted_iota(jnp.int32, scores.shape, 1)
        allowed = (position < length) & ((position < SINKS) | (position >= length + 1 - WIN))
        peak = jnp.max(jnp.where(allowed, scores, NEG), axis=1, keepdims=True)
        weights = jnp.where(allowed, jnp.exp(scores - peak), 0.0).astype(BF16)
        total = jnp.sum(weights.astype(F32), axis=1, keepdims=True)
        sums = jnp.dot(weights, latents, preferred_element_type=F32)
        for i in range(tiles):
            result[i, mine, :] = sums[:, i * LANES : (i + 1) * LANES]
        result[tiles, mine, :] = jnp.where(side < LANES // 2, peak, total)

    few = min(2, per_dev)
    for r in range(requests):
        length = lengths[r]
        past = length <= base
        short = length <= base + few * PAGE

        @pl.when(past)
        def _():
            mine = pl.ds(r, heads, stride=requests)
            for i in range(tiles):
                result[i, mine, :] = jnp.zeros((heads, LANES), F32)
            result[tiles, mine, :] = jnp.where(side < LANES // 2, NEG, 0.0)

        @pl.when(jnp.logical_not(past) & short)
        def _():
            attend(r, few)

        @pl.when(jnp.logical_not(short))
        def _():
            attend(r, per_dev)

    for k in range(blocks):
        block = pl.ds(k * rows, rows)
        marks = result[tiles, block, :]
        peak, total = marks[:, :1], marks[:, LANES // 2 : LANES // 2 + 1]
        some = total > 0.0
        safe = jnp.where(some, total, 1.0)
        level = jnp.where(some, peak + jnp.log(safe), NEG)
        high = level.astype(BF16).astype(F32)
        middle = (level - high).astype(BF16).astype(F32)
        low = level - high - middle
        lane = lax.broadcasted_iota(jnp.int32, marks.shape, 1)
        split = jnp.where(lane == 0, high, jnp.where(lane == 1, middle, low))
        share = 1.0 / safe
        pieces = [result[i, block, :] * share for i in range(tiles)] + [split]
        outs[k][...] = jnp.concatenate(pieces, axis=1).astype(BF16)
    for copy in copies:
        copy.wait()


def finish_kernel(blocks, requests, lat_size, *refs):
    parts = refs[:blocks]
    query, new, value_up, w_out, out, sent = refs[blocks:]
    local_heads = value_up.shape[0]
    scale = (NOPE + ROPE) ** (-0.5)
    fresh = jnp.concatenate([new[:, : lat_size + ROPE]] * local_heads, axis=0)
    q_own = query[...].astype(F32)
    new_score = jnp.sum(q_own * fresh, axis=1, keepdims=True) * scale
    peak = new_score
    means = []
    for part in parts:
        wide = part[...].astype(F32)
        marks = wide[:, lat_size:]
        level = marks[:, 0:1] + marks[:, 1:2] + marks[:, 2:3]
        means.append((level, wide[:, :lat_size]))
        peak = jnp.maximum(peak, level)
    new_factor = jnp.exp(new_score - peak)
    denom = new_factor
    numer = new_factor * fresh[:, :lat_size]
    for level, mean in means:
        factor = jnp.exp(level - peak)
        denom += factor
        numer += factor * mean
    o_lat = numer / denom
    vals = []
    for h in range(local_heads):
        one = o_lat[h * requests : (h + 1) * requests, :].astype(BF16)
        vals.append(jnp.dot(one, value_up[h], preferred_element_type=F32).astype(BF16))
    o_val = jnp.concatenate(vals, axis=1)
    value = jnp.dot(o_val, w_out[...], preferred_element_type=F32)
    out[...] = value
    sent[...] = value.astype(BF16)


def norm_kernel(blocks, *refs):
    slot = refs[0]
    parts = refs[1 : 1 + blocks]
    x, gain = refs[1 + blocks : 3 + blocks]
    row_out, h_out = refs[-2:]
    attn = parts[0][...]
    for part in parts[1:]:
        attn += part[...].astype(F32)
    h_one = (x[...].astype(F32) + attn).astype(BF16)
    h_out[...] = h_one
    wide = h_one.astype(F32)
    normed = rms_norm(wide, gain[...])
    mark = jnp.full((wide.shape[0], LANES), slot[0], jnp.int32).astype(F32)
    row_out[...] = jnp.concatenate([normed, mark], axis=1).astype(BF16)


def copy_pages(table, slot, lat, lat_out, sems, first, count):
    copies = [
        pltpu.make_async_copy(
            lat.at[table[slot[0], first + j]], lat_out.at[pl.ds(j * PAGE, PAGE)], sems.at[j]
        )
        for j in range(count)
    ]
    for copy in copies:
        copy.start()
    return copies


def order_kernel(groups, requests, rank, route_ids, router, *refs):
    pieces = refs[:groups]
    x_out, coef_out, _ = refs[groups + 1 :]
    size = router.shape[1]
    wide = jnp.concatenate([p[...].astype(F32) for p in pieces], axis=0)
    rows = wide.shape[0]
    reps = rows // requests
    moved = wide[:, size : size + 1]
    other = jnp.concatenate([moved[rows // 2 :], moved[: rows // 2]], axis=0)
    row = lax.broadcasted_iota(jnp.int32, (rows, 1), 0)
    place = row // requests
    across = ((place + reps // 2) % reps) * requests
    source = jnp.where(
        row % requests == moved.astype(jnp.int32), across + other.astype(jnp.int32), row
    )
    column = lax.broadcasted_iota(jnp.int32, (rows, rows), 1)
    picks = (column == source).astype(F32).astype(BF16)
    x = jnp.dot(picks, wide[:, :size].astype(BF16), preferred_element_type=F32).astype(BF16)
    x_out[...] = x
    gates = jax.nn.sigmoid(lax.dot_general(x, router[...], NT, preferred_element_type=F32))
    home = (place ^ rank[0]) * requests + row % requests
    turns = (column == home).astype(F32).astype(BF16)
    ids = jnp.dot(turns, route_ids[...].astype(F32).astype(BF16), preferred_element_type=F32)
    ids = ids.astype(jnp.int32)
    expert = lax.broadcasted_iota(jnp.int32, gates.shape, 1)
    chosen = jnp.zeros(gates.shape, F32)
    for k in range(ids.shape[1]):
        chosen += jnp.where(expert == ids[:, k : k + 1], gates, 0.0)
    coef_out[...] = chosen / jnp.sum(chosen, axis=1, keepdims=True) * ROUTE_SCALE


def expert_kernel(
    requests, chunk, hidden, rank, x, coef, gate, up, down, kept, sent, gate_v, up_v, down_v, total, sems,
):
    units = gate.shape[0]
    pieces = [slice(b, min(b + chunk, units)) for b in range(0, units, chunk)]

    def fetch(which, source, target, i):
        piece = pl.ds(pieces[i].start, pieces[i].stop - pieces[i].start)
        return pltpu.make_async_copy(source.at[piece], target.at[piece], sems.at[which, i])

    copies = [
        [fetch(w, s, t, i) for w, (s, t) in enumerate([(gate, gate_v), (up, up_v), (down, down_v)])]
        for i in range(len(pieces))
    ]
    for trio in copies:
        for copy in trio:
            copy.start()
    count = units // hidden
    first = rank[0] * count
    weights = coef[...]
    expert = lax.broadcasted_iota(jnp.int32, weights.shape, 1)
    shares = [
        jnp.sum(jnp.where(expert == first + e, weights, 0.0), axis=1, keepdims=True)
        for e in range(count)
    ]
    rows = x.shape[0]
    for i, piece in enumerate(pieces):
        copies[i][0].wait()
        gate_val = lax.dot_general(x[...], gate_v[piece, :], NT, preferred_element_type=F32)
        copies[i][1].wait()
        up_val = lax.dot_general(x[...], up_v[piece, :], NT, preferred_element_type=F32)
        unit = piece.start + lax.broadcasted_iota(jnp.int32, gate_val.shape, 1)
        low, high = piece.start // hidden, (piece.stop - 1) // hidden
        share = jnp.broadcast_to(shares[high], gate_val.shape)
        for e in range(high - 1, low - 1, -1):
            share = jnp.where(unit < (e + 1) * hidden, shares[e], share)
        hid = (silu(gate_val) * up_val * share).astype(BF16)
        copies[i][2].wait()
        term = jnp.dot(hid, down_v[piece, :], preferred_element_type=F32)
        if i == 0:
            total[...] = term
        else:
            total[...] += term
    value = total[...]
    blocks = [value[p * requests : (p + 1) * requests] for p in range(rows // requests)]
    kept[...] = jnp.concatenate(blocks[0::2], axis=0)
    sent[...] = jnp.concatenate(blocks[1::2], axis=0).astype(BF16)


def pair_kernel(requests, kept, got, _, own, *blocks):
    total = kept[...] + got[...].astype(F32)
    own[...] = total[:requests]
    for k, block in enumerate(blocks):
        block[...] = total[(k + 1) * requests : (k + 2) * requests].astype(BF16)


def shared_kernel(
    first, count, table, slot, rows, h_one, new, _, gate, up, lat,
    out, next_out, gate_v, up_v, sems, page_sems,
):
    copies = [
        pltpu.make_async_copy(gate, gate_v, sems.at[0]),
        pltpu.make_async_copy(up, up_v, sems.at[1]),
    ]
    for copy in copies:
        copy.start()
    pages = copy_pages(table, slot, lat, next_out, page_sems, first, count)
    x = rows[:, : gate.shape[1]]
    copies[0].wait()
    gate_val = lax.dot_general(x, gate_v[...], NT, preferred_element_type=F32)
    copies[1].wait()
    up_val = lax.dot_general(x, up_v[...], NT, preferred_element_type=F32)
    hid = silu(gate_val) * up_val
    out[...] = hid.astype(BF16)
    every = jnp.concatenate([h_one[...].astype(F32), new[...], hid], axis=1)
    row = lax.broadcasted_iota(jnp.int32, every.shape, 0)
    every = jnp.sum(jnp.where(row == slot[0], every, 0.0), axis=0, keepdims=True)
    lat_size = next_out.shape[1]
    lines = [every[:, b : b + lat_size] for b in range(0, every.shape[1], lat_size)]
    lines[-1] = jnp.pad(lines[-1], ((0, 0), (0, lat_size - lines[-1].shape[1])))
    lines.append(jnp.zeros((ROWS - len(lines), lat_size), F32))
    next_out[count * PAGE :, :] = jnp.concatenate(lines, axis=0).astype(BF16)
    for copy in pages:
        copy.wait()


def total_kernel(own, shared, *refs):
    others, (total, sent) = refs[:-2], refs[-2:]
    value = own[...] + shared[...]
    for other in others:
        value += other[...].astype(F32)
    total[...] = value
    sent[...] = value.astype(BF16)


def token_spot(r, table, lengths, rank):
    per_dev = table.shape[1]
    local = lengths[r] // PAGE - rank[0] * per_dev
    owned = (local >= 0) & (local < per_dev)
    local = jnp.clip(local, 0, per_dev - 1)
    inside = lengths[r] % PAGE
    return owned, local, table[r, local], inside, pl.multiple_of(inside // 16 * 16, 16)


def cache_kernel(
    first, table, slot, _, hid, got_hid, down, got_lat, got_rope, lat_in, rope_in,
    lat_out, rope_out, shared, lat_v, rope_v, down_v, got_sems, sems,
):
    del lat_in, rope_in
    per_dev = table.shape[1]
    moved = slot[0]
    weights = pltpu.make_async_copy(down, down_v, got_sems.at[2])
    weights.start()
    fetches = [
        pltpu.make_async_copy(got_rope, rope_v, got_sems.at[0]),
        pltpu.make_async_copy(got_lat, lat_v, got_sems.at[1]),
    ]
    for copy in fetches:
        copy.start()
    for copy in fetches:
        copy.wait()
    copies = []
    for j in range(per_dev):
        page = table[moved, j]
        if j < first:
            copies.append(pltpu.make_async_copy(lat_v.at[j], lat_out.at[page], sems.at[0, j]))
        copies.append(pltpu.make_async_copy(rope_v.at[j], rope_out.at[page], sems.at[1, j]))
    for copy in copies:
        copy.start()
    row = lax.broadcasted_iota(jnp.int32, hid.shape, 0)
    served = jnp.where(row == moved, got_hid[...].astype(F32), hid[...].astype(F32)).astype(BF16)
    weights.wait()
    shared[...] = jnp.dot(served, down_v[...], preferred_element_type=F32)
    for copy in copies:
        copy.wait()


def token_kernel(
    first, last, table, slot, lengths, rank, new_lat, new_rope, got, _, lat_in, rope_in,
    lat_out, rope_out, got_v, lat_tile, rope_tile, got_sem, sems, tile_sems,
):
    requests, _ = table.shape
    moved = slot[0]
    fetch = pltpu.make_async_copy(got.at[pl.ds(0, got_v.shape[0])], got_v, got_sem.at[0])
    fetch.start()
    spots = [token_spot(r, table, lengths, rank) for r in range(requests)]

    def received(r):
        local = spots[r][1]
        return (moved == r) & (local >= first) & (local < last)

    def lat_read(r):
        _, _, page, _, group = spots[r]
        return pltpu.make_async_copy(lat_in.at[page, pl.ds(group, 16), :], lat_tile.at[r], tile_sems.at[0, r])

    def rope_read(r):
        return pltpu.make_async_copy(rope_in.at[spots[r][2]], rope_tile.at[r], tile_sems.at[1, r])

    def lat_write(r):
        _, _, page, _, group = spots[r]
        return pltpu.make_async_copy(lat_tile.at[r], lat_out.at[page, pl.ds(group, 16), :], tile_sems.at[0, r])

    def rope_write(r):
        return pltpu.make_async_copy(rope_tile.at[r], rope_out.at[spots[r][2]], tile_sems.at[1, r])

    def in_pool(r):
        owned, local = spots[r][:2]
        return owned & ((moved != r) | (local < first))

    for r in range(requests):
        @pl.when(spots[r][0])
        def _():
            rope_read(r).start()

        @pl.when(in_pool(r))
        def _():
            lat_read(r).start()

    fetch.wait()
    for r in range(requests):
        owned, local, _, inside, group = spots[r]

        @pl.when(owned & received(r))
        def _():
            index = jnp.clip(local - first, 0, last - first - 1)
            piece = pl.ds(pl.multiple_of(index * PAGE + group, 16), 16)
            tile = got_v[piece, :].astype(F32)
            row = lax.broadcasted_iota(jnp.int32, tile.shape, 0)
            got_v[piece, :] = jnp.where(
                row == inside - group, new_lat[r : r + 1, :], tile
            ).astype(BF16)

    pages = [
        pltpu.make_async_copy(
            got_v.at[pl.ds(j * PAGE, PAGE)], lat_out.at[table[moved, first + j]], sems.at[j]
        )
        for j in range(last - first)
    ]
    for copy in pages:
        copy.start()
    for r in range(requests):
        owned, local, _, inside, group = spots[r]

        @pl.when(owned)
        def _():
            rope_read(r).wait()
            lane = lax.broadcasted_iota(jnp.int32, rope_tile.shape[1:], 1)
            rope_tile[r] = jnp.where(
                lane == inside, new_rope[:, r : r + 1], rope_tile[r].astype(F32)
            ).astype(BF16)
            rope_write(r).start()

        @pl.when(in_pool(r))
        def _():
            lat_read(r).wait()
            row = lax.broadcasted_iota(jnp.int32, lat_tile.shape[1:], 0)
            lat_tile[r] = jnp.where(
                row == inside - group, new_lat[r : r + 1, :], lat_tile[r].astype(F32)
            ).astype(BF16)
            lat_write(r).start()

    for r in range(requests):
        @pl.when(spots[r][0])
        def _():
            rope_write(r).wait()

        @pl.when(in_pool(r))
        def _():
            lat_write(r).wait()
    for copy in pages:
        copy.wait()


def body(
    hidden,
    lengths,
    page_table,
    move_slot,
    lat_pool,
    rope_pool,
    norm_attn,
    w_query,
    w_latent,
    latent_gain,
    w_key_up,
    w_value_up,
    w_output,
    norm_ffn,
    w_router,
    route_ids,
    expert_gate,
    expert_up,
    expert_down,
    shared_gate,
    shared_up,
    shared_down,
):
    requests, size = hidden.shape
    per_dev = page_table.shape[1]
    local_heads, nope_size, lat_size = w_key_up.shape
    local_experts, _, units = expert_gate.shape
    n_tp, n_rep = lax.axis_size("tp"), lax.axis_size("rep")
    groups = n_rep // 2
    half = n_rep // 2
    rows = local_heads * requests
    everyone = n_rep * requests
    pages = requests * per_dev
    width = lat_size + LANES
    tp_one = lax.axis_index("tp").astype(jnp.int32)[None]
    rep_one = lax.axis_index("rep").astype(jnp.int32)[None]
    page_bytes = PAGE * (lat_size + ROPE) * 2
    dma = pltpu.SemaphoreType.DMA
    first_span = per_dev * 6 // 10
    second_span = per_dev - first_span
    lat_page = lat_pool.shape[1:]
    rope_page = rope_pool.shape[1:]
    lat_hbm, rope_hbm = in_hbm(lat_pool), in_hbm(rope_pool)
    gate_t = jnp.swapaxes(expert_gate, 1, 2).reshape(-1, size)
    up_t = jnp.swapaxes(expert_up, 1, 2).reshape(-1, size)

    q_own, normed, out_first, out_rope = call(
        functools.partial(query_kernel, first_span),
        (
            struct((rows, lat_size + ROPE), BF16),
            struct((requests, size), BF16),
            struct((first_span,) + lat_page, BF16),
            struct((per_dev,) + rope_page, BF16),
        ),
        [ANY] * 8,
        (VMEM,) * 4,
        [
            pltpu.SMEM(page_table.shape, jnp.int32),
            pltpu.SMEM((1,), jnp.int32),
            pltpu.VMEM(hidden.shape, BF16),
            pltpu.VMEM((1, size), F32),
            pltpu.VMEM(w_query.shape, BF16),
            pltpu.VMEM(w_key_up.shape, BF16),
            dma((2, per_dev)),
            dma((7,)),
        ],
        vmem=8,
        flops=2 * requests * w_query.size,
        nbytes=2 * w_query.size,
    )(
        page_table, move_slot, in_hbm(hidden), in_hbm(norm_attn[None, :]),
        in_hbm(w_query), in_hbm(w_key_up), lat_hbm, rope_hbm,
    )
    got_first = xored(out_first, "rep", half)
    got_rope = xored(out_rope, "rep", half)
    q_blocks = [q_own] + [xored(q_own, "tp", k) for k in range(1, n_tp)]

    lat_v, rope_v, _ = call(
        functools.partial(fetch_kernel, requests),
        (
            pltpu.VMEM((pages,) + lat_page, BF16),
            pltpu.VMEM((pages,) + rope_page, BF16),
            struct((8, LANES), F32),
        ),
        [VMEM, ANY, ANY],
        (VMEM,) * 3,
        [dma((requests + 1,))],
        vmem=6,
        flops=2 * requests * w_latent.size,
        nbytes=pages * page_bytes + 2 * (w_latent.size + w_output.size + w_value_up.size),
    )(q_own, lat_hbm, rope_hbm)

    *partial, lat_most, rope_most = call(
        functools.partial(attention_kernel, n_tp, per_dev, requests, lat_size),
        tuple(struct((rows, width), BF16) for _ in range(n_tp))
        + (struct(lat_pool.shape, BF16), struct(rope_pool.shape, BF16)),
        [SMEM] * 3 + [VMEM] * (n_tp + 2),
        (VMEM,) * n_tp + (ANY, ANY),
        [pltpu.VMEM((width // LANES, n_tp * rows, LANES), F32)] * 2 + [dma((requests + 1,))],
        vmem=6,
        flops=4 * n_tp * rows * per_dev * PAGE * lat_size,
        nbytes=pages * page_bytes,
    )(page_table, lengths, tp_one, *q_blocks, lat_v, rope_v)
    parts = [partial[0]] + [xored(partial[k], "tp", k) for k in range(1, n_tp)]
    value_v, out_v, new = call(
        token_weights_kernel,
        (
            pltpu.VMEM(w_value_up.shape, BF16),
            pltpu.VMEM(w_output.shape, BF16),
            struct((requests, width), F32),
        ),
        [SMEM] + [VMEM] * 3 + [ANY] * 3,
        (VMEM,) * 3,
        [pltpu.VMEM((w_latent.shape[1], size), BF16), dma((3,))],
        vmem=6,
        flops=2 * requests * w_latent.size,
        nbytes=2 * (w_latent.size + w_output.size + w_value_up.size),
    )(
        lengths, normed, latent_gain[None, :], partial[0], in_hbm(w_latent.T),
        in_hbm(w_value_up), in_hbm(w_output),
    )

    out_part, out_sent = call(
        functools.partial(finish_kernel, n_tp, requests, lat_size),
        (struct((requests, size), F32), struct((requests, size), BF16)),
        [VMEM] * (n_tp + 4),
        (VMEM, VMEM),
        vmem=4,
        flops=2 * requests * size * w_output.shape[0],
        nbytes=2 * w_output.size + 2 * w_value_up.size,
    )(*parts, q_own, new, value_v, out_v)
    out_parts = [out_part] + [xored(out_sent, "tp", k) for k in range(1, n_tp)]

    ffn_row, h_one = call(
        functools.partial(norm_kernel, n_tp),
        (
            struct((requests, size + LANES), BF16),
            struct((requests, size), BF16),
        ),
        [SMEM] + [VMEM] * (n_tp + 2) + [ANY] * 2,
        (VMEM,) * 2,
        vmem=4,
        nbytes=8 * n_tp * requests * size,
    )(move_slot, *out_parts, hidden, norm_ffn[None, :], got_first, got_rope)

    pair = jnp.concatenate([ffn_row, xored(ffn_row, "rep", 1)], axis=0)
    pieces = [pair] + [xored(pair, "rep", 2 * k) for k in range(1, groups)]

    shared_hid, out_second = call(
        functools.partial(shared_kernel, first_span, second_span),
        (
            struct((requests, shared_gate.shape[1]), BF16),
            struct((second_span * PAGE + ROWS, lat_size), BF16),
        ),
        [SMEM, SMEM] + [VMEM] * 4 + [ANY] * 3,
        (VMEM, VMEM),
        [
            pltpu.VMEM((shared_gate.shape[1], size), BF16),
            pltpu.VMEM((shared_gate.shape[1], size), BF16),
            dma((2,)),
            dma((second_span,)),
        ],
        vmem=12,
        flops=6 * requests * shared_gate.size,
        nbytes=6 * shared_gate.size,
    )(
        page_table, move_slot, ffn_row, h_one, new, pair, in_hbm(shared_gate.T),
        in_hbm(shared_up.T), lat_hbm,
    )
    x_all, coef, out_second = call(
        functools.partial(order_kernel, groups, requests),
        (
            struct((everyone, size), BF16),
            struct((everyone, w_router.shape[1]), F32),
            struct(out_second.shape, BF16),
        ),
        [SMEM] + [VMEM] * (groups + 3),
        (VMEM,) * 3,
        vmem=6,
        flops=4 * everyone * size * everyone,
        nbytes=4 * everyone * size,
        aliases={3 + groups: 2},
    )(rep_one, route_ids, w_router.T, *pieces, out_second)
    got_second = xored(out_second, "rep", half)
    got_row = got_second[second_span * PAGE :].reshape(1, -1)

    kept, sent = call(
        functools.partial(expert_kernel, requests, 512, units),
        (
            struct((groups * requests, size), F32),
            struct((groups * requests, size), BF16),
        ),
        [SMEM] + [VMEM] * 2 + [ANY] * 3,
        (VMEM, VMEM),
        [pltpu.VMEM((local_experts * units, size), BF16)] * 3
        + [pltpu.VMEM((everyone, size), F32), dma((3, pl.cdiv(local_experts * units, 512)))],
        vmem=42,
        flops=6 * everyone * expert_gate.size,
        nbytes=6 * expert_gate.size,
    )(
        rep_one, x_all, coef, in_hbm(gate_t), in_hbm(up_t), in_hbm(expert_down.reshape(-1, size)),
    )
    summed = call(
        functools.partial(pair_kernel, requests),
        (struct((requests, size), F32),) + (struct((requests, size), BF16),) * (groups - 1),
        [VMEM, VMEM, ANY],
        (VMEM,) * groups,
        vmem=4,
        nbytes=8 * everyone * size,
    )(kept, xored(sent, "rep", 1), got_second)
    others = [xored(summed[k], "rep", 2 * k) for k in range(1, groups)]
    lat_most, rope_most, shared_part = call(
        functools.partial(cache_kernel, first_span),
        (struct(lat_pool.shape, BF16), struct(rope_pool.shape, BF16), struct((requests, size), F32)),
        [SMEM] * 2 + [VMEM] * 3 + [ANY] * 5,
        (ANY, ANY, VMEM),
        [
            pltpu.VMEM((first_span,) + lat_page, BF16),
            pltpu.VMEM((per_dev,) + rope_page, BF16),
            pltpu.VMEM(shared_down.shape, BF16),
            dma((3,)),
            dma((2, per_dev)),
        ],
        vmem=8,
        nbytes=2 * first_span * page_bytes,
        aliases={8: 0, 9: 1},
    )(
        page_table, move_slot, summed[0], shared_hid,
        got_row[:, size + width : size + width + shared_gate.shape[1]], in_hbm(shared_down),
        got_first, got_rope, lat_most, rope_most,
    )
    total, total_sent = call(
        total_kernel,
        (struct((requests, size), F32), struct((requests, size), BF16)),
        [VMEM] * (groups + 1),
        (VMEM, VMEM),
        vmem=4,
        nbytes=8 * everyone * size,
    )(summed[0], shared_part, *others)

    is_moved = (jnp.arange(requests, dtype=jnp.int32) == move_slot[0])[:, None]
    new_served = jnp.where(is_moved, got_row[:, size : size + width].astype(F32), new)
    marks = new_served[:, lat_size + ROPE : lat_size + ROPE + 2].astype(jnp.int32)
    len_served = marks[:, 0] * PAGE + marks[:, 1]
    lat_new = new_served[:, :lat_size]
    rope_new = new_served[:, lat_size : lat_size + ROPE].T
    lat_cache, rope_cache = call(
        functools.partial(token_kernel, first_span, per_dev),
        (struct(lat_pool.shape, BF16), struct(rope_pool.shape, BF16)),
        [SMEM] * 4 + [VMEM] * 2 + [ANY, VMEM] + [ANY] * 2,
        (ANY, ANY),
        [
            pltpu.VMEM((second_span * PAGE, lat_size), BF16),
            pltpu.VMEM((requests, 16, lat_size), BF16),
            pltpu.VMEM((requests,) + rope_page, BF16),
            dma((1,)),
            dma((second_span,)),
            dma((2, requests)),
        ],
        vmem=2,
        nbytes=2 * second_span * page_bytes,
        aliases={8: 0, 9: 1},
    )(
        page_table, move_slot, len_served, tp_one, lat_new, rope_new, got_second, total,
        lat_most, rope_most,
    )

    total_all = total
    for other in [xored(total_sent, "tp", k) for k in range(1, n_tp)]:
        total_all = total_all + other.astype(F32)
    h_served = jnp.where(is_moved, got_row[:, :size], h_one)
    mixed = (h_served.astype(F32) + total_all).astype(BF16)
    return (mixed, lat_cache, rope_cache)


def solution(mesh):
    in_specs = (
        P("rep", None),
        P("rep"),
        P("rep", "tp"),
        P("rep"),
        P(("rep", "tp"), None, None),
        P(("rep", "tp"), None, None),
        P(),
        P(None, "tp"),
        P(),
        P(),
        P("tp", None, None),
        P("tp", None, None),
        P("tp", None),
        P(),
        P(),
        P(),
        P("rep", None, "tp"),
        P("rep", None, "tp"),
        P("rep", "tp", None),
        P(None, "tp"),
        P(None, "tp"),
        P("tp", None),
    )
    out_specs = (P("rep", None), P(("rep", "tp"), None, None), P(("rep", "tp"), None, None))
    return jax.shard_map(body, mesh=mesh, in_specs=in_specs, out_specs=out_specs, check_vma=False)
```
